32 devices in a mesh: exp: 8 (over z, y), tp: 4 (over x, core).
Axes of the slice: x: 2, y: 2, z: 4, core: 2. Of those that a mesh axis runs over, the one named last changes fastest.
Arguments:
- tokens: bfloat16 [4096, 2048], P(('exp', 'tp')), may hold values from -6 to 6
- out_grad: bfloat16 [4096, 2048], P(('exp', 'tp')), may hold values from -6 to 6
- first_gain: float32 [2048], replicated, may hold values from 0.5 to 1.5
- second_gain: float32 [2048], replicated, may hold values from 0.5 to 1.5
- query_gain: float32 [128], replicated, may hold values from 0.1 to 1.9
- key_gain: float32 [128], replicated, may hold values from 0.1 to 1.9
- query_weight: bfloat16 [2048, 4096], P('exp', 'tp'), may hold values from -0.125 to 0.125
- key_weight: bfloat16 [2048, 512], P('exp', 'tp'), may hold values from -0.125 to 0.125
- value_weight: bfloat16 [2048, 512], P('exp', 'tp'), may hold values from -0.125 to 0.125
- output_weight: bfloat16 [4096, 2048], P('tp', 'exp'), may hold values from -0.75 to 0.75
- router_weight: bfloat16 [2048, 32], replicated, may hold values from -0.125 to 0.125
- gate_weight: bfloat16 [32, 2048, 768], P(('exp', 'tp')), may hold values from -0.125 to 0.125
- up_weight: bfloat16 [32, 2048, 768], P(('exp', 'tp')), may hold values from -0.125 to 0.125
- down_weight: bfloat16 [32, 768, 2048], P(('exp', 'tp')), may hold values from -0.4375 to 0.4375
- expert_ids: int32 [4096, 8], P(('exp', 'tp')), may hold values from 0 to 31, all different within a row
- router_order: int32 [32, 128], P(('exp', 'tp')), may hold values from 0 to 127, each once within a row
- image_starts: int32 [4, 2], replicated, may hold values from 0 to 768, as said below
Outputs:
- block_out: bfloat16 [4096, 2048], P(('exp', 'tp'))
- tokens_grad: float32 [4096, 2048], P(('exp', 'tp'))
- first_gain_grad: float32 [2048], replicated
- second_gain_grad: float32 [2048], replicated
- query_gain_grad: float32 [128], replicated
- key_gain_grad: float32 [128], replicated
- query_grad: float32 [2048, 4096], P('exp', 'tp')
- key_grad: float32 [2048, 512], P('exp', 'tp')
- value_grad: float32 [2048, 512], P('exp', 'tp')
- output_grad: float32 [4096, 2048], P('tp', 'exp')
- router_grad: float32 [2048, 32], replicated
- gate_grad: float32 [32, 2048, 768], P(('exp', 'tp'))
- up_grad: float32 [32, 2048, 768], P(('exp', 'tp'))
- down_grad: float32 [32, 768, 2048], P(('exp', 'tp'))
The draws below stay inside these ranges and needn't reach their ends.
Inputs may be any that keep to these rules, and one draw needn't show every extreme that they name: `image_starts`: in each sequence the k-th image piece (k from 0) starts between k * 512 and (k + 1) * 512 - 256, so pieces never intersect. `router_order`: each device's row orders its 128 tokens, each number once. `expert_ids`: each row names 8 different experts.
All inputs are finite; a program needn't handle non-finite values.
Results may differ from the reference program's by a relative error of at most 0.02.
Values may be sent and summed in bfloat16 or wider, within the bound.
A program may use at most 256 MiB of HBM per device.

```python
import jax
import jax.numpy as jnp
from jax import lax

D = 2048
FF = 768
QH = 32
KVH = 4
HD = 128
TOP = 8
SEQ = 1024
IMG_LEN = 256
IMGS = 2
EXPERTS = 32
SEQS = 4
TOK_DEV = 128
TOKENS = 4096
CAP = 36
N_EXP = 8
N_TP = 4


def draw_image_starts(key, part):
    stretch = SEQ // IMGS - IMG_LEN
    margin = stretch // 4 + 1
    offsets = jax.random.randint(key, (SEQS, IMGS), -margin, stretch + margin + 1)
    offsets = jnp.clip(offsets, 0, stretch)
    return (offsets + jnp.arange(IMGS, dtype=jnp.int32)[None, :] * (SEQ // IMGS)).astype(jnp.int32)


def steps_of(key, shape, cuts, smallest, top_value):
    factor_of = 1.0
    for dim, blocks in cuts:
        heights = jax.random.uniform(jax.random.fold_in(jax.random.fold_in(key, 6), dim), (blocks,), jnp.float32, smallest / len(cuts), top_value / len(cuts))
        factor_of = factor_of * jnp.repeat(jnp.exp(heights), shape[dim] // blocks).reshape((-1,) + (1,) * (len(shape) - 1 - dim))
    return factor_of


def choose_distinct(stream_key, rows, number_of, top, lift):
    sequence = jax.random.permutation(jax.random.fold_in(stream_key, 1), number_of)
    favour = sequence
    for power in range(3):
        favour = favour * favour // number_of
    favour = favour * lift // number_of
    lots = jax.random.randint(jax.random.fold_in(stream_key, 2), (rows, number_of), 0, 4096) + favour
    fixed_rows = jax.random.permutation(jax.random.fold_in(stream_key, 3), rows)[jnp.arange(number_of) % rows]
    lots = jnp.where(jnp.arange(rows)[:, None] == fixed_rows[None, :], 1 << 14, lots)
    priority = lots * number_of + jnp.arange(number_of)
    return lax.top_k(priority.astype(jnp.int32), top)[1].astype(jnp.int32)


def normal_values(own_key, extent, scale, reach, cuts=(), held_as=jnp.bfloat16):
    drawn = jax.random.normal(own_key, extent, jnp.float32) * scale
    if len(cuts) > 0:
        drawn = steps_of(own_key, extent, cuts, -0.22, 0.18) * drawn
    return jnp.clip(drawn, min=-reach, max=reach).astype(held_as)


def setup_inputs(seed: int = 0) -> dict:
    streams_of = jax.random.split(jax.random.key(seed), 18)
    return {
        "tokens": normal_values(streams_of[0], (TOKENS, D), 1.0, 6.0, ((0, 32),)),
        "out_grad": normal_values(streams_of[1], (TOKENS, D), 1.0, 6.0, ((0, 32),)),
        "first_gain": jnp.clip(1.0 + 0.1 * jax.random.normal(streams_of[2], (D,), jnp.float32), 0.5, 1.5),
        "second_gain": jnp.clip(1.0 + 0.1 * jax.random.normal(streams_of[3], (D,), jnp.float32), 0.5, 1.5),
        "query_gain": jnp.clip(1.0 + 0.18 * jax.random.normal(streams_of[4], (HD,), jnp.float32), 0.1, 1.9),
        "key_gain": jnp.clip(1.0 + 0.18 * jax.random.normal(streams_of[5], (HD,), jnp.float32), 0.1, 1.9),
        "query_weight": normal_values(streams_of[6], (D, QH * HD), D ** -0.5, 0.125, ((0, 8), (1, 4))),
        "key_weight": normal_values(streams_of[7], (D, KVH * HD), D ** -0.5, 0.125, ((0, 8), (1, 4))),
        "value_weight": normal_values(streams_of[8], (D, KVH * HD), D ** -0.5, 0.125, ((0, 8), (1, 4))),
        "output_weight": normal_values(streams_of[9], (QH * HD, D), (QH * HD * 16 // SEQ) ** -0.5, 0.75, ((0, 4), (1, 8))),
        "router_weight": normal_values(streams_of[10], (D, EXPERTS), D ** -0.5, 0.125),
        "gate_weight": normal_values(streams_of[11], (EXPERTS, D, FF), D ** -0.5, 0.125, ((0, 32),)),
        "up_weight": normal_values(streams_of[12], (EXPERTS, D, FF), D ** -0.5, 0.125, ((0, 32),)),
        "down_weight": normal_values(streams_of[13], (EXPERTS, FF, D), (FF // 4) ** -0.5, 0.4375, ((0, 32),)),
        "expert_ids": choose_distinct(streams_of[14], TOKENS, EXPERTS, TOP, 4096),
        "router_order": jax.vmap(lambda own: jax.random.permutation(own, TOK_DEV))(jax.random.split(streams_of[15], (N_EXP * N_TP))).reshape((N_EXP * N_TP, TOK_DEV)).astype(jnp.int32),
        "image_starts": draw_image_starts(jax.random.fold_in(streams_of[17], 71), 0),
    }


@jax.custom_vjp
def low(v):
    return lax.optimization_barrier(v.astype(jnp.bfloat16)).astype(jnp.float32)

@jax.custom_vjp
def low_back(v):
    return v

def low_keep(v):
    return (low(v), None)

def low_pass(kept, grad):
    return (grad,)

def back_keep(v):
    return (v, None)

def back_low(kept, grad):
    return (low(grad),)
low.defvjp(low_keep, low_pass)
low_back.defvjp(back_keep, back_low)
EPSILON = 1e-06
THETA = 1000000.0
NEGATIVE = -1e+30
HIGH = lax.Precision.HIGHEST

def rms_scale(values):
    return lax.rsqrt(lax.optimization_barrier(jnp.mean(values * values, axis=-1, keepdims=True)) + EPSILON)

def rotary_tables(positions, width):
    half = width // 2
    freqs = THETA ** (-(jnp.arange(half, dtype=jnp.float32) * 2.0 / width))
    angles = positions.astype(jnp.float32)[:, None] * freqs[None, :]
    return (jnp.cos(angles), jnp.sin(angles))

def rotate(values, cosine, sine):
    half = values.shape[-1] // 2
    first = values[..., :half]
    second = values[..., half:]
    return jnp.concatenate([first * cosine - second * sine, second * cosine + first * sine], axis=-1)

def piece_ids(positions, starts):
    inside = (positions[:, None] >= starts[None, :]) & (positions[:, None] < starts[None, :] + IMG_LEN)
    labels = jnp.arange(1, starts.shape[0] + 1, dtype=jnp.int32)
    return lax.optimization_barrier(jnp.sum(jnp.where(inside, labels[None, :], 0), axis=1))

def allowed_mask(query_pos, key_pos, query_piece, key_piece):
    causal = key_pos[None, :] <= query_pos[:, None]
    same = (query_piece[:, None] == key_piece[None, :]) & (query_piece[:, None] > 0)
    return causal | same

def slot_tables(expert_ids, router_order):
    sources = N_EXP * N_TP
    block_ids = expert_ids.reshape(sources, TOK_DEV, TOP)
    expert_axis = jnp.arange(EXPERTS, dtype=jnp.int32)

    def block_slots(inputs):
        ids_here, order_here = inputs
        onehot = ids_here[:, :, None] == expert_axis[None, None, :]
        member = lax.optimization_barrier(jnp.sum(onehot.astype(jnp.int32), axis=1))
        earlier = order_here[None, :] < order_here[:, None]
        counts = lax.optimization_barrier(jnp.sum(jnp.where(earlier[:, :, None], member[None, :, :], 0), axis=1)).astype(jnp.int32)
        return lax.optimization_barrier(jnp.sum(jnp.where(onehot, counts[:, None, :], 0), axis=2)).astype(jnp.int32)
    slots = lax.map(block_slots, (block_ids, router_order))
    keep = slots < CAP
    source = jnp.arange(sources, dtype=jnp.int32)[:, None, None]
    total = EXPERTS * sources * CAP
    dest = block_ids * (sources * CAP) + source * CAP + slots
    dest = jnp.where(keep, dest, total).reshape(-1).astype(jnp.int32)
    token_of = jnp.broadcast_to(source * TOK_DEV + jnp.arange(TOK_DEV, dtype=jnp.int32)[None, :, None], block_ids.shape).reshape(-1)
    pair_of = jnp.arange(TOKENS * TOP, dtype=jnp.int32)
    slot_tokens = jnp.full((total,), TOKENS, jnp.int32).at[dest].set(token_of, mode='drop')
    slot_pairs = jnp.full((total,), TOKENS * TOP, jnp.int32).at[dest].set(pair_of, mode='drop')
    return (slot_tokens.reshape(EXPERTS, sources * CAP), slot_pairs.reshape(EXPERTS, sources * CAP))

def attend(seq_norm, starts, query_weight, key_weight, value_weight, query_gain, key_gain):
    length = seq_norm.shape[0]
    positions = jnp.arange(length, dtype=jnp.int32)
    cosine, sine = rotary_tables(positions, HD)
    query_pre = low_back(jnp.dot(seq_norm, query_weight, precision=HIGH)).reshape(length, QH, HD)
    key_pre = low_back(jnp.dot(seq_norm, key_weight, precision=HIGH)).reshape(length, KVH, HD)
    value_rows = low(low_back(jnp.dot(seq_norm, value_weight, precision=HIGH))).reshape(length, KVH, HD)
    query_rot = low(rotate(query_pre * rms_scale(query_pre) * query_gain, cosine[:, None, :], sine[:, None, :]))
    key_rot = low(rotate(key_pre * rms_scale(key_pre) * key_gain, cosine[:, None, :], sine[:, None, :]))
    group = QH // KVH
    query_grp = query_rot.reshape(length, KVH, group, HD)
    scores = jnp.einsum('qhgd,khd->hgqk', query_grp, key_rot, precision=HIGH) * HD ** (-0.5)
    scores = low_back(scores)
    pieces = piece_ids(positions, starts)
    mask = allowed_mask(positions, positions, pieces, pieces)
    scores = jnp.where(mask[None, None], scores, NEGATIVE)
    probs = low(jax.nn.softmax(scores, axis=-1))
    context = jnp.einsum('hgqk,khd->qhgd', probs, value_rows, precision=HIGH)
    return low(low_back(context.reshape(length, QH * HD)))

def layer(tokens, first_gain, second_gain, query_gain, key_gain, query_weight, key_weight, value_weight, output_weight, router_weight, gate_weight, up_weight, down_weight, expert_ids, image_starts, slot_tokens, slot_pairs):
    first_norm = low(tokens * rms_scale(tokens) * first_gain)
    seq_view = first_norm.reshape(SEQS, SEQ, D)

    def one_sequence(inputs):
        return attend(inputs[0], inputs[1], query_weight, key_weight, value_weight, query_gain, key_gain)
    contexts = lax.map(jax.checkpoint(one_sequence), (seq_view, image_starts))
    attention = low_back(jnp.dot(contexts.reshape(TOKENS, QH * HD), output_weight, precision=HIGH))
    middle = tokens + attention
    second_norm = low(middle * rms_scale(middle) * second_gain)
    logits = low_back(jnp.dot(second_norm, router_weight, precision=HIGH))
    chosen = jnp.take_along_axis(logits, expert_ids, axis=1)
    mix = jax.nn.softmax(chosen, axis=-1)
    padded_norm = jnp.concatenate([second_norm, jnp.zeros((1, D), jnp.float32)], axis=0)
    padded_mix = jnp.concatenate([mix.reshape(-1), jnp.zeros((1,), jnp.float32)], axis=0)

    def one_expert(gate_here, up_here, down_here, rows, pairs):
        arrived = low_back(padded_norm[rows])
        gate_val = low_back(jnp.dot(arrived, gate_here, precision=HIGH))
        up_val = low_back(jnp.dot(arrived, up_here, precision=HIGH))
        inner = low(jax.nn.silu(gate_val) * up_val)
        result = low(low_back(jnp.dot(inner, down_here, precision=HIGH)))
        return padded_mix[pairs][:, None] * result
    expert_fn = jax.checkpoint(one_expert)

    def expert_step(carry, inputs):
        contrib = expert_fn(inputs[0], inputs[1], inputs[2], inputs[3], inputs[4])
        return (carry.at[inputs[3]].add(contrib), None)
    start_mix = jnp.zeros((TOKENS + 1, D), jnp.float32)
    mixture, unused = lax.scan(expert_step, start_mix, (gate_weight, up_weight, down_weight, slot_tokens, slot_pairs))
    return middle + mixture[:TOKENS]

def reference(tokens, out_grad, first_gain, second_gain, query_gain, key_gain, query_weight, key_weight, value_weight, output_weight, router_weight, gate_weight, up_weight, down_weight, expert_ids, router_order, image_starts):
    slot_tokens, slot_pairs = slot_tables(expert_ids, router_order)
    floats = tuple((arr.astype(jnp.float32) for arr in (tokens, first_gain, second_gain, query_gain, key_gain, query_weight, key_weight, value_weight, output_weight, router_weight, gate_weight, up_weight, down_weight)))

    def forward(*params):
        return layer(*params, expert_ids, image_starts, slot_tokens, slot_pairs)
    result, pullback = jax.vjp(forward, *floats)
    grads = pullback(out_grad.astype(jnp.float32))
    return (result.astype(jnp.bfloat16), grads[0], grads[1], grads[2], grads[3], grads[4], grads[5], grads[6], grads[7], grads[8], grads[9], grads[10], grads[11], grads[12])
```

```python
import functools

import jax
import jax.numpy as jnp
from jax import lax
from jax.experimental import pallas as pl
from jax.experimental.pallas import tpu as pltpu
from jax.sharding import PartitionSpec as P

HD = 128
TOP = 8
IMG_LEN = 256
PLANE = 8

EPSILON = 1e-06
THETA = 1000000.0
NEGATIVE = -1e30

MESH = pl.DeviceIdType.MESH
f32 = jnp.float32
bf16 = jnp.bfloat16
VMEM_LIMIT = 60 << 20


def rms_scale(values):
    return lax.rsqrt(jnp.mean(values * values, axis=-1, keepdims=True) + EPSILON)


def rotary_tables(positions, width):
    half = width // 2
    freqs = THETA ** (-(jnp.arange(half, dtype=f32) * 2.0 / width))
    angles = positions.astype(f32)[:, None] * freqs[None, :]
    return (jnp.cos(angles), jnp.sin(angles))


def rotate(values, cosine, sine):
    half = values.shape[-1] // 2
    first = values[..., :half]
    second = values[..., half:]
    return jnp.concatenate(
        [first * cosine - second * sine, second * cosine + first * sine], axis=-1
    )


def unrotate(values, cosine, sine):
    half = values.shape[-1] // 2
    first = values[..., :half]
    second = values[..., half:]
    return jnp.concatenate(
        [first * cosine + second * sine, second * cosine - first * sine], axis=-1
    )


def piece_ids(positions, starts):
    inside = (positions[:, None] >= starts[None, :]) & (
        positions[:, None] < starts[None, :] + IMG_LEN
    )
    labels = jnp.arange(1, starts.shape[0] + 1, dtype=jnp.int32)
    return jnp.sum(jnp.where(inside, labels[None, :], 0), axis=1)


def allowed_mask(query_pos, key_pos, query_piece, key_piece):
    causal = key_pos[None, :] <= query_pos[:, None]
    same = (query_piece[:, None] == key_piece[None, :]) & (query_piece[:, None] > 0)
    return causal | same


def norm_back(grad_norm, hat, rms, gain):
    scaled = grad_norm * gain
    inner_mean = jnp.mean(scaled * hat, axis=-1, keepdims=True)
    lead_axes = tuple(range(grad_norm.ndim - 1))
    return (rms * (scaled - hat * inner_mean), jnp.sum(grad_norm * hat, axis=lead_axes))


class Place:
    def __init__(self):
        self.e = lax.axis_index("exp")
        self.t = lax.axis_index("tp")
        self.z = self.e // 2
        self.y = self.e % 2
        self.x = self.t // 2
        self.c = self.t % 2
        self.p = self.y * 4 + self.t

    def at(self, z, p):
        return (z * 2 + p // 4, p % 4)

    def flip(self, dy=0, dx=0, dc=0):
        y = 1 - self.y if dy else self.y
        x = 1 - self.x if dx else self.x
        c = 1 - self.c if dc else self.c
        return y * 4 + x * 2 + c

    def peer(self, dy=0, dx=0, dc=0):
        return self.at(self.z, self.flip(dy, dx, dc))

    def by(self, k):
        return self.flip((k >> 2) & 1, (k >> 1) & 1, k & 1)


class Sends:
    def __init__(self):
        self.kept = []

    def start(self, src, dst, send_sem, recv_sem, device, when=None):
        def make():
            return pltpu.make_async_remote_copy(
                src_ref=src,
                dst_ref=dst,
                send_sem=send_sem,
                recv_sem=recv_sem,
                device_id=device,
                device_id_type=MESH,
            )

        def go():
            make().start()

        if when is None:
            go()
        else:
            pl.when(when)(go)
        self.kept.append((make, when))

    def finish(self):
        for make, when in self.kept:
            if when is None:
                make().wait_send()
            else:
                pl.when(when)(lambda make=make: make().wait_send())
        self.kept = []


def arrived(dst, recv_sem, when=None):
    def go():
        pltpu.make_async_copy(dst, dst, recv_sem).wait()

    if when is None:
        go()
    else:
        pl.when(when)(go)


def greet(place, zn, ends=False, everyone=True, planes=True):
    bar = pltpu.get_barrier_semaphore()
    count = 0
    if planes:
        for k in range(1, PLANE):
            pl.semaphore_signal(
                bar, inc=1, device_id=place.at(place.z, place.by(k)), device_id_type=MESH
            )
        count += PLANE - 1
    if everyone:
        for k in range(1, zn):
            pl.semaphore_signal(
                bar,
                inc=1,
                device_id=place.at((place.z + k) % zn, place.p),
                device_id_type=MESH,
            )
        count += zn - 1
    pl.semaphore_wait(bar, count)
    if ends:
        bar2 = 0
        del bar2


class PlaneGather:
    sems = 8

    def __init__(self, place, sends, buf, ss, rs):
        self.place, self.sends, self.buf, self.ss, self.rs = place, sends, buf, ss, rs
        half = buf.shape[2] // 2
        self.cols_a = pl.ds(0, half)
        self.cols_b = pl.ds(half, half)

    def _send(self, block, which, device, cols=None):
        ref = self.buf.at[block] if cols is None else self.buf.at[block, :, cols]
        self.sends.start(ref, ref, self.ss.at[which], self.rs.at[which], device)

    def _wait(self, block, which, cols=None):
        ref = self.buf.at[block] if cols is None else self.buf.at[block, :, cols]
        arrived(ref, self.rs.at[which])

    def first(self):
        pc = self.place
        self._send(pc.p, 0, pc.peer(dy=1))
        self._send(pc.p, 1, pc.peer(dx=1))
        self._send(pc.p, 2, pc.peer(dc=1))

    def second(self):
        pc = self.place
        px, py = pc.flip(dx=1), pc.flip(dy=1)
        self._wait(px, 1)
        self._send(px, 3, pc.peer(dy=1), self.cols_a)
        self._send(px, 4, pc.peer(dc=1))
        self._wait(py, 0)
        self._send(py, 5, pc.peer(dx=1), self.cols_b)
        self._send(py, 6, pc.peer(dc=1))

    def third(self):
        pc = self.place
        pd = pc.flip(dy=1, dx=1)
        self._wait(pd, 3, self.cols_a)
        self._wait(pd, 5, self.cols_b)
        self._send(pd, 7, pc.peer(dc=1))

    def last(self):
        pc = self.place
        self._wait(pc.flip(dc=1), 2)
        self._wait(pc.flip(dc=1, dx=1), 4)
        self._wait(pc.flip(dc=1, dy=1), 6)
        self._wait(pc.flip(dc=1, dy=1, dx=1), 7)


def add_rows(dst, first, second, rows, step=32):
    def body(i, carry):
        at = pl.ds(pl.multiple_of(i * step, step), step)
        dst(at, first(at).astype(f32) + second(at).astype(f32))
        return carry

    lax.fori_loop(0, rows // step, body, 0)


class PlaneReduce:
    sems = 4 + 4 + 2

    @staticmethod
    def scratch(rows, width):
        return [
            pltpu.VMEM((4, rows, width), bf16),
            pltpu.VMEM((4, rows, width), bf16),
            pltpu.VMEM((2, rows, width // 2), bf16),
            pltpu.VMEM((2, rows, width // 2), bf16),
            pltpu.VMEM((2, rows, width // 2), bf16),
        ]

    def __init__(self, place, sends, part, out, scratch, ss, rs):
        self.place, self.sends, self.part, self.out = place, sends, part, out
        self.c1, self.s1, self.ra, self.rb, self.last = scratch
        self.ss, self.rs = ss, rs
        self.rows = part.shape[1]
        half = part.shape[2] // 2
        self.half = half
        self.cols_a = pl.ds(0, half)
        self.cols_b = pl.ds(half, half)
        pc = place
        self.chips = [(1, 1), (0, 1), (1, 0), (0, 0)]

    def _chip(self, dy, dx):
        pc = self.place
        y = 1 - pc.y if dy else pc.y
        x = 1 - pc.x if dx else pc.x
        return y, x, y * 2 + x

    def first(self, k):
        pc = self.place
        y, x, j = self._chip(*self.chips[k])
        block = y * 4 + x * 2 + (1 - pc.c)
        self.sends.start(
            self.part.at[block], self.c1.at[j], self.ss.at[k], self.rs.at[k], pc.peer(dc=1)
        )

    def second(self, k):
        pc = self.place
        y, x, j = self._chip(*self.chips[k])
        arrived(self.c1.at[j], self.rs.at[k])
        mine = y * 4 + x * 2 + pc.c

        def put(at, v):
            self.s1[j, at, :] = v.astype(bf16)

        add_rows(put, lambda at: self.part[mine, at, :], lambda at: self.c1[j, at, :], self.rows)
        dy, dx = self.chips[k]
        if dx:
            self.sends.start(
                self.s1.at[j, :, self.cols_a],
                self.ra.at[y],
                self.ss.at[4 + (0 if dy else 1)],
                self.rs.at[4 + (0 if dy else 1)],
                pc.peer(dx=1),
            )
        if dy:
            self.sends.start(
                self.s1.at[j, :, self.cols_b],
                self.rb.at[x],
                self.ss.at[6 + (0 if dx else 1)],
                self.rs.at[6 + (0 if dx else 1)],
                pc.peer(dy=1),
            )

    def third(self):
        pc = self.place
        other_y, other_x = 1 - pc.y, 1 - pc.x
        arrived(self.ra.at[other_y], self.rs.at[4])
        j = other_y * 2 + pc.x

        def put_a(at, v):
            self.ra[other_y, at, :] = v.astype(bf16)

        add_rows(
            put_a,
            lambda at: self.s1[j, at, self.cols_a],
            lambda at: self.ra[other_y, at, :],
            self.rows,
        )
        self.sends.start(
            self.ra.at[other_y], self.last.at[0], self.ss.at[8], self.rs.at[8], pc.peer(dy=1)
        )
        arrived(self.rb.at[other_x], self.rs.at[6])
        i = pc.y * 2 + other_x

        def put_b(at, v):
            self.rb[other_x, at, :] = v.astype(bf16)

        add_rows(
            put_b,
            lambda at: self.s1[i, at, self.cols_b],
            lambda at: self.rb[other_x, at, :],
            self.rows,
        )
        self.sends.start(
            self.rb.at[other_x], self.last.at[1], self.ss.at[9], self.rs.at[9], pc.peer(dx=1)
        )

    def finish(self):
        pc = self.place
        own = pc.y * 2 + pc.x
        arrived(self.ra.at[pc.y], self.rs.at[5])
        arrived(self.rb.at[pc.x], self.rs.at[7])

        def put_a(at, v):
            self.out[at, self.cols_a] = v + self.ra[pc.y, at, :].astype(f32)

        def put_b(at, v):
            self.out[at, self.cols_b] = v + self.rb[pc.x, at, :].astype(f32)

        arrived(self.last.at[0], self.rs.at[8])
        add_rows(
            put_a,
            lambda at: self.s1[own, at, self.cols_a],
            lambda at: self.last[0, at, :],
            self.rows,
        )
        arrived(self.last.at[1], self.rs.at[9])
        add_rows(
            put_b,
            lambda at: self.s1[own, at, self.cols_b],
            lambda at: self.last[1, at, :],
            self.rows,
        )


class ColumnGather:
    def __init__(self, place, sends, zn, pack, full, pair_ss, pair_rs, ss_r, ss_l, rs):
        self.place, self.sends, self.zn = place, sends, zn
        self.pack, self.full = pack, full
        self.pair_ss, self.pair_rs, self.ss_r, self.ss_l, self.rs = pair_ss, pair_rs, ss_r, ss_l, rs

    def _on(self, src, piece, right, left):
        pc = self.place
        if right is not None:
            self.sends.start(
                src,
                self.full.at[piece],
                self.ss_r.at[piece],
                self.rs.at[piece],
                pc.at(jnp.minimum(pc.z + 1, self.zn - 1), pc.p),
                right,
            )
        if left is not None:
            self.sends.start(
                src,
                self.full.at[piece],
                self.ss_l.at[piece],
                self.rs.at[piece],
                pc.at(jnp.maximum(pc.z - 1, 0), pc.p),
                left,
            )

    def pair(self):
        pc = self.place
        self.sends.start(
            self.pack.at[1 - pc.y],
            self.full.at[pc.e],
            self.pair_ss,
            self.pair_rs,
            pc.peer(dy=1),
        )

    def own(self):
        pc = self.place
        self._on(self.pack.at[pc.y], pc.e, pc.z < self.zn - 1, pc.z > 0)

    def keep(self):
        pc = self.place
        self.full[pc.e] = self.pack[pc.y]

    def partner(self):
        pc = self.place
        other = pc.z * 2 + 1 - pc.y
        arrived(self.full.at[other], self.pair_rs)
        self._on(self.full.at[other], other, pc.z < self.zn - 1, pc.z > 0)

    def step(self, k):
        pc = self.place
        for first in (True, False):
            y = pc.y if first else 1 - pc.y
            below = jnp.maximum(pc.z - k, 0) * 2 + y
            has = pc.z - k >= 0
            arrived(self.full.at[below], self.rs.at[below], has)
            self._on(
                self.full.at[below], below, jnp.logical_and(has, pc.z < self.zn - 1), None
            )
            above = jnp.minimum(pc.z + k, self.zn - 1) * 2 + y
            has = pc.z + k < self.zn
            arrived(self.full.at[above], self.rs.at[above], has)
            self._on(self.full.at[above], above, None, jnp.logical_and(has, pc.z > 0))


def open_kernel(zn, own_ref, pq_ref, po_ref, seq_ref, wq_ref, wo_ref, gs, gr, ps, pr, sr, sl, rs):
    place, sends = Place(), Sends()
    greet(place, zn)
    q = ColumnGather(
        place, sends, zn, pq_ref, wq_ref, ps.at[0], pr.at[0], sr.at[0], sl.at[0], rs.at[0]
    )
    o = ColumnGather(
        place, sends, zn, po_ref, wo_ref, ps.at[1], pr.at[1], sr.at[1], sl.at[1], rs.at[1]
    )
    q.pair()
    q.own()
    seq_ref[place.p] = own_ref[...]
    rows = PlaneGather(place, sends, seq_ref, gs, gr)
    rows.first()
    o.pair()
    q.keep()
    o.keep()
    q.partner()
    o.own()
    rows.second()
    o.partner()
    rows.third()
    for k in range(1, zn):
        q.step(k)
    for k in range(1, zn):
        o.step(k)
    rows.last()
    sends.finish()


def dma_sems(*shape):
    return pltpu.SemaphoreType.DMA(shape)


VSPEC = pl.BlockSpec(memory_space=pltpu.VMEM)
ASPEC = pl.BlockSpec(memory_space=pl.ANY)


def params(cid):
    return pltpu.CompilerParams(
        collective_id=cid, has_side_effects=True, vmem_limit_bytes=VMEM_LIMIT
    )


def open_gather(zn, own, pack_q, pack_o):
    rows, width = own.shape
    e = 2 * zn
    return pl.pallas_call(
        functools.partial(open_kernel, zn),
        out_shape=(
            jax.ShapeDtypeStruct((PLANE, rows, width), bf16),
            jax.ShapeDtypeStruct((e,) + pack_q.shape[1:], bf16),
            jax.ShapeDtypeStruct((e,) + pack_o.shape[1:], bf16),
        ),
        in_specs=[VSPEC] * 3,
        out_specs=(VSPEC,) * 3,
        scratch_shapes=[
            dma_sems(8),
            dma_sems(8),
            dma_sems(2),
            dma_sems(2),
            dma_sems(2, e),
            dma_sems(2, e),
            dma_sems(2, e),
        ],
        compiler_params=params(0),
        name="open_gather",
    )(own, pack_q, pack_o)


def rows_kernel(zn, own_ref, seq_ref, gs, gr):
    place, sends = Place(), Sends()
    greet(place, zn, everyone=False)
    seq_ref[place.p] = own_ref[...]
    rows = PlaneGather(place, sends, seq_ref, gs, gr)
    rows.first()
    rows.second()
    rows.third()
    rows.last()
    sends.finish()


def rows_gather(zn, own):
    rows, width = own.shape
    return pl.pallas_call(
        functools.partial(rows_kernel, zn),
        out_shape=jax.ShapeDtypeStruct((PLANE, rows, width), bf16),
        in_specs=[VSPEC],
        out_specs=VSPEC,
        scratch_shapes=[dma_sems(8), dma_sems(8)],
        compiler_params=params(1),
        name="rows_gather",
    )(own)


def rows_sum_kernel(zn, part_ref, out_ref, *rest):
    scratch, (ss, rs) = rest[:5], rest[5:]
    place, sends = Place(), Sends()
    greet(place, zn, everyone=False)
    red = PlaneReduce(place, sends, part_ref, out_ref, scratch, ss, rs)
    for k in range(4):
        red.first(k)
    for k in range(4):
        red.second(k)
    red.third()
    red.finish()
    sends.finish()


def rows_sum(zn, part):
    _, rows, width = part.shape
    return pl.pallas_call(
        functools.partial(rows_sum_kernel, zn),
        out_shape=jax.ShapeDtypeStruct((rows, width), f32),
        in_specs=[VSPEC],
        out_specs=VSPEC,
        scratch_shapes=PlaneReduce.scratch(rows, width) + [dma_sems(10), dma_sems(10)],
        compiler_params=params(2),
        name="rows_sum",
    )(part)


def send_kernel(
    zn, cap, chunk, norm_ref, grad_ref, slot_ref, mix_ref, an_ref, ag_ref, so_ref, mo_ref,
    nb, gb, sn, sg, hot, mixrow, zs, zr, ts, tr, xs, xr,
):
    place, sends = Place(), Sends()
    pc = place
    greet(place, zn)
    width = norm_ref.shape[1]
    chunks = width // chunk
    tok = norm_ref.shape[0]
    far = [(pc.z + k) % zn for k in range(1, zn)]
    for k, d in enumerate(far):
        back = pc.z
        for i, (src, dst) in enumerate(((slot_ref, so_ref), (mix_ref, mo_ref))):
            sends.start(
                src.at[d], dst.at[back], ts.at[i, k], tr.at[i, back], pc.at(d, pc.p)
            )
    for c in range(chunks):
        cols = pl.ds(c * chunk, chunk)
        for k, d in enumerate(far):
            for i, (src, dst) in enumerate(((norm_ref, nb), (grad_ref, gb))):
                sends.start(
                    src.at[:, cols],
                    dst.at[pc.z, :, cols],
                    zs.at[i, c, k],
                    zr.at[i, c, pc.z],
                    pc.at(d, pc.p),
                )
    nb[pc.z] = norm_ref[...]
    gb[pc.z] = grad_ref[...]
    so_ref[pc.z] = slot_ref[pc.z]
    mo_ref[pc.z] = mix_ref[pc.z]
    for k, d in enumerate(far):
        arrived(so_ref.at[d], tr.at[0, d])
        arrived(mo_ref.at[d], tr.at[1, d])
    slots = zn * cap
    row = lax.broadcasted_iota(jnp.int32, (slots, tok), 0).astype(f32)
    for p in range(PLANE):
        total = jnp.zeros((slots, 1), f32)
        for z in range(zn):
            want = so_ref[z, pl.ds(p, 1), :] + float(z * cap)
            want = jnp.where(so_ref[z, pl.ds(p, 1), :] < 0, -1.0, want)
            one = jnp.where(row == want, 1.0, 0.0)
            hot[p, :, pl.ds(z * tok, tok)] = one.astype(bf16)
            total = total + jnp.sum(one * mo_ref[z, pl.ds(p, 1), :], axis=1, keepdims=True)
        mixrow[p] = jnp.broadcast_to(total, (slots, 128))
    for c in range(chunks):
        cols = pl.ds(c * chunk, chunk)
        for d in far:
            arrived(nb.at[d, :, cols], zr.at[0, c, d])
            arrived(gb.at[d, :, cols], zr.at[1, c, d])
        rows_n = nb[:, :, cols].reshape(zn * tok, chunk)
        rows_g = gb[:, :, cols].reshape(zn * tok, chunk)

        for k in [1, 2, 3, 4, 5, 6, 7, 0]:
            p = pc.by(k) if k else pc.p
            one = hot[p]
            got_n = jnp.dot(one, rows_n, preferred_element_type=f32).astype(bf16)
            got_g = jnp.dot(one, rows_g, preferred_element_type=f32)
            got_g = (got_g * mixrow[p][:, :1]).astype(bf16)
            if k:
                sn[p, :, cols] = got_n
                sg[p, :, cols] = got_g
                for i, (src, dst) in enumerate(((sn, an_ref), (sg, ag_ref))):
                    sends.start(
                        src.at[p, :, cols],
                        dst.at[pc.p, :, cols],
                        xs.at[i, c, k],
                        xr.at[i, c, k],
                        pc.at(pc.z, p),
                    )
            else:
                an_ref[pc.p, :, cols] = got_n
                ag_ref[pc.p, :, cols] = got_g
    for c in range(chunks):
        cols = pl.ds(c * chunk, chunk)
        for k in range(1, PLANE):
            p = pc.by(k)
            arrived(an_ref.at[p, :, cols], xr.at[0, c, k])
            arrived(ag_ref.at[p, :, cols], xr.at[1, c, k])
    sends.finish()


def send_rows(zn, cap, norm, grad, slot, mix, chunk=512):
    tok, width = norm.shape
    slots = zn * cap
    chunks = width // chunk
    shape = jax.ShapeDtypeStruct((PLANE, slots, width), bf16)
    small = jax.ShapeDtypeStruct(slot.shape, f32)
    return pl.pallas_call(
        functools.partial(send_kernel, zn, cap, chunk),
        out_shape=(shape, shape, small, small),
        in_specs=[VSPEC] * 4,
        out_specs=(VSPEC,) * 4,
        scratch_shapes=[
            pltpu.VMEM((zn, tok, width), bf16),
            pltpu.VMEM((zn, tok, width), bf16),
            pltpu.VMEM((PLANE, slots, width), bf16),
            pltpu.VMEM((PLANE, slots, width), bf16),
            pltpu.VMEM((PLANE, slots, zn * tok), bf16),
            pltpu.VMEM((PLANE, slots, 128), f32),
            dma_sems(2, chunks, zn),
            dma_sems(2, chunks, zn),
            dma_sems(2, zn),
            dma_sems(2, zn),
            dma_sems(2, chunks, PLANE),
            dma_sems(2, chunks, PLANE),
        ],
        compiler_params=params(3),
        name="send_rows",
    )(norm, grad, slot, mix)


def back_kernel(
    zn, chunk, res_ref, pair_ref, dot_ref, comb_ref, hot_ref, mixture_ref, sum_ref, dots_ref,
    rr, rp, rd, zb, zp, zd, am, ap, xs, xr, ds, dr, zs, zr, es, er,
):
    place, sends = Place(), Sends()
    pc = place
    greet(place, zn)
    width = res_ref.shape[2]
    chunks = width // chunk
    tok = mixture_ref.shape[0]
    slots = res_ref.shape[1]
    far = [(pc.z + k) % zn for k in range(1, zn)]
    both = ((pair_ref, rp), (res_ref, rr))
    for k in range(1, PLANE):
        p = pc.by(k)
        sends.start(dot_ref.at[p], rd.at[pc.p], ds.at[k], dr.at[k], pc.at(pc.z, p))
    for i, (src, dst) in enumerate(both):
        for c in range(chunks):
            cols = pl.ds(c * chunk, chunk)
            for k in range(1, PLANE):
                p = pc.by(k)
                sends.start(
                    src.at[p, :, cols],
                    dst.at[pc.p, :, cols],
                    xs.at[i, c, k],
                    xr.at[i, c, k],
                    pc.at(pc.z, p),
                )
    rd[pc.p] = dot_ref[pc.p]
    own = [
        pltpu.make_async_copy(src.at[pc.p], dst.at[pc.p], xr.at[i, 0, 0])
        for i, (src, dst) in enumerate(both)
    ]
    for copy in own:
        copy.start()
    for k in range(1, PLANE):
        arrived(rd.at[pc.by(k)], dr.at[k])
    zd[...] = jnp.dot(
        hot_ref[...], rd[...].reshape(PLANE * slots, 128), preferred_element_type=f32
    ).reshape(zn, tok, 128)
    for k, d in enumerate(far):
        sends.start(zd.at[d], dots_ref.at[pc.z], es.at[k], er.at[pc.z], pc.at(d, pc.p))
    dots_ref[pc.z] = zd[pc.z]
    for i, (buf, mat, out) in enumerate(((rp, hot_ref, zp), (rr, comb_ref, zb))):
        land = (ap, am)[i]
        own[i].wait()
        for c in range(chunks):
            cols = pl.ds(c * chunk, chunk)
            for k in range(1, PLANE):
                arrived(buf.at[pc.by(k), :, cols], xr.at[i, c, k])
            got = jnp.dot(
                mat[...],
                buf[:, :, cols].reshape(PLANE * slots, chunk),
                preferred_element_type=f32,
            )
            out[:, :, cols] = got.astype(bf16).reshape(zn, tok, chunk)
            for k, d in enumerate(far):
                sends.start(
                    out.at[d, :, cols],
                    land.at[pc.z, :, cols],
                    zs.at[i, c, k],
                    zr.at[i, c, pc.z],
                    pc.at(d, pc.p),
                )
    for i, (land, out, dst) in enumerate(((ap, zp, sum_ref), (am, zb, mixture_ref))):
        for c in range(chunks):
            cols = pl.ds(c * chunk, chunk)
            total = out[pc.z, :, cols].astype(f32)
            for d in far:
                arrived(land.at[d, :, cols], zr.at[i, c, d])
                total = total + land[d, :, cols].astype(f32)
            dst[:, cols] = total
    for d in far:
        arrived(dots_ref.at[d], er.at[d])
    sends.finish()


def back_rows(zn, tok, res, pair, dots, comb, hot, chunk=512):
    _, slots, width = res.shape
    chunks = width // chunk
    shape = jax.ShapeDtypeStruct((tok, width), f32)
    return pl.pallas_call(
        functools.partial(back_kernel, zn, chunk),
        out_shape=(shape, shape, jax.ShapeDtypeStruct((zn, tok, 128), f32)),
        in_specs=[ASPEC] * 2 + [VSPEC] * 3,
        out_specs=(VSPEC,) * 3,
        scratch_shapes=[
            pltpu.VMEM((PLANE, slots, width), bf16),
            pltpu.VMEM((PLANE, slots, width), bf16),
            pltpu.VMEM((PLANE, slots, 128), bf16),
            pltpu.VMEM((zn, tok, width), bf16),
            pltpu.VMEM((zn, tok, width), bf16),
            pltpu.VMEM((zn, tok, 128), f32),
            pltpu.VMEM((zn, tok, width), bf16),
            pltpu.VMEM((zn, tok, width), bf16),
            dma_sems(2, chunks, PLANE),
            dma_sems(2, chunks, PLANE),
            dma_sems(PLANE),
            dma_sems(PLANE),
            dma_sems(2, chunks, zn),
            dma_sems(2, chunks, zn),
            dma_sems(zn),
            dma_sems(zn),
        ],
        compiler_params=params(4),
        name="back_rows",
    )(res, pair, dots, comb, hot)


class ColumnReduce:
    def __init__(self, place, sends, zn, part, up, down, give, take, out, ss_r, ss_l, rs_r, rs_l, ps, pr):
        self.place, self.sends, self.zn = place, sends, zn
        self.part, self.up, self.down, self.give, self.take, self.out = part, up, down, give, take, out
        self.ss_r, self.ss_l, self.rs_r, self.rs_l, self.ps, self.pr = ss_r, ss_l, rs_r, rs_l, ps, pr

    def _hop(self, buf, rs, ss, d, start, inner, device):
        rows = self.part.shape[2]

        def add():
            arrived(buf.at[d], rs.at[d])
            for h in range(2):

                def put(at, v):
                    buf[d, h, at, :] = v.astype(bf16)

                add_rows(
                    put,
                    lambda at: self.part[d, h, at, :],
                    lambda at: buf[d, h, at, :],
                    rows,
                )

        pl.when(jnp.logical_and(start, inner))(add)
        self.sends.start(
            buf.at[d], buf.at[d], ss.at[d], rs.at[d], device, jnp.logical_and(start, inner)
        )
        self.sends.start(
            self.part.at[d],
            buf.at[d],
            ss.at[d],
            rs.at[d],
            device,
            jnp.logical_and(start, jnp.logical_not(inner)),
        )

    def step(self, k):
        pc, zn = self.place, self.zn
        d = zn - 1 - k
        right = pc.at(jnp.minimum(pc.z + 1, zn - 1), pc.p)
        left = pc.at(jnp.maximum(pc.z - 1, 0), pc.p)
        self._hop(self.up, self.rs_r, self.ss_r, d, pc.z < d, pc.z > 0, right)
        d = k
        self._hop(self.down, self.rs_l, self.ss_l, d, pc.z > d, pc.z < zn - 1, left)

    def pair(self):
        pc, zn = self.place, self.zn
        rows = self.part.shape[2]
        lower, upper = pc.z > 0, pc.z < zn - 1
        arrived(self.up.at[pc.z], self.rs_r.at[pc.z], lower)
        arrived(self.down.at[pc.z], self.rs_l.at[pc.z], upper)

        def total(h, at):
            v = self.part[pc.z, h, at, :].astype(f32)
            v = v + jnp.where(lower, self.up[pc.z, h, at, :].astype(f32), 0.0)
            return v + jnp.where(upper, self.down[pc.z, h, at, :].astype(f32), 0.0)

        def give(i, carry):
            at = pl.ds(pl.multiple_of(i * 32, 32), 32)
            self.give[at, :] = total(1 - pc.y, at).astype(bf16)
            return carry

        lax.fori_loop(0, rows // 32, give, 0)
        self.sends.start(self.give, self.take, self.ps, self.pr, pc.peer(dy=1))

        def keep(i, carry):
            at = pl.ds(pl.multiple_of(i * 32, 32), 32)
            self.out[pc.y, at, :] = total(pc.y, at)
            return carry

        lax.fori_loop(0, rows // 32, keep, 0)

    def finish(self):
        pc = self.place
        arrived(self.take, self.pr)
        self.out[1 - pc.y] = self.take[...].astype(f32)


def close_kernel(
    zn, part_ref, gq_ref, go_ref, out_ref, oq_ref, oo_ref,
    c1, s1, ra, rb, last, uq, dq, uo, do, vq, tq, vo, to, gs, gr, sr, sl, rr, rl, ps, pr,
):
    place, sends = Place(), Sends()
    greet(place, zn)
    rows = PlaneReduce(place, sends, part_ref, out_ref, (c1, s1, ra, rb, last), gs, gr)
    o = ColumnReduce(
        place, sends, zn, go_ref, uo, do, vo, to, oo_ref,
        sr.at[1], sl.at[1], rr.at[1], rl.at[1], ps.at[1], pr.at[1],
    )
    q = ColumnReduce(
        place, sends, zn, gq_ref, uq, dq, vq, tq, oq_ref,
        sr.at[0], sl.at[0], rr.at[0], rl.at[0], ps.at[0], pr.at[0],
    )
    for k in range(4):
        rows.first(k)
    o.step(0)
    q.step(0)
    for k in range(4):
        rows.second(k)
    rows.third()
    for k in range(1, zn - 1):
        o.step(k)
        q.step(k)
    o.pair()
    q.pair()
    rows.finish()
    o.finish()
    q.finish()
    sends.finish()


def close_sum(zn, part, gq, go):
    _, rows, width = part.shape
    _, _, r, wq = gq.shape
    wo = go.shape[3]
    return pl.pallas_call(
        functools.partial(close_kernel, zn),
        out_shape=(
            jax.ShapeDtypeStruct((rows, width), f32),
            jax.ShapeDtypeStruct((2, r, wq), f32),
            jax.ShapeDtypeStruct((2, r, wo), f32),
        ),
        in_specs=[VSPEC] * 3,
        out_specs=(VSPEC,) * 3,
        scratch_shapes=PlaneReduce.scratch(rows, width)
        + [
            pltpu.VMEM((zn, 2, r, wq), bf16),
            pltpu.VMEM((zn, 2, r, wq), bf16),
            pltpu.VMEM((zn, 2, r, wo), bf16),
            pltpu.VMEM((zn, 2, r, wo), bf16),
            pltpu.VMEM((r, wq), bf16),
            pltpu.VMEM((r, wq), bf16),
            pltpu.VMEM((r, wo), bf16),
            pltpu.VMEM((r, wo), bf16),
            dma_sems(10),
            dma_sems(10),
            dma_sems(2, zn),
            dma_sems(2, zn),
            dma_sems(2, zn),
            dma_sems(2, zn),
            dma_sems(2),
            dma_sems(2),
        ],
        compiler_params=params(5),
        name="close_sum",
    )(part, gq, go)


def small_kernel(zn, in_ref, out_ref, l1, mid, l2, as_, ar, bs, br, cs, cr):
    place, sends = Place(), Sends()
    pc = place
    greet(place, zn)
    far = [(pc.z + k) % zn for k in range(1, zn)]
    for k in range(1, PLANE):
        p = pc.by(k)
        sends.start(in_ref.at[p], l1.at[k], as_.at[k], ar.at[k], pc.at(pc.z, p))
    total = in_ref[pc.p]
    for k in range(1, PLANE):
        arrived(l1.at[k], ar.at[k])
        total = total + l1[k]
    mid[...] = total
    for k, d in enumerate(far):
        sends.start(mid, l2.at[pc.z], bs.at[k], br.at[pc.z], pc.at(d, pc.p))
    l2[pc.z] = total
    for d in far:
        arrived(l2.at[d], br.at[d])
    total = l2[0]
    for z in range(1, zn):
        total = total + l2[z]
    out_ref[pc.p] = total
    for k in range(1, PLANE):
        p = pc.by(k)
        sends.start(out_ref.at[pc.p], out_ref.at[pc.p], cs.at[k], cr.at[k], pc.at(pc.z, p))
    for k in range(1, PLANE):
        p = pc.by(k)
        arrived(out_ref.at[p], cr.at[k])
    sends.finish()


def small_sum(zn, flat):
    _, rows, lanes = flat.shape
    return pl.pallas_call(
        functools.partial(small_kernel, zn),
        out_shape=jax.ShapeDtypeStruct(flat.shape, f32),
        in_specs=[VSPEC],
        out_specs=VSPEC,
        scratch_shapes=[
            pltpu.VMEM((PLANE, rows, lanes), f32),
            pltpu.VMEM((rows, lanes), f32),
            pltpu.VMEM((zn, rows, lanes), f32),
            dma_sems(PLANE),
            dma_sems(PLANE),
            dma_sems(zn),
            dma_sems(zn),
            dma_sems(PLANE),
            dma_sems(PLANE),
        ],
        compiler_params=params(6),
        name="small_sum",
    )(flat)


def local(
    tokens,
    out_grad,
    first_gain,
    second_gain,
    query_gain,
    key_gain,
    query_weight,
    key_weight,
    value_weight,
    output_weight,
    router_weight,
    gate_weight,
    up_weight,
    down_weight,
    expert_ids,
    router_order,
    image_starts,
):
    tok, width = tokens.shape
    zn = lax.axis_size("exp") // 2
    experts = PLANE * zn
    cap = (9 * tok * TOP + 8 * experts - 1) // (8 * experts)
    slots = zn * cap
    length = PLANE * tok
    own_rows = query_weight.shape[0]
    half = query_weight.shape[1] // 2
    heads = half // HD
    scale = HD ** (-0.5)
    exp_index = lax.axis_index("exp")
    starts = lax.dynamic_slice_in_dim(image_starts, exp_index // 2, 1, 0)[0]

    expert_axis = jnp.arange(experts, dtype=jnp.int32)
    member = jnp.any(expert_ids[:, :, None] == expert_axis[None, None, :], axis=1)
    order_here = router_order[0]
    earlier = (order_here[None, :] < order_here[:, None]).astype(bf16)
    counts = jnp.dot(earlier, member.astype(bf16), preferred_element_type=f32)
    keep = member & (counts < cap)
    slot_of = jnp.where(keep, counts, -1.0)

    resid_in = tokens.astype(f32)
    first_rms = rms_scale(resid_in)
    first_hat = resid_in * first_rms
    first_norm = (first_hat * first_gain).astype(bf16)
    q_halves = query_weight.reshape(own_rows, 2, half).transpose(1, 0, 2)
    kv = jnp.concatenate([key_weight, value_weight], axis=1)
    pack_q = jnp.concatenate([q_halves, jnp.broadcast_to(kv[None], (2,) + kv.shape)], axis=2)
    pack_o = output_weight.reshape(2, half, own_rows).transpose(0, 2, 1)
    seq_norm, full_q, full_o = open_gather(zn, first_norm, pack_q, pack_o)
    seq_norm = seq_norm.reshape(length, width)
    full_q = full_q.reshape(width, half + 2 * HD)
    full_o = full_o.reshape(width, half)
    pre = jnp.dot(seq_norm, full_q, preferred_element_type=f32)
    query_pre = pre[:, :half].reshape(length, heads, HD)
    key_pre = pre[:, half : half + HD]
    value_rows = pre[:, half + HD :].astype(bf16)
    pos = jnp.arange(length, dtype=jnp.int32)
    cosine, sine = rotary_tables(pos, HD)
    query_rms = rms_scale(query_pre)
    query_hat = query_pre * query_rms
    query_rot = rotate(query_hat * query_gain, cosine[:, None, :], sine[:, None, :]).astype(bf16)
    key_rms = rms_scale(key_pre)
    key_hat = key_pre * key_rms
    key_rot = rotate(key_hat * key_gain, cosine, sine).astype(bf16)
    pieces = piece_ids(pos, starts)
    mask = allowed_mask(pos, pos, pieces, pieces)

    def scores_of():
        scores = jnp.einsum("qhd,kd->hqk", query_rot, key_rot, preferred_element_type=f32) * scale
        return jnp.where(mask[None], scores, NEGATIVE)

    scores = scores_of()
    top_score = jnp.max(scores, axis=-1, keepdims=True)
    expo = jnp.exp(scores - top_score)
    total = jnp.sum(expo, axis=-1, keepdims=True)
    probs_low = (expo / total).astype(bf16)
    log_norm = top_score + jnp.log(total)
    context = jnp.einsum("hqk,kd->qhd", probs_low, value_rows, preferred_element_type=f32)
    context_rows = context.astype(bf16).reshape(length, half)
    part = lax.dot_general(
        context_rows, full_o, (((1,), (1,)), ((), ())), preferred_element_type=f32
    )
    attention = rows_sum(zn, part.astype(bf16).reshape(PLANE, tok, width))
    resid_mid = resid_in + attention
    second_rms = rms_scale(resid_mid)
    second_hat = resid_mid * second_rms
    second_norm = (second_hat * second_gain).astype(bf16)
    logits = jnp.dot(second_norm, router_weight, preferred_element_type=f32)
    mix = jax.nn.softmax(jnp.where(member, logits, NEGATIVE), axis=-1)
    mix = jnp.where(member, mix, 0.0)
    keep_mix = jnp.where(keep, mix, 0.0)
    slot_t = slot_of.T.reshape(zn, PLANE, tok)
    mix_t = keep_mix.T.reshape(zn, PLANE, tok)
    rows_n, rows_g, slots_all, mix_all = send_rows(zn, cap, second_norm, out_grad, slot_t, mix_t)
    arrived_n = rows_n.reshape(PLANE * slots, width)
    arrived_g = rows_g.reshape(PLANE * slots, width)

    gate_val = jnp.dot(arrived_n, gate_weight[0], preferred_element_type=f32)
    up_val = jnp.dot(arrived_n, up_weight[0], preferred_element_type=f32)
    gate_sig = jax.nn.sigmoid(gate_val)
    gate_act = gate_val * gate_sig
    inner = (gate_act * up_val).astype(bf16)
    result = jnp.dot(inner, down_weight[0], preferred_element_type=f32).astype(bf16)
    inner_grad = jnp.dot(arrived_g, down_weight[0].T, preferred_element_type=f32)
    down_grad = jnp.dot(inner.T, arrived_g, preferred_element_type=f32)[None]
    gate_back = (inner_grad * up_val * gate_sig * (1.0 + gate_val * (1.0 - gate_sig))).astype(bf16)
    up_back = (inner_grad * gate_act).astype(bf16)
    gate_grad = jnp.dot(arrived_n.T, gate_back, preferred_element_type=f32)[None]
    up_grad = jnp.dot(arrived_n.T, up_back, preferred_element_type=f32)[None]
    pair_back = jnp.dot(gate_back, gate_weight[0].T, preferred_element_type=f32) + jnp.dot(
        up_back, up_weight[0].T, preferred_element_type=f32
    )
    pair_back = pair_back.astype(bf16)
    dots = jnp.sum(arrived_g.astype(f32) * result.astype(f32), axis=1, keepdims=True)
    dots_high = dots.astype(bf16)
    dots_low = (dots - dots_high.astype(f32)).astype(bf16)
    place = (exp_index % 2) * 4 + lax.axis_index("tp")
    lane = jnp.arange(128, dtype=jnp.int32)[None, :]
    zero = jnp.zeros((), bf16)
    dot_lanes = jnp.where(lane == place, dots_high, zero) + jnp.where(
        lane == place + PLANE, dots_low, zero
    )

    slot_col = slots_all.transpose(0, 2, 1).reshape(zn, tok, PLANE, 1)
    mix_col = mix_all.transpose(0, 2, 1).reshape(zn, tok, PLANE, 1)
    want = jnp.where(slot_col < 0, -1.0, slot_col + (jnp.arange(zn, dtype=f32) * cap)[:, None, None, None])
    hot = want == jnp.arange(slots, dtype=f32)[None, None, None, :]
    comb = jnp.where(hot, mix_col, 0.0).astype(bf16).reshape(zn * tok, PLANE * slots)
    hot = hot.astype(bf16).reshape(zn * tok, PLANE * slots)
    mixture, pairs_sum, dots_all = back_rows(
        zn,
        tok,
        result.reshape(PLANE, slots, width),
        pair_back.reshape(PLANE, slots, width),
        dot_lanes.reshape(PLANE, slots, 128),
        comb,
        hot,
    )
    block_out = (resid_mid + mixture).astype(bf16)
    grad_out = out_grad.astype(f32)
    mix_dots = dots_all[:, :, :PLANE] + dots_all[:, :, PLANE : 2 * PLANE]
    mix_dots = mix_dots.transpose(1, 0, 2).reshape(tok, experts)
    chosen_grad = mix_dots - mix * jnp.sum(mix_dots, axis=1, keepdims=True)
    logit_grad = chosen_grad.astype(bf16)
    router_part = jnp.dot(second_norm.T, logit_grad, preferred_element_type=f32)
    norm2_back = pairs_sum + jnp.dot(logit_grad, router_weight.T, preferred_element_type=f32)
    mid_from_norm, second_gain_part = norm_back(norm2_back, second_hat, second_rms, second_gain)
    middle_grad = grad_out + mid_from_norm

    seq_grad = rows_gather(zn, middle_grad.astype(bf16)).reshape(length, width)
    output_part = lax.dot_general(
        seq_grad, context_rows, (((0,), (0,)), ((), ())), preferred_element_type=f32
    )
    context_back = jnp.dot(seq_grad, full_o, preferred_element_type=f32).astype(bf16)
    context_back = context_back.reshape(length, heads, HD)
    probs = jnp.exp(scores_of() - log_norm)
    value_back = jnp.einsum(
        "hqk,qhd->kd", probs.astype(bf16), context_back, preferred_element_type=f32
    )
    probs_back = jnp.einsum("qhd,kd->hqk", context_back, value_rows, preferred_element_type=f32)
    delta = jnp.sum(probs * probs_back, axis=-1, keepdims=True)
    score_back = (probs * (probs_back - delta)).astype(bf16)
    rot_query_back = (
        jnp.einsum("hqk,kd->qhd", score_back, key_rot, preferred_element_type=f32) * scale
    )
    rot_key_back = (
        jnp.einsum("hqk,qhd->kd", score_back, query_rot, preferred_element_type=f32) * scale
    )
    query_gained = unrotate(rot_query_back, cosine[:, None, :], sine[:, None, :])
    query_back, query_gain_part = norm_back(query_gained, query_hat, query_rms, query_gain)
    key_gained = unrotate(rot_key_back, cosine, sine)
    key_back, key_gain_part = norm_back(key_gained, key_hat, key_rms, key_gain)
    all_back = jnp.concatenate(
        [query_back.reshape(length, half), key_back, value_back], axis=1
    ).astype(bf16)
    grad_q = lax.dot_general(
        seq_norm, all_back, (((0,), (0,)), ((), ())), preferred_element_type=f32
    )
    norm1_part = lax.dot_general(
        all_back, full_q, (((1,), (1,)), ((), ())), preferred_element_type=f32
    )
    norm1_back, sum_q, sum_o = close_sum(
        zn,
        norm1_part.astype(bf16).reshape(PLANE, tok, width),
        grad_q.astype(bf16).reshape(zn, 2, own_rows, half + 2 * HD),
        output_part.astype(bf16).reshape(zn, 2, own_rows, half),
    )
    query_grad = jnp.concatenate([sum_q[0, :, :half], sum_q[1, :, :half]], axis=1)
    kv_grad = sum_q[0, :, half:] + sum_q[1, :, half:]
    key_grad, value_grad = kv_grad[:, :HD], kv_grad[:, HD:]
    output_grad = jnp.concatenate([sum_o[0].T, sum_o[1].T], axis=0)
    tok_from_norm, first_gain_part = norm_back(norm1_back, first_hat, first_rms, first_gain)
    tokens_grad = middle_grad + tok_from_norm

    flat = jnp.concatenate(
        [
            router_part.reshape(-1),
            first_gain_part,
            second_gain_part,
            query_gain_part,
            key_gain_part,
        ]
    )
    count = flat.shape[0]
    unit = PLANE * 8 * 128
    padded = -(-count // unit) * unit
    flat = jnp.pad(flat, (0, padded - count)).reshape(PLANE, padded // (PLANE * 128), 128)
    flat = small_sum(zn, flat).reshape(-1)
    n_router = width * experts
    router_grad = flat[:n_router].reshape(width, experts)
    rest = flat[n_router:]
    first_gain_grad = rest[:width]
    second_gain_grad = rest[width : 2 * width]
    query_gain_grad = rest[2 * width : 2 * width + HD]
    key_gain_grad = rest[2 * width + HD : 2 * width + 2 * HD]
    return (
        block_out,
        tokens_grad,
        first_gain_grad,
        second_gain_grad,
        query_gain_grad,
        key_gain_grad,
        query_grad,
        key_grad,
        value_grad,
        output_grad,
        router_grad,
        gate_grad,
        up_grad,
        down_grad,
    )


def solution(mesh):
    both = ("exp", "tp")
    in_specs = (
        P(both, None),
        P(both, None),
        P(),
        P(),
        P(),
        P(),
        P("exp", "tp"),
        P("exp", "tp"),
        P("exp", "tp"),
        P("tp", "exp"),
        P(),
        P(both, None, None),
        P(both, None, None),
        P(both, None, None),
        P(both, None),
        P(both, None),
        P(),
    )
    out_specs = (
        P(both, None),
        P(both, None),
        P(),
        P(),
        P(),
        P(),
        P("exp", "tp"),
        P("exp", "tp"),
        P("exp", "tp"),
        P("tp", "exp"),
        P(),
        P(both, None, None),
        P(both, None, None),
        P(both, None, None),
    )
    return jax.shard_map(local, mesh=mesh, in_specs=in_specs, out_specs=out_specs, check_vma=False)
```

```python
import functools

import jax
import jax.numpy as jnp
from jax import lax
from jax.experimental import pallas as pl
from jax.experimental.pallas import tpu as pltpu
from jax.sharding import PartitionSpec as P

HD = 128
TOP = 8
IMG_LEN = 256
PLANE = 8

EPSILON = 1e-06
THETA = 1000000.0
NEGATIVE = -1e30

MESH = pl.DeviceIdType.MESH
f32 = jnp.float32
bf16 = jnp.bfloat16
VMEM_LIMIT = 60 << 20


def rms_scale(values):
    return lax.rsqrt(jnp.mean(values * values, axis=-1, keepdims=True) + EPSILON)


def rotary_tables(positions, width):
    half = width // 2
    freqs = THETA ** (-(jnp.arange(half, dtype=f32) * 2.0 / width))
    angles = positions.astype(f32)[:, None] * freqs[None, :]
    return (jnp.cos(angles), jnp.sin(angles))


def rotate(values, cosine, sine):
    half = values.shape[-1] // 2
    first = values[..., :half]
    second = values[..., half:]
    return jnp.concatenate(
        [first * cosine - second * sine, second * cosine + first * sine], axis=-1
    )


def unrotate(values, cosine, sine):
    half = values.shape[-1] // 2
    first = values[..., :half]
    second = values[..., half:]
    return jnp.concatenate(
        [first * cosine + second * sine, second * cosine - first * sine], axis=-1
    )


def piece_ids(positions, starts):
    inside = (positions[:, None] >= starts[None, :]) & (
        positions[:, None] < starts[None, :] + IMG_LEN
    )
    labels = jnp.arange(1, starts.shape[0] + 1, dtype=jnp.int32)
    return jnp.sum(jnp.where(inside, labels[None, :], 0), axis=1)


def allowed_mask(query_pos, key_pos, query_piece, key_piece):
    causal = key_pos[None, :] <= query_pos[:, None]
    same = (query_piece[:, None] == key_piece[None, :]) & (query_piece[:, None] > 0)
    return causal | same


def norm_back(grad_norm, hat, rms, gain):
    scaled = grad_norm * gain
    inner_mean = jnp.mean(scaled * hat, axis=-1, keepdims=True)
    lead_axes = tuple(range(grad_norm.ndim - 1))
    return (rms * (scaled - hat * inner_mean), jnp.sum(grad_norm * hat, axis=lead_axes))


class Place:
    def __init__(self):
        self.e = lax.axis_index("exp")
        self.t = lax.axis_index("tp")
        self.z = self.e // 2
        self.y = self.e % 2
        self.x = self.t // 2
        self.c = self.t % 2
        self.p = self.y * 4 + self.t

    def at(self, z, p):
        return (z * 2 + p // 4, p % 4)

    def flip(self, dy=0, dx=0, dc=0):
        y = 1 - self.y if dy else self.y
        x = 1 - self.x if dx else self.x
        c = 1 - self.c if dc else self.c
        return y * 4 + x * 2 + c

    def peer(self, dy=0, dx=0, dc=0):
        return self.at(self.z, self.flip(dy, dx, dc))

    def by(self, k):
        return self.flip((k >> 2) & 1, (k >> 1) & 1, k & 1)


class Sends:
    def __init__(self):
        self.kept = []

    def start(self, src, dst, send_sem, recv_sem, device, when=None):
        def make():
            return pltpu.make_async_remote_copy(
                src_ref=src,
                dst_ref=dst,
                send_sem=send_sem,
                recv_sem=recv_sem,
                device_id=device,
                device_id_type=MESH,
            )

        def go():
            make().start()

        if when is None:
            go()
        else:
            pl.when(when)(go)
        self.kept.append((make, when))

    def finish(self):
        for make, when in self.kept:
            if when is None:
                make().wait_send()
            else:
                pl.when(when)(lambda make=make: make().wait_send())
        self.kept = []


def arrived(dst, recv_sem, when=None):
    def go():
        pltpu.make_async_copy(dst, dst, recv_sem).wait()

    if when is None:
        go()
    else:
        pl.when(when)(go)


def greet(place, zn, ends=False, everyone=True, planes=True):
    bar = pltpu.get_barrier_semaphore()
    count = 0
    if planes:
        for k in range(1, PLANE):
            pl.semaphore_signal(
                bar, inc=1, device_id=place.at(place.z, place.by(k)), device_id_type=MESH
            )
        count += PLANE - 1
    if everyone:
        for k in range(1, zn):
            pl.semaphore_signal(
                bar,
                inc=1,
                device_id=place.at((place.z + k) % zn, place.p),
                device_id_type=MESH,
            )
        count += zn - 1
    pl.semaphore_wait(bar, count)
    if ends:
        bar2 = 0
        del bar2


class PlaneGather:
    sems = 8

    def __init__(self, place, sends, buf, ss, rs):
        self.place, self.sends, self.buf, self.ss, self.rs = place, sends, buf, ss, rs
        half = buf.shape[2] // 2
        self.cols_a = pl.ds(0, half)
        self.cols_b = pl.ds(half, half)

    def _send(self, block, which, device, cols=None):
        ref = self.buf.at[block] if cols is None else self.buf.at[block, :, cols]
        self.sends.start(ref, ref, self.ss.at[which], self.rs.at[which], device)

    def _wait(self, block, which, cols=None):
        ref = self.buf.at[block] if cols is None else self.buf.at[block, :, cols]
        arrived(ref, self.rs.at[which])

    def first(self):
        pc = self.place
        self._send(pc.p, 0, pc.peer(dy=1))
        self._send(pc.p, 1, pc.peer(dx=1))
        self._send(pc.p, 2, pc.peer(dc=1))

    def second(self):
        pc = self.place
        px, py = pc.flip(dx=1), pc.flip(dy=1)
        self._wait(px, 1)
        self._send(px, 3, pc.peer(dy=1), self.cols_a)
        self._send(px, 4, pc.peer(dc=1))
        self._wait(py, 0)
        self._send(py, 5, pc.peer(dx=1), self.cols_b)
        self._send(py, 6, pc.peer(dc=1))

    def third(self):
        pc = self.place
        pd = pc.flip(dy=1, dx=1)
        self._wait(pd, 3, self.cols_a)
        self._wait(pd, 5, self.cols_b)
        self._send(pd, 7, pc.peer(dc=1))

    def last(self):
        pc = self.place
        self._wait(pc.flip(dc=1), 2)
        self._wait(pc.flip(dc=1, dx=1), 4)
        self._wait(pc.flip(dc=1, dy=1), 6)
        self._wait(pc.flip(dc=1, dy=1, dx=1), 7)


def add_rows(dst, first, second, rows, step=32):
    def body(i, carry):
        at = pl.ds(pl.multiple_of(i * step, step), step)
        dst(at, first(at).astype(f32) + second(at).astype(f32))
        return carry

    lax.fori_loop(0, rows // step, body, 0)


class PlaneReduce:
    sems = 4 + 4 + 2

    @staticmethod
    def scratch(rows, width):
        return [
            pltpu.VMEM((4, rows, width), bf16),
            pltpu.VMEM((4, rows, width), bf16),
            pltpu.VMEM((2, rows, width // 2), bf16),
            pltpu.VMEM((2, rows, width // 2), bf16),
            pltpu.VMEM((2, rows, width // 2), bf16),
        ]

    def __init__(self, place, sends, part, out, scratch, ss, rs):
        self.place, self.sends, self.part, self.out = place, sends, part, out
        self.c1, self.s1, self.ra, self.rb, self.last = scratch
        self.ss, self.rs = ss, rs
        self.rows = part.shape[1]
        half = part.shape[2] // 2
        self.half = half
        self.cols_a = pl.ds(0, half)
        self.cols_b = pl.ds(half, half)
        pc = place
        self.chips = [(1, 1), (0, 1), (1, 0), (0, 0)]

    def _chip(self, dy, dx):
        pc = self.place
        y = 1 - pc.y if dy else pc.y
        x = 1 - pc.x if dx else pc.x
        return y, x, y * 2 + x

    def first(self, k):
        pc = self.place
        y, x, j = self._chip(*self.chips[k])
        block = y * 4 + x * 2 + (1 - pc.c)
        self.sends.start(
            self.part.at[block], self.c1.at[j], self.ss.at[k], self.rs.at[k], pc.peer(dc=1)
        )

    def second(self, k):
        pc = self.place
        y, x, j = self._chip(*self.chips[k])
        arrived(self.c1.at[j], self.rs.at[k])
        mine = y * 4 + x * 2 + pc.c

        def put(at, v):
            self.s1[j, at, :] = v.astype(bf16)

        add_rows(put, lambda at: self.part[mine, at, :], lambda at: self.c1[j, at, :], self.rows)
        dy, dx = self.chips[k]
        if dx:
            self.sends.start(
                self.s1.at[j, :, self.cols_a],
                self.ra.at[y],
                self.ss.at[4 + (0 if dy else 1)],
                self.rs.at[4 + (0 if dy else 1)],
                pc.peer(dx=1),
            )
        if dy:
            self.sends.start(
                self.s1.at[j, :, self.cols_b],
                self.rb.at[x],
                self.ss.at[6 + (0 if dx else 1)],
                self.rs.at[6 + (0 if dx else 1)],
                pc.peer(dy=1),
            )

    def third(self):
        pc = self.place
        other_y, other_x = 1 - pc.y, 1 - pc.x
        arrived(self.ra.at[other_y], self.rs.at[4])
        j = other_y * 2 + pc.x

        def put_a(at, v):
            self.ra[other_y, at, :] = v.astype(bf16)

        add_rows(
            put_a,
            lambda at: self.s1[j, at, self.cols_a],
            lambda at: self.ra[other_y, at, :],
            self.rows,
        )
        self.sends.start(
            self.ra.at[other_y], self.last.at[0], self.ss.at[8], self.rs.at[8], pc.peer(dy=1)
        )
        arrived(self.rb.at[other_x], self.rs.at[6])
        i = pc.y * 2 + other_x

        def put_b(at, v):
            self.rb[other_x, at, :] = v.astype(bf16)

        add_rows(
            put_b,
            lambda at: self.s1[i, at, self.cols_b],
            lambda at: self.rb[other_x, at, :],
            self.rows,
        )
        self.sends.start(
            self.rb.at[other_x], self.last.at[1], self.ss.at[9], self.rs.at[9], pc.peer(dx=1)
        )

    def finish(self):
        pc = self.place
        own = pc.y * 2 + pc.x
        arrived(self.ra.at[pc.y], self.rs.at[5])
        arrived(self.rb.at[pc.x], self.rs.at[7])

        def put_a(at, v):
            self.out[at, self.cols_a] = v + self.ra[pc.y, at, :].astype(f32)

        def put_b(at, v):
            self.out[at, self.cols_b] = v + self.rb[pc.x, at, :].astype(f32)

        arrived(self.last.at[0], self.rs.at[8])
        add_rows(
            put_a,
            lambda at: self.s1[own, at, self.cols_a],
            lambda at: self.last[0, at, :],
            self.rows,
        )
        arrived(self.last.at[1], self.rs.at[9])
        add_rows(
            put_b,
            lambda at: self.s1[own, at, self.cols_b],
            lambda at: self.last[1, at, :],
            self.rows,
        )


class ColumnGather:
    def __init__(self, place, sends, zn, pack, full, pair_ss, pair_rs, ss_r, ss_l, rs):
        self.place, self.sends, self.zn = place, sends, zn
        self.pack, self.full = pack, full
        self.pair_ss, self.pair_rs, self.ss_r, self.ss_l, self.rs = pair_ss, pair_rs, ss_r, ss_l, rs

    def _on(self, src, piece, right, left):
        pc = self.place
        if right is not None:
            self.sends.start(
                src,
                self.full.at[piece],
                self.ss_r.at[piece],
                self.rs.at[piece],
                pc.at(jnp.minimum(pc.z + 1, self.zn - 1), pc.p),
                right,
            )
        if left is not None:
            self.sends.start(
                src,
                self.full.at[piece],
                self.ss_l.at[piece],
                self.rs.at[piece],
                pc.at(jnp.maximum(pc.z - 1, 0), pc.p),
                left,
            )

    def pair(self):
        pc = self.place
        self.sends.start(
            self.pack.at[1 - pc.y],
            self.full.at[pc.e],
            self.pair_ss,
            self.pair_rs,
            pc.peer(dy=1),
        )

    def own(self):
        pc = self.place
        self._on(self.pack.at[pc.y], pc.e, pc.z < self.zn - 1, pc.z > 0)

    def keep(self):
        pc = self.place
        self.full[pc.e] = self.pack[pc.y]

    def partner(self):
        pc = self.place
        other = pc.z * 2 + 1 - pc.y
        arrived(self.full.at[other], self.pair_rs)
        self._on(self.full.at[other], other, pc.z < self.zn - 1, pc.z > 0)

    def step(self, k):
        pc = self.place
        for first in (True, False):
            y = pc.y if first else 1 - pc.y
            below = jnp.maximum(pc.z - k, 0) * 2 + y
            has = pc.z - k >= 0
            arrived(self.full.at[below], self.rs.at[below], has)
            self._on(
                self.full.at[below], below, jnp.logical_and(has, pc.z < self.zn - 1), None
            )
            above = jnp.minimum(pc.z + k, self.zn - 1) * 2 + y
            has = pc.z + k < self.zn
            arrived(self.full.at[above], self.rs.at[above], has)
            self._on(self.full.at[above], above, None, jnp.logical_and(has, pc.z > 0))


def dma_sems(*shape):
    return pltpu.SemaphoreType.DMA(shape)


VSPEC = pl.BlockSpec(memory_space=pltpu.VMEM)
ASPEC = pl.BlockSpec(memory_space=pl.ANY)


def params(cid):
    return pltpu.CompilerParams(
        collective_id=cid, has_side_effects=True, vmem_limit_bytes=VMEM_LIMIT
    )


class RowChain:
    def __init__(self, place, sends, zn, src, buf, chunk, ss_r, ss_l, rs):
        self.place, self.sends, self.zn = place, sends, zn
        self.src, self.buf, self.chunk = src, buf, chunk
        self.ss_r, self.ss_l, self.rs = ss_r, ss_l, rs

    def _on(self, src, c, origin, right, left):
        pc = self.place
        dst = self.buf.at[origin, :, pl.ds(c * self.chunk, self.chunk)]
        if right is not None:
            self.sends.start(
                src,
                dst,
                self.ss_r.at[c, origin],
                self.rs.at[c, origin],
                pc.at(jnp.minimum(pc.z + 1, self.zn - 1), pc.p),
                right,
            )
        if left is not None:
            self.sends.start(
                src,
                dst,
                self.ss_l.at[c, origin],
                self.rs.at[c, origin],
                pc.at(jnp.maximum(pc.z - 1, 0), pc.p),
                left,
            )

    def own(self, c):
        pc = self.place
        src = self.src.at[:, pl.ds(c * self.chunk, self.chunk)]
        self._on(src, c, pc.z, pc.z < self.zn - 1, pc.z > 0)

    def keep(self):
        self.buf[self.place.z] = self.src[...]

    def step(self, c, k):
        pc = self.place
        cols = pl.ds(c * self.chunk, self.chunk)
        below = jnp.maximum(pc.z - k, 0)
        has = pc.z - k >= 0
        ref = self.buf.at[below, :, cols]
        arrived(ref, self.rs.at[c, below], has)
        self._on(ref, c, below, jnp.logical_and(has, pc.z < self.zn - 1), None)
        above = jnp.minimum(pc.z + k, self.zn - 1)
        has = pc.z + k < self.zn
        ref = self.buf.at[above, :, cols]
        arrived(ref, self.rs.at[c, above], has)
        self._on(ref, c, above, None, jnp.logical_and(has, pc.z > 0))


def turned(values):
    return pltpu.roll(values, HD // 2, 1)


def nt_dot(a, b):
    return lax.dot_general(a, b, (((1,), (1,)), ((), ())), preferred_element_type=f32)


def tn_dot(a, b):
    return lax.dot_general(a, b, (((0,), (0,)), ((), ())), preferred_element_type=f32)


def nn_dot(a, b):
    return jnp.dot(a, b, preferred_element_type=f32)


QBLOCK = 256


def key_limit(i, length):
    return min(length, (i + 1) * QBLOCK + IMG_LEN)


def send_slots(place, sends, zn, src, dst, ss, rs):
    for k in range(1, zn):
        d = (place.z + k) % zn
        sends.start(src.at[d], dst.at[place.z], ss.at[k], rs.at[place.z], place.at(d, place.p))


def take_slots(place, zn, src, dst, rs):
    dst[place.z] = src[place.z]
    for k in range(1, zn):
        d = (place.z + k) % zn
        arrived(dst.at[d], rs.at[d])


def make_hot(zn, cap, tok, slots_ref, hot):
    row = lax.broadcasted_iota(jnp.int32, (zn * cap, tok), 0).astype(f32)

    def body(p, carry):
        for z in range(zn):
            have = slots_ref[z, pl.ds(p, 1), :]
            want = jnp.where(have < 0, -1.0, have + float(z * cap))
            hot[p, :, pl.ds(z * tok, tok)] = jnp.where(row == want, 1.0, 0.0).astype(bf16)
        return carry

    lax.fori_loop(0, PLANE, body, 0)


class PlaneSend:
    def __init__(self, place, sends, hot, rows, buf, out, chunk, ss, rs):
        self.place, self.sends = place, sends
        self.hot, self.rows, self.buf, self.out, self.chunk = hot, rows, buf, out, chunk
        self.ss, self.rs = ss, rs

    def send(self, c):
        pc = self.place
        cols = pl.ds(c * self.chunk, self.chunk)
        zn, tok, _ = self.rows.shape
        for k in (1, 2, 3, 4, 5, 6, 7, 0):
            p = pc.by(k) if k else pc.p
            got = nn_dot(self.hot[p], self.rows[:, :, cols].reshape(zn * tok, self.chunk))
            if k:
                self.buf[p, :, cols] = got.astype(bf16)
                self.sends.start(
                    self.buf.at[p, :, cols],
                    self.out.at[pc.p, :, cols],
                    self.ss.at[c, k],
                    self.rs.at[c, k],
                    pc.at(pc.z, p),
                )
            else:
                self.out[pc.p, :, cols] = got.astype(bf16)

    def take(self, c):
        cols = pl.ds(c * self.chunk, self.chunk)
        for k in range(1, PLANE):
            arrived(self.out.at[self.place.by(k), :, cols], self.rs.at[c, k])


def front_kernel(
    zn, cap, chunk, heads,
    tok_ref, gain_ref, pq_ref, po_ref, tab_ref, hg_ref, bias_ref, grad_ref, slot_ref,
    seq_ref, wq_ref, wo_ref, pre_ref, rot_ref, val_ref, lse_ref, ctx_ref, att_ref, ag_ref, so_ref,
    part, c1, s1, ra, rb, last, gb, sn, hot,
    gs, gr, ps, pr, sr, sl, rs, hs, hr, zsr, zsl, zr, ts, tr, xs, xr,
):
    place, sends = Place(), Sends()
    pc = place
    tok, width = tok_ref.shape
    length = PLANE * tok
    own_rows = pq_ref.shape[1]
    half = heads * HD
    chunks = width // chunk
    scale = HD ** (-0.5)
    greet(place, zn)
    q = ColumnGather(
        place, sends, zn, pq_ref, wq_ref, ps.at[0], pr.at[0], sr.at[0], sl.at[0], rs.at[0]
    )
    o = ColumnGather(
        place, sends, zn, po_ref, wo_ref, ps.at[1], pr.at[1], sr.at[1], sl.at[1], rs.at[1]
    )
    g = RowChain(place, sends, zn, grad_ref, gb, chunk, zsr, zsl, zr)
    q.pair()
    q.own()

    def first_norm(i, carry):
        at = pl.ds(pl.multiple_of(i * 32, 32), 32)
        v = tok_ref[at, :].astype(f32)
        seq_ref[pc.p, at, :] = (v * rms_scale(v) * gain_ref[...]).astype(bf16)
        return carry

    lax.fori_loop(0, tok // 32, first_norm, 0)
    rows = PlaneGather(place, sends, seq_ref, gs, gr)
    rows.first()
    send_slots(place, sends, zn, slot_ref, so_ref, ts, tr)
    q.keep()
    q.partner()
    rows.second()
    o.pair()
    o.keep()
    g.keep()
    rows.third()
    take_slots(place, zn, slot_ref, so_ref, tr)
    make_hot(zn, cap, tok, so_ref, hot)
    pre_ref[...] = jnp.zeros_like(pre_ref)

    def project(origin):
        cols = pl.ds(pl.multiple_of(origin * 2 * own_rows, 2 * own_rows), 2 * own_rows)
        weight = wq_ref.at[pl.ds(2 * origin, 2)]

        def body(i, carry):
            at = pl.ds(pl.multiple_of(i * 2 * tok, 2 * tok), 2 * tok)
            lhs = seq_ref[pl.ds(2 * i, 2), :, cols].reshape(2 * tok, 2 * own_rows)
            pre_ref[at, :] += nn_dot(lhs, weight[...].reshape(2 * own_rows, half + 2 * HD))
            return carry

        lax.fori_loop(0, PLANE // 2, body, 0)

    def project_step(k):
        pl.when(pc.z - k >= 0)(lambda: project(jnp.maximum(pc.z - k, 0)))
        pl.when(pc.z + k < zn)(lambda: project(jnp.minimum(pc.z + k, zn - 1)))

    for k in range(1, zn):
        q.step(k)
        if k == 1:
            rows.last()
            project(pc.z)
        if k == zn - 1:
            for c in range(chunks):
                g.own(c)
            o.own()
            o.partner()
        project_step(k)

    def turn(i, carry):
        at = pl.ds(pl.multiple_of(i * 128, 128), 128)
        cos, sin = tab_ref[0, at, :], tab_ref[1, at, :]
        for h in range(heads + 1):
            v = pre_ref[at, h * HD : (h + 1) * HD]
            gain = hg_ref[pl.ds(0 if h < heads else 1, 1), :]
            v = v * rms_scale(v) * gain
            rot_ref[h, at, :] = (v * cos + turned(v) * sin).astype(bf16)
        val_ref[at, :] = pre_ref[at, half + HD : half + 2 * HD].astype(bf16)
        return carry

    lax.fori_loop(0, length // 128, turn, 0)
    lane = lax.broadcasted_iota(jnp.int32, (QBLOCK, 128), 1)

    def attend(i):
        limit = key_limit(i, length)
        at = slice(i * QBLOCK, (i + 1) * QBLOCK)

        def body(h, carry):
            scores = nt_dot(rot_ref[h, at, :], rot_ref[heads, :limit, :]) * scale
            scores = scores + bias_ref[at, :limit].astype(f32)
            top = jnp.max(scores, axis=1, keepdims=True)
            expo = jnp.exp(scores - top)
            total = jnp.sum(expo, axis=1, keepdims=True)
            low = (expo * (1.0 / total)).astype(bf16)
            cols = pl.ds(pl.multiple_of(h * HD, HD), HD)
            ctx_ref[at, cols] = nn_dot(low, val_ref[:limit, :]).astype(bf16)
            lse_ref[at, :] = jnp.where(lane == h, top + jnp.log(total), lse_ref[at, :])
            return carry

        lax.fori_loop(0, heads, body, 0)

    lse_ref[...] = jnp.zeros_like(lse_ref)
    hops = [(c, k) for k in range(1, zn) for c in range(chunks)]
    blocks = length // QBLOCK
    ahead = min(len(hops), 2 * (blocks - 1))
    done = 0
    for i in range(blocks):
        attend(i)
        while i < blocks - 1 and done < ahead and done < 2 * (i + 1):
            g.step(*hops[done])
            done += 1

    def output(origin):
        cols = pl.ds(pl.multiple_of(origin * 2 * own_rows, 2 * own_rows), 2 * own_rows)
        weight = wo_ref.at[pl.ds(2 * origin, 2)]

        def body(i, carry):
            at = pl.ds(pl.multiple_of(i * 2 * tok, 2 * tok), 2 * tok)
            got = nt_dot(ctx_ref[at, :], weight[...].reshape(2 * own_rows, half))
            part[pl.ds(2 * i, 2), :, cols] = got.astype(bf16).reshape(2, tok, 2 * own_rows)
            return carry

        lax.fori_loop(0, PLANE // 2, body, 0)

    def output_step(k):
        pl.when(pc.z - k >= 0)(lambda: output(jnp.maximum(pc.z - k, 0)))
        pl.when(pc.z + k < zn)(lambda: output(jnp.minimum(pc.z + k, zn - 1)))

    output(pc.z)
    give = PlaneSend(place, sends, hot, gb, sn, ag_ref, chunk, xs, xr)
    for c, k in hops[done:]:
        g.step(c, k)
        if k == zn - 1:
            give.send(c)
    for k in range(1, zn):
        o.step(k)
        output_step(k)
    red = PlaneReduce(place, sends, part, att_ref, (c1, s1, ra, rb, last), hs, hr)
    for k in range(4):
        red.first(k)
    for k in range(4):
        red.second(k)
    red.third()
    red.finish()
    for c in range(chunks):
        give.take(c)
    sends.finish()


def front(zn, cap, heads, tokens, gain, pack_q, pack_o, tables, gains, bias, grad, slot, chunk=512):
    tok, width = tokens.shape
    length = PLANE * tok
    e = 2 * zn
    slots = zn * cap
    chunks = width // chunk
    half = heads * HD
    shape = jax.ShapeDtypeStruct
    return pl.pallas_call(
        functools.partial(front_kernel, zn, cap, chunk, heads),
        out_shape=(
            shape((PLANE, tok, width), bf16),
            shape((e,) + pack_q.shape[1:], bf16),
            shape((e,) + pack_o.shape[1:], bf16),
            shape((length, half + 2 * HD), f32),
            shape((heads + 1, length, HD), bf16),
            shape((length, HD), bf16),
            shape((length, 128), f32),
            shape((length, half), bf16),
            shape((tok, width), f32),
            shape((PLANE, slots, width), bf16),
            shape(slot.shape, f32),
        ),
        in_specs=[VSPEC] * 9,
        out_specs=(VSPEC,) * 11,
        scratch_shapes=[pltpu.VMEM((PLANE, tok, width), bf16)]
        + PlaneReduce.scratch(tok, width)
        + [
            pltpu.VMEM((zn, tok, width), bf16),
            pltpu.VMEM((PLANE, slots, width), bf16),
            pltpu.VMEM((PLANE, slots, zn * tok), bf16),
            dma_sems(8),
            dma_sems(8),
            dma_sems(2),
            dma_sems(2),
            dma_sems(2, e),
            dma_sems(2, e),
            dma_sems(2, e),
            dma_sems(10),
            dma_sems(10),
            dma_sems(chunks, zn),
            dma_sems(chunks, zn),
            dma_sems(chunks, zn),
            dma_sems(zn),
            dma_sems(zn),
            dma_sems(chunks, PLANE),
            dma_sems(chunks, PLANE),
        ],
        compiler_params=params(0),
        name="front",
    )(tokens, gain, pack_q, pack_o, tables, gains, bias, grad, slot)


def send_kernel(
    zn, cap, chunk, norm_ref, slots_ref, mix_ref, an_ref, mr_ref, mo_ref,
    nb, sn, hot, mrow, zsr, zsl, zr, ts, tr, xs, xr, ys, yr,
):
    place, sends = Place(), Sends()
    pc = place
    greet(place, zn)
    tok, width = norm_ref.shape
    slots = zn * cap
    chunks = width // chunk
    n = RowChain(place, sends, zn, norm_ref, nb, chunk, zsr, zsl, zr)
    send_slots(place, sends, zn, mix_ref, mo_ref, ts, tr)
    for c in range(chunks):
        n.own(c)
    n.keep()
    make_hot(zn, cap, tok, slots_ref, hot)
    take_slots(place, zn, mix_ref, mo_ref, tr)

    def mixes(p, carry):
        row = jnp.concatenate([mo_ref[z, pl.ds(p, 1), :] for z in range(zn)], axis=1)
        high = row.astype(bf16)
        rest = row - high.astype(f32)
        middle = rest.astype(bf16)
        low = (rest - middle.astype(f32)).astype(bf16)
        zero = jnp.zeros((13, zn * tok), bf16)
        got = nt_dot(jnp.concatenate([high, middle, low, zero], axis=0), hot[p])
        mrow[p] = jnp.sum(got, axis=0, keepdims=True)
        return carry

    lax.fori_loop(0, PLANE, mixes, 0)
    for k in range(1, PLANE):
        p = pc.by(k)
        sends.start(mrow.at[p], mr_ref.at[pc.p], ys.at[k], yr.at[k], pc.at(pc.z, p))
    mr_ref[pc.p] = mrow[pc.p]
    give = PlaneSend(place, sends, hot, nb, sn, an_ref, chunk, xs, xr)
    for c in range(chunks):
        for k in range(1, zn):
            n.step(c, k)
        give.send(c)
    for k in range(1, PLANE):
        arrived(mr_ref.at[pc.by(k)], yr.at[k])
    for c in range(chunks):
        give.take(c)
    sends.finish()


def send_rows(zn, cap, norm, slots_all, mix, chunk=512):
    tok, width = norm.shape
    slots = zn * cap
    chunks = width // chunk
    return pl.pallas_call(
        functools.partial(send_kernel, zn, cap, chunk),
        out_shape=(
            jax.ShapeDtypeStruct((PLANE, slots, width), bf16),
            jax.ShapeDtypeStruct((PLANE, 1, slots), f32),
            jax.ShapeDtypeStruct(mix.shape, f32),
        ),
        in_specs=[VSPEC] * 3,
        out_specs=(VSPEC,) * 3,
        scratch_shapes=[
            pltpu.VMEM((zn, tok, width), bf16),
            pltpu.VMEM((PLANE, slots, width), bf16),
            pltpu.VMEM((PLANE, slots, zn * tok), bf16),
            pltpu.VMEM((PLANE, 1, slots), f32),
            dma_sems(chunks, zn),
            dma_sems(chunks, zn),
            dma_sems(chunks, zn),
            dma_sems(zn),
            dma_sems(zn),
            dma_sems(chunks, PLANE),
            dma_sems(chunks, PLANE),
            dma_sems(PLANE),
            dma_sems(PLANE),
        ],
        compiler_params=params(3),
        name="send_rows",
    )(norm, slots_all, mix)


def back_kernel(
    zn, chunk, pair_ref, dot_ref, hot_ref, sum_ref, dots_ref,
    rp, rd, zd, zp, ap, xs, xr, ds, dr, zs, zr, es, er,
):
    place, sends = Place(), Sends()
    pc = place
    greet(place, zn)
    _, slots, width = pair_ref.shape
    chunks = width // chunk
    tok = sum_ref.shape[0]
    far = [(pc.z + k) % zn for k in range(1, zn)]
    for k in range(1, PLANE):
        p = pc.by(k)
        sends.start(dot_ref.at[p], rd.at[pc.p], ds.at[k], dr.at[k], pc.at(pc.z, p))
    for c in range(chunks):
        cols = pl.ds(c * chunk, chunk)
        for k in range(1, PLANE):
            p = pc.by(k)
            sends.start(
                pair_ref.at[p, :, cols],
                rp.at[pc.p, :, cols],
                xs.at[c, k],
                xr.at[c, k],
                pc.at(pc.z, p),
            )
    rd[pc.p] = dot_ref[pc.p]
    rp[pc.p] = pair_ref[pc.p]
    for k in range(1, PLANE):
        arrived(rd.at[pc.by(k)], dr.at[k])
    zd[...] = nn_dot(hot_ref[...], rd[...].reshape(PLANE * slots, 128)).reshape(zn, tok, 128)
    for k, d in enumerate(far):
        sends.start(zd.at[d], dots_ref.at[pc.z], es.at[k], er.at[pc.z], pc.at(d, pc.p))
    dots_ref[pc.z] = zd[pc.z]
    for c in range(chunks):
        cols = pl.ds(c * chunk, chunk)
        for k in range(1, PLANE):
            arrived(rp.at[pc.by(k), :, cols], xr.at[c, k])
        got = nn_dot(hot_ref[...], rp[:, :, cols].reshape(PLANE * slots, chunk))
        zp[:, :, cols] = got.astype(bf16).reshape(zn, tok, chunk)
        for k, d in enumerate(far):
            sends.start(
                zp.at[d, :, cols],
                ap.at[pc.z, :, cols],
                zs.at[c, k],
                zr.at[c, pc.z],
                pc.at(d, pc.p),
            )
    for c in range(chunks):
        cols = pl.ds(c * chunk, chunk)
        total = zp[pc.z, :, cols].astype(f32)
        for d in far:
            arrived(ap.at[d, :, cols], zr.at[c, d])
            total = total + ap[d, :, cols].astype(f32)
        sum_ref[:, cols] = total
    for d in far:
        arrived(dots_ref.at[d], er.at[d])
    sends.finish()


def back_rows(zn, tok, pair, dots, hot, chunk=512):
    _, slots, width = pair.shape
    chunks = width // chunk
    return pl.pallas_call(
        functools.partial(back_kernel, zn, chunk),
        out_shape=(
            jax.ShapeDtypeStruct((tok, width), f32),
            jax.ShapeDtypeStruct((zn, tok, 128), f32),
        ),
        in_specs=[VSPEC] * 3,
        out_specs=(VSPEC,) * 2,
        scratch_shapes=[
            pltpu.VMEM((PLANE, slots, width), bf16),
            pltpu.VMEM((PLANE, slots, 128), bf16),
            pltpu.VMEM((zn, tok, 128), f32),
            pltpu.VMEM((zn, tok, width), bf16),
            pltpu.VMEM((zn, tok, width), bf16),
            dma_sems(chunks, PLANE),
            dma_sems(chunks, PLANE),
            dma_sems(PLANE),
            dma_sems(PLANE),
            dma_sems(chunks, zn),
            dma_sems(chunks, zn),
            dma_sems(zn),
            dma_sems(zn),
        ],
        compiler_params=params(4),
        name="back_rows",
    )(pair, dots, hot)


class ColumnReduce:
    def __init__(self, place, sends, zn, part, buf, ss_r, ss_l, rs_r, rs_l):
        self.place, self.sends, self.zn = place, sends, zn
        self.part, self.buf = part, buf
        self.ss_r, self.ss_l, self.rs_r, self.rs_l = ss_r, ss_l, rs_r, rs_l

    def _hop(self, slot, rs, ss, d, start, inner, device):
        rows = self.part.shape[1]

        def add():
            arrived(self.buf.at[slot], rs.at[d])

            def put(at, v):
                self.buf[slot, at, :] = v.astype(bf16)

            add_rows(put, lambda at: self.part[d, at, :], lambda at: self.buf[slot, at, :], rows)

        both = jnp.logical_and(start, inner)
        pl.when(both)(add)
        self.sends.start(
            self.buf.at[slot], self.buf.at[slot], ss.at[d], rs.at[d], device, both
        )
        self.sends.start(
            self.part.at[d],
            self.buf.at[slot],
            ss.at[d],
            rs.at[d],
            device,
            jnp.logical_and(start, jnp.logical_not(inner)),
        )

    def step(self, k):
        pc, zn = self.place, self.zn
        d = zn - 1 - k
        right = pc.at(jnp.minimum(pc.z + 1, zn - 1), pc.p)
        left = pc.at(jnp.maximum(pc.z - 1, 0), pc.p)
        self._hop(d + 1, self.rs_r, self.ss_r, d, pc.z < d, pc.z > 0, right)
        d = k
        self._hop(d, self.rs_l, self.ss_l, d, pc.z > d, pc.z < zn - 1, left)

    def own(self, use, step=32):
        pc, zn = self.place, self.zn
        lower, upper = pc.z > 0, pc.z < zn - 1
        arrived(self.buf.at[pc.z + 1], self.rs_r.at[pc.z], lower)
        arrived(self.buf.at[pc.z], self.rs_l.at[pc.z], upper)

        def body(i, carry):
            at = pl.ds(pl.multiple_of(i * step, step), step)
            v = self.part[pc.z, at, :].astype(f32)
            v = v + jnp.where(lower, self.buf[pc.z + 1, at, :].astype(f32), 0.0)
            v = v + jnp.where(upper, self.buf[pc.z, at, :].astype(f32), 0.0)
            use(at, v)
            return carry

        lax.fori_loop(0, self.part.shape[1] // step, body, 0)


class SmallSum:
    @staticmethod
    def scratch(zn, rows, lanes):
        return [
            pltpu.VMEM((PLANE, rows, lanes), f32),
            pltpu.VMEM((rows, lanes), f32),
            pltpu.VMEM((zn, rows, lanes), f32),
            dma_sems(PLANE),
            dma_sems(PLANE),
            dma_sems(zn),
            dma_sems(zn),
            dma_sems(PLANE),
            dma_sems(PLANE),
        ]

    def __init__(self, place, sends, zn, flat, out, scratch):
        self.place, self.sends, self.zn, self.flat, self.out = place, sends, zn, flat, out
        self.l1, self.mid, self.l2, self.a, self.ar, self.b, self.br, self.c, self.cr = scratch

    def first(self):
        pc = self.place
        for k in range(1, PLANE):
            p = pc.by(k)
            self.sends.start(
                self.flat.at[p], self.l1.at[pc.p], self.a.at[k], self.ar.at[k], pc.at(pc.z, p)
            )
        self.l1[pc.p] = self.flat[pc.p]

    def second(self):
        pc, zn = self.place, self.zn
        for k in range(1, PLANE):
            arrived(self.l1.at[pc.by(k)], self.ar.at[k])
        total = self.l1[0]
        for k in range(1, PLANE):
            total = total + self.l1[k]
        self.mid[...] = total
        self.l2[pc.z] = total
        for k in range(1, zn):
            d = (pc.z + k) % zn
            self.sends.start(
                self.mid, self.l2.at[pc.z], self.b.at[k], self.br.at[pc.z], pc.at(d, pc.p)
            )

    def _column(self):
        pc, zn = self.place, self.zn
        for k in range(1, zn):
            d = (pc.z + k) % zn
            arrived(self.l2.at[d], self.br.at[d])
        total = self.l2[0]
        for z in range(1, zn):
            total = total + self.l2[z]
        return total

    def third(self):
        pc = self.place
        self.out[pc.p] = self._column()
        for k in range(1, PLANE):
            p = pc.by(k)
            self.sends.start(
                self.out.at[pc.p], self.out.at[pc.p], self.c.at[k], self.cr.at[k], pc.at(pc.z, p)
            )

    def last(self):
        pc = self.place
        for k in range(1, PLANE):
            arrived(self.out.at[pc.by(k)], self.cr.at[k])


class TinySum:
    @staticmethod
    def scratch(zn, lanes):
        return [
            pltpu.VMEM((1, lanes), f32),
            pltpu.VMEM((PLANE, 1, lanes), f32),
            pltpu.VMEM((1, lanes), f32),
            pltpu.VMEM((zn, 1, lanes), f32),
            dma_sems(PLANE),
            dma_sems(PLANE),
            dma_sems(zn),
            dma_sems(zn),
        ]

    def __init__(self, place, sends, zn, out, scratch):
        self.place, self.sends, self.zn, self.out = place, sends, zn, out
        self.vec, self.l1, self.mid, self.l2, self.a, self.ar, self.b, self.br = scratch

    def first(self):
        pc = self.place
        for k in range(1, PLANE):
            p = pc.by(k)
            self.sends.start(
                self.vec, self.l1.at[pc.p], self.a.at[k], self.ar.at[k], pc.at(pc.z, p)
            )
        self.l1[pc.p] = self.vec[...]

    def second(self):
        pc, zn = self.place, self.zn
        for k in range(1, PLANE):
            arrived(self.l1.at[pc.by(k)], self.ar.at[k])
        total = self.l1[0]
        for k in range(1, PLANE):
            total = total + self.l1[k]
        self.mid[...] = total
        self.l2[pc.z] = total
        for k in range(1, zn):
            d = (pc.z + k) % zn
            self.sends.start(
                self.mid, self.l2.at[pc.z], self.b.at[k], self.br.at[pc.z], pc.at(d, pc.p)
            )

    def last(self):
        pc, zn = self.place, self.zn
        for k in range(1, zn):
            d = (pc.z + k) % zn
            arrived(self.l2.at[d], self.br.at[d])
        total = self.l2[0]
        for z in range(1, zn):
            total = total + self.l2[z]
        self.out[...] = total


class Result:
    def __init__(self, place, zn, res, comb, rr, am, rbuf, zbuf, chunk, xs, xr, zs, zr, ls, os):
        self.place, self.zn, self.res, self.comb = place, zn, res, comb
        self.rr, self.am, self.rbuf, self.zbuf, self.chunk = rr, am, rbuf, zbuf, chunk
        self.xs, self.xr, self.zs, self.zr, self.ls, self.os = xs, xr, zs, zr, ls, os
        self.flight = {}

    def first(self, sends, chunks):
        pc = self.place
        for c in range(chunks):
            cols = pl.ds(c * self.chunk, self.chunk)
            for k in range(1, PLANE):
                p = pc.by(k)
                sends.start(
                    self.res.at[p, :, cols],
                    self.rr.at[pc.p, :, cols],
                    self.xs.at[c, k],
                    self.xr.at[c, k],
                    pc.at(pc.z, p),
                )

    def mix(self, c):
        pc, zn = self.place, self.zn
        cols = pl.ds(c * self.chunk, self.chunk)
        own = pltpu.make_async_copy(self.res.at[pc.p, :, cols], self.rbuf.at[pc.p], self.ls.at[0])
        own.start()
        copies = []
        for k in range(1, PLANE):
            p = pc.by(k)
            arrived(self.rr.at[p, :, cols], self.xr.at[c, k])
            copy = pltpu.make_async_copy(self.rr.at[p, :, cols], self.rbuf.at[p], self.ls.at[k])
            copy.start()
            copies.append(copy)
        own.wait()
        for copy in copies:
            copy.wait()
        self.settle(c - 2)
        slot = c % 2
        _, slots, chunk = self.rbuf.shape
        tok = self.zbuf.shape[2]
        unit = min(512, zn * tok)
        per = unit // tok
        rows = self.rbuf[...].reshape(PLANE * slots, chunk)
        for i in range(zn * tok // unit):
            got = nn_dot(self.comb[i * unit : (i + 1) * unit, :], rows)
            self.zbuf[slot, i * per : (i + 1) * per] = got.astype(bf16).reshape(per, tok, chunk)
        flight = []
        for k in range(1, zn):
            d = (pc.z + k) % zn
            flight.append(
                pltpu.make_async_remote_copy(
                    src_ref=self.zbuf.at[slot, d],
                    dst_ref=self.am.at[pc.z, :, cols],
                    send_sem=self.zs.at[c, k],
                    recv_sem=self.zr.at[c, pc.z],
                    device_id=pc.at(d, pc.p),
                    device_id_type=MESH,
                )
            )
        for copy in flight:
            copy.start()
        keep = pltpu.make_async_copy(
            self.zbuf.at[slot, pc.z], self.am.at[pc.z, :, cols], self.os.at[c]
        )
        keep.start()
        self.flight[c] = (flight, keep)

    def settle(self, c):
        if c in self.flight:
            flight, keep = self.flight.pop(c)
            for copy in flight:
                copy.wait_send()
            keep.wait()

    def last(self, chunks):
        pc, zn = self.place, self.zn
        for c in range(chunks):
            self.settle(c)
            for k in range(1, zn):
                d = (pc.z + k) % zn
                arrived(self.am.at[d, :, pl.ds(c * self.chunk, self.chunk)], self.zr.at[c, d])


def rear_kernel(
    zn, chunk, heads,
    mid_ref, tok_ref, gain_ref, hg_ref, flat_ref, comb_ref,
    res_hbm, seq_hbm, wq_hbm, wo_hbm, pre_hbm, rot_hbm, val_hbm, lse_hbm, ctx_hbm, tab_hbm, bias_hbm,
    grad_ref, oq_ref, oo_ref, sum_ref, tiny_ref, am_hbm, rr_hbm,
    big, wq, wo, pre, rot, val, lse, ctx, tab, bias,
    lse_t, del_t, key_t, cback, aback, dk, dv, dgain,
    gq, bq, vq, tq, go, bo, vo, to,
    c1, s1, ra, rb, last, rbuf, zbuf,
    gs, gr, hs, hr, sr, sl, rr, rl, ps, pr, xs, xr, zs, zr, ls, os, loads,
    *rest,
):
    place, sends = Place(), Sends()
    pc = place
    small_scratch, tiny_scratch = rest[:9], rest[9:]
    tok, width = mid_ref.shape
    length = PLANE * tok
    half = heads * HD
    own_rows = wq.shape[1]
    chunks = width // chunk
    scale = HD ** (-0.5)
    greet(place, zn)
    pairs = (
        (wo_hbm, wo), (ctx_hbm, ctx), (rot_hbm, rot), (val_hbm, val), (lse_hbm, lse),
        (bias_hbm, bias), (pre_hbm, pre), (tab_hbm, tab), (wq_hbm, wq),
    )
    fetch = [pltpu.make_async_copy(a, b, loads.at[i]) for i, (a, b) in enumerate(pairs)]
    small = SmallSum(place, sends, zn, flat_ref, sum_ref, small_scratch)
    tiny = TinySum(place, sends, zn, tiny_ref, tiny_scratch)
    row_sends = Sends()
    rows = PlaneGather(place, row_sends, big, gs, gr)
    result = Result(
        place, zn, res_hbm, comb_ref, rr_hbm, am_hbm, rbuf, zbuf, chunk, xs, xr, zs, zr, ls, os
    )
    o = ColumnReduce(place, sends, zn, go, bo, sr.at[1], sl.at[1], rr.at[1], rl.at[1])
    q = ColumnReduce(place, sends, zn, gq, bq, sr.at[0], sl.at[0], rr.at[0], rl.at[0])

    def stage(i, carry):
        at = pl.ds(pl.multiple_of(i * 32, 32), 32)
        big[pc.p, at, :] = mid_ref[at, :].astype(bf16)
        return carry

    lax.fori_loop(0, tok // 32, stage, 0)
    rows.first()
    for copy in fetch:
        copy.start()
    small.first()
    rows.second()
    rows.third()
    for copy in fetch[:6]:
        copy.wait()
    key_t[...] = rot[heads].astype(f32).T.astype(bf16)
    lse_t[...] = lse[...].T
    small.second()
    rows.last()
    result.first(sends, chunks)

    order = []
    for k in range(zn):
        for d in (zn - 1 - k, k):
            if d not in order:
                order.append(d)

    def output_grad(d):
        cols = pl.ds(d * 2 * own_rows, 2 * own_rows)
        rhs = big[:, :, cols].reshape(length, 2 * own_rows)

        def body(i, carry):
            m = pl.ds(pl.multiple_of(i * 256, 256), 256)
            go[d, m, :] = tn_dot(ctx[:, m], rhs).astype(bf16)
            return carry

        lax.fori_loop(0, half // 256, body, 0)

    made = 0
    for k in range(1):
        while made < len(order) and not {zn - 1 - k, k} <= set(order[:made]):
            output_grad(order[made])
            made += 1
        o.step(k)

    def context_back(i, carry):
        at = pl.ds(pl.multiple_of(i * 2 * tok, 2 * tok), 2 * tok)
        lhs = big[pl.ds(2 * i, 2)].reshape(2 * tok, width)
        got = nn_dot(lhs, wo[...].reshape(width, half))
        cback[at, :] = got.astype(bf16)
        prod = got.astype(bf16).astype(f32) * ctx[at, :].astype(f32)
        for h in range(heads):
            s = jnp.sum(prod[:, h * HD : (h + 1) * HD], axis=1, keepdims=True)
            lse[at, h : h + 1] = s
        return carry

    lax.fori_loop(0, PLANE // 2, context_back, 0)
    while made < len(order):
        output_grad(order[made])
        made += 1
    del_t[...] = lse[...].T
    row_sends.finish()
    fill = pltpu.make_async_copy(seq_hbm, big, loads.at[len(pairs)])
    fill.start()
    small.third()
    dk[...] = jnp.zeros_like(dk)
    dv[...] = jnp.zeros_like(dv)
    dgain[...] = jnp.zeros_like(dgain)
    for copy in fetch[6:]:
        copy.wait()

    def norm_of(d, at, h, gain_row):
        d = d * tab[0, at, :] - turned(d) * tab[1, at, :]
        v = pre[at, pl.ds(h * HD if isinstance(h, int) else pl.multiple_of(h * HD, HD), HD)]
        r = rms_scale(v)
        hat = v * r
        s = d * hg_ref[pl.ds(gain_row, 1), :]
        got = r * (s - hat * jnp.mean(s * hat, axis=1, keepdims=True))
        dgain[pl.ds(gain_row, 1), :] += jnp.sum(d * hat, axis=0, keepdims=True)
        return got.astype(bf16)

    def attend(i):
        limit = key_limit(i, length)
        at = slice(i * QBLOCK, (i + 1) * QBLOCK)

        def body(h, carry):
            cols = pl.ds(pl.multiple_of(h * HD, HD), HD)
            query = rot[h, at, :]
            dctx = cback[at, cols]
            scores = nt_dot(rot[heads, :limit, :], query) * scale
            scores = scores + bias[:limit, at].astype(f32)
            probs = jnp.exp(scores - lse_t[pl.ds(h, 1), at])
            dprobs = nt_dot(val[:limit, :], dctx)
            dscores = (probs * (dprobs - del_t[pl.ds(h, 1), at])).astype(bf16)
            dv[:limit, :] += nn_dot(probs.astype(bf16), dctx)
            dk[:limit, :] += nn_dot(dscores, query)
            dq = nn_dot(key_t[:, :limit], dscores).T * scale
            aback[at, cols] = norm_of(dq, at, h, 0)
            return carry

        lax.fori_loop(0, heads, body, 0)

    blocks = length // QBLOCK
    hop = 1
    for i in range(blocks):
        attend(i)
        if i % 2 == 1 and hop < zn - 1:
            o.step(hop)
            hop += 1
        if i == 2:
            result.mix(0)
    while hop < zn - 1:
        o.step(hop)
        hop += 1

    def keys(i, carry):
        at = pl.ds(pl.multiple_of(i * 256, 256), 256)
        aback[at, half : half + HD] = norm_of(dk[at, :] * scale, at, heads, 1)
        aback[at, half + HD : half + 2 * HD] = dv[at, :].astype(bf16)
        return carry

    lax.fori_loop(0, length // 256, keys, 0)
    fill.wait()

    def query_grad(d):
        for h in range(2):
            cols = pl.ds((2 * d + h) * own_rows, own_rows) if own_rows % 128 == 0 else None
            if cols is None:
                lhs = big[:, :, pl.ds(2 * d * own_rows, 2 * own_rows)]
                lhs = lhs.reshape(length, 2 * own_rows)
                if h == 0:
                    gq[d] = tn_dot(lhs, aback[...]).astype(bf16)
            else:
                lhs = big[:, :, cols].reshape(length, own_rows)
                gq[d, h * own_rows : (h + 1) * own_rows, :] = tn_dot(lhs, aback[...]).astype(bf16)

    made = 0
    for k in range(zn - 1):
        while made < len(order) and not {zn - 1 - k, k} <= set(order[:made]):
            query_grad(order[made])
            made += 1
        if k == 0:
            q.step(0)
    while made < len(order):
        query_grad(order[made])
        made += 1

    red = PlaneReduce(place, sends, big, grad_ref, (c1, s1, ra, rb, last), hs, hr)

    def norm1_part(k):
        y, x, j = red._chip(*red.chips[k])
        lhs = aback[pl.ds(pl.multiple_of(j * 2 * tok, 2 * tok), 2 * tok), :]

        def body(i, carry):
            cols = pl.ds(pl.multiple_of(i * chunk, chunk), chunk)
            e = i * (chunk // own_rows)
            rhs = wq[pl.ds(e, chunk // own_rows)].reshape(chunk, half + 2 * HD)
            big[pl.ds(j * 2, 2), :, cols] = nt_dot(lhs, rhs).astype(bf16).reshape(2, tok, chunk)
            return carry

        lax.fori_loop(0, width // chunk, body, 0)

    for k in range(4):
        norm1_part(k)
        red.first(k)
    if zn > 2:
        q.step(1)
    for k in range(4):
        red.second(k)
    red.third()
    result.mix(1)
    for k in range(2, zn - 1):
        q.step(k)
    result.mix(2)
    red.finish()

    def tokens_back(i, carry):
        at = pl.ds(pl.multiple_of(i * 16, 16), 16)
        v = tok_ref[at, :].astype(f32)
        r = rms_scale(v)
        hat = v * r
        d = grad_ref[at, :]
        s = d * gain_ref[...]
        got = r * (s - hat * jnp.mean(s * hat, axis=1, keepdims=True))
        grad_ref[at, :] = mid_ref[at, :] + got
        return carry + jnp.sum(d * hat, axis=0, keepdims=True)

    total = lax.fori_loop(0, tok // 16, tokens_back, jnp.zeros((1, width), f32))
    tiny.vec[:, :width] = total
    tiny.vec[:, width : width + HD] = dgain[0:1, :]
    tiny.vec[:, width + HD : width + 2 * HD] = dgain[1:2, :]
    tiny.first()
    for c in range(3, chunks):
        result.mix(c)

    def split_o(at, v):
        first, second = v[:, :own_rows], v[:, own_rows:]
        low = pc.y == 0
        vo[at, :] = jnp.where(low, second, first).astype(bf16)
        oo_ref[pc.y, at, :] = jnp.where(low, first, second)

    o.own(split_o)
    sends.start(vo, to, ps.at[1], pr.at[1], pc.peer(dy=1))
    tiny.second()
    q_own(q, pc, zn, gq, bq, vq, oq_ref, own_rows)
    sends.start(vq, tq, ps.at[0], pr.at[0], pc.peer(dy=1))
    tiny.last()
    small.last()
    result.last(chunks)
    arrived(to, pr.at[1])
    oo_ref[1 - pc.y] = to[...].astype(f32)
    arrived(tq, pr.at[0])
    oq_ref[1 - pc.y] = tq[...].astype(f32)
    sends.finish()


def q_own(q, pc, zn, part, buf, give, out, rows, step=32):
    lower, upper = pc.z > 0, pc.z < zn - 1
    arrived(buf.at[pc.z + 1], q.rs_r.at[pc.z], lower)
    arrived(buf.at[pc.z], q.rs_l.at[pc.z], upper)

    def total(at):
        v = part[pc.z, at, :].astype(f32)
        v = v + jnp.where(lower, buf[pc.z + 1, at, :].astype(f32), 0.0)
        return v + jnp.where(upper, buf[pc.z, at, :].astype(f32), 0.0)

    def body(i, carry):
        at = pl.ds(pl.multiple_of(i * step, step), step)
        theirs = pl.ds(pl.multiple_of((1 - pc.y) * rows + i * step, step), step)
        mine = pl.ds(pl.multiple_of(pc.y * rows + i * step, step), step)
        give[at, :] = total(theirs).astype(bf16)
        out[pc.y, at, :] = total(mine)
        return carry

    lax.fori_loop(0, rows // step, body, 0)


def rear(
    zn, heads, middle, tokens, gain, gains, flat, comb, res, seq, full_q, full_o, pre, rot, val, lse,
    ctx, tables, bias, chunk=512,
):
    tok, width = tokens.shape
    length = PLANE * tok
    e, own_rows, wide = full_q.shape
    half = heads * HD
    chunks = width // chunk
    slots = res.shape[1]
    lanes = width + 2 * HD
    shape = jax.ShapeDtypeStruct
    vmem = pltpu.VMEM
    return pl.pallas_call(
        functools.partial(rear_kernel, zn, chunk, heads),
        out_shape=(
            shape((tok, width), f32),
            shape((2, own_rows, wide), f32),
            shape((2, half, own_rows), f32),
            shape(flat.shape, f32),
            shape((1, lanes), f32),
            shape((zn, tok, width), bf16),
            shape((PLANE, slots, width), bf16),
        ),
        in_specs=[VSPEC] * 6 + [ASPEC] * 11,
        out_specs=(VSPEC,) * 5 + (ASPEC,) * 2,
        scratch_shapes=[
            vmem((PLANE, tok, width), bf16),
            vmem((e, own_rows, wide), bf16),
            vmem((e, own_rows, half), bf16),
            vmem((length, wide), f32),
            vmem((heads + 1, length, HD), bf16),
            vmem((length, HD), bf16),
            vmem((length, 128), f32),
            vmem((length, half), bf16),
            vmem((2, length, HD), f32),
            vmem((length, length), bf16),
            vmem((128, length), f32),
            vmem((128, length), f32),
            vmem((HD, length), bf16),
            vmem((length, half), bf16),
            vmem((length, wide), bf16),
            vmem((length, HD), f32),
            vmem((length, HD), f32),
            vmem((8, HD), f32),
            vmem((zn, 2 * own_rows, wide), bf16),
            vmem((zn + 1, 2 * own_rows, wide), bf16),
            vmem((own_rows, wide), bf16),
            vmem((own_rows, wide), bf16),
            vmem((zn, half, 2 * own_rows), bf16),
            vmem((zn + 1, half, 2 * own_rows), bf16),
            vmem((half, own_rows), bf16),
            vmem((half, own_rows), bf16),
        ]
        + PlaneReduce.scratch(tok, width)
        + [
            vmem((PLANE, slots, chunk), bf16),
            vmem((2, zn, tok, chunk), bf16),
            dma_sems(8),
            dma_sems(8),
            dma_sems(10),
            dma_sems(10),
            dma_sems(2, zn),
            dma_sems(2, zn),
            dma_sems(2, zn),
            dma_sems(2, zn),
            dma_sems(2),
            dma_sems(2),
            dma_sems(chunks, PLANE),
            dma_sems(chunks, PLANE),
            dma_sems(chunks, zn),
            dma_sems(chunks, zn),
            dma_sems(PLANE),
            dma_sems(chunks),
            dma_sems(10),
        ]
        + SmallSum.scratch(zn, flat.shape[1], flat.shape[2])
        + TinySum.scratch(zn, lanes),
        compiler_params=params(5),
        name="rear",
    )(
        middle, tokens, gain, gains, flat, comb, res, seq, full_q, full_o, pre, rot, val, lse, ctx,
        tables, bias,
    )


def local(
    tokens,
    out_grad,
    first_gain,
    second_gain,
    query_gain,
    key_gain,
    query_weight,
    key_weight,
    value_weight,
    output_weight,
    router_weight,
    gate_weight,
    up_weight,
    down_weight,
    expert_ids,
    router_order,
    image_starts,
):
    tok, width = tokens.shape
    zn = lax.axis_size("exp") // 2
    experts = PLANE * zn
    cap = (9 * tok * TOP + 8 * experts - 1) // (8 * experts)
    slots = zn * cap
    length = PLANE * tok
    own_rows = query_weight.shape[0]
    half = query_weight.shape[1] // 2
    heads = half // HD
    scale = HD ** (-0.5)
    exp_index = lax.axis_index("exp")
    starts = lax.dynamic_slice_in_dim(image_starts, exp_index // 2, 1, 0)[0]

    expert_axis = jnp.arange(experts, dtype=jnp.int32)
    member = jnp.any(expert_ids[:, :, None] == expert_axis[None, None, :], axis=1)
    order_here = router_order[0]
    earlier = (order_here[None, :] < order_here[:, None]).astype(bf16)
    counts = jnp.dot(earlier, member.astype(bf16), preferred_element_type=f32)
    keep = member & (counts < cap)
    slot_of = jnp.where(keep, counts, -1.0)

    resid_in = tokens.astype(f32)
    first_rms = rms_scale(resid_in)
    first_hat = resid_in * first_rms
    first_norm = (first_hat * first_gain).astype(bf16)
    q_halves = query_weight.reshape(own_rows, 2, half).transpose(1, 0, 2)
    kv = jnp.concatenate([key_weight, value_weight], axis=1)
    pack_q = jnp.concatenate([q_halves, jnp.broadcast_to(kv[None], (2,) + kv.shape)], axis=2)
    pack_o = output_weight.reshape(2, half, own_rows).transpose(0, 2, 1)
    pos = jnp.arange(length, dtype=jnp.int32)
    cosine, sine = rotary_tables(pos, HD)
    tables = jnp.stack(
        [jnp.concatenate([cosine, cosine], axis=1), jnp.concatenate([-sine, sine], axis=1)]
    )
    pieces = piece_ids(pos, starts)
    mask = allowed_mask(pos, pos, pieces, pieces)
    bias = jnp.where(mask, 0.0, NEGATIVE).astype(bf16)
    slot_t = slot_of.T.reshape(zn, PLANE, tok)
    (
        seq_norm, full_q, full_o, pre, rot, value_rows, lse, context_rows, attention, rows_g, slots_all,
    ) = front(
        zn, cap, heads, tokens, first_gain[None], pack_q, pack_o, tables,
        jnp.stack([query_gain, key_gain]), bias, out_grad, slot_t,
    )
    resid_mid = resid_in + attention
    second_rms = rms_scale(resid_mid)
    second_hat = resid_mid * second_rms
    second_norm = (second_hat * second_gain).astype(bf16)
    logits = jnp.dot(second_norm, router_weight, preferred_element_type=f32)
    mix = jax.nn.softmax(jnp.where(member, logits, NEGATIVE), axis=-1)
    mix = jnp.where(member, mix, 0.0)
    keep_mix = jnp.where(keep, mix, 0.0)
    mix_t = keep_mix.T.reshape(zn, PLANE, tok)
    rows_n, mix_rows, mix_all = send_rows(zn, cap, second_norm, slots_all, mix_t)
    mix_rows = mix_rows.reshape(PLANE * slots, 1)
    arrived_n = rows_n.reshape(PLANE * slots, width)
    arrived_g = rows_g.reshape(PLANE * slots, width)

    gate_val = jnp.dot(arrived_n, gate_weight[0], preferred_element_type=f32)
    up_val = jnp.dot(arrived_n, up_weight[0], preferred_element_type=f32)
    gate_sig = jax.nn.sigmoid(gate_val)
    gate_act = gate_val * gate_sig
    inner = (gate_act * up_val).astype(bf16)
    result = jnp.dot(inner, down_weight[0], preferred_element_type=f32).astype(bf16)
    unmixed = jnp.dot(arrived_g, down_weight[0].T, preferred_element_type=f32)
    dots = mix_rows * jnp.sum(unmixed * inner.astype(f32), axis=1, keepdims=True)
    inner_grad = unmixed * mix_rows
    mixed_inner = (inner.astype(f32) * mix_rows).astype(bf16)
    down_grad = jnp.dot(mixed_inner.T, arrived_g, preferred_element_type=f32)[None]
    gate_back = (inner_grad * up_val * gate_sig * (1.0 + gate_val * (1.0 - gate_sig))).astype(bf16)
    up_back = (inner_grad * gate_act).astype(bf16)
    gate_grad = jnp.dot(arrived_n.T, gate_back, preferred_element_type=f32)[None]
    up_grad = jnp.dot(arrived_n.T, up_back, preferred_element_type=f32)[None]
    pair_back = jnp.dot(gate_back, gate_weight[0].T, preferred_element_type=f32) + jnp.dot(
        up_back, up_weight[0].T, preferred_element_type=f32
    )
    pair_back = pair_back.astype(bf16)
    dots_high = dots.astype(bf16)
    dots_low = (dots - dots_high.astype(f32)).astype(bf16)
    place = (exp_index % 2) * 4 + lax.axis_index("tp")
    lane = jnp.arange(128, dtype=jnp.int32)[None, :]
    zero = jnp.zeros((), bf16)
    dot_lanes = jnp.where(lane == place, dots_high, zero) + jnp.where(
        lane == place + PLANE, dots_low, zero
    )

    slot_col = slots_all.transpose(0, 2, 1).reshape(zn, tok, PLANE, 1)
    mix_col = mix_all.transpose(0, 2, 1).reshape(zn, tok, PLANE, 1)
    want = jnp.where(slot_col < 0, -1.0, slot_col + (jnp.arange(zn, dtype=f32) * cap)[:, None, None, None])
    hot = want == jnp.arange(slots, dtype=f32)[None, None, None, :]
    comb = jnp.where(hot, mix_col, 0.0).astype(bf16).reshape(zn * tok, PLANE * slots)
    hot = hot.astype(bf16).reshape(zn * tok, PLANE * slots)
    pairs_sum, dots_all = back_rows(
        zn, tok, pair_back.reshape(PLANE, slots, width), dot_lanes.reshape(PLANE, slots, 128), hot
    )
    grad_out = out_grad.astype(f32)
    mix_dots = dots_all[:, :, :PLANE] + dots_all[:, :, PLANE : 2 * PLANE]
    mix_dots = mix_dots.transpose(1, 0, 2).reshape(tok, experts)
    chosen_grad = mix_dots - mix * jnp.sum(mix_dots, axis=1, keepdims=True)
    logit_grad = chosen_grad.astype(bf16)
    router_part = jnp.dot(second_norm.T, logit_grad, preferred_element_type=f32)
    norm2_back = pairs_sum + jnp.dot(logit_grad, router_weight.T, preferred_element_type=f32)
    mid_from_norm, second_gain_part = norm_back(norm2_back, second_hat, second_rms, second_gain)
    middle_grad = grad_out + mid_from_norm

    flat = jnp.concatenate([router_part.reshape(-1), second_gain_part])
    count = flat.shape[0]
    unit = PLANE * 8 * 128
    padded = -(-count // unit) * unit
    flat = jnp.pad(flat, (0, padded - count)).reshape(PLANE, padded // (PLANE * 128), 128)
    tokens_grad, sum_q, sum_o, flat, tiny, mixtures, _ = rear(
        zn, heads, middle_grad, tokens, first_gain[None], jnp.stack([query_gain, key_gain]), flat, comb,
        result.reshape(PLANE, slots, width), seq_norm, full_q, full_o, pre, rot, value_rows, lse,
        context_rows, tables, bias.T,
    )
    block_out = (resid_mid + jnp.sum(mixtures.astype(f32), axis=0)).astype(bf16)
    query_grad = jnp.concatenate([sum_q[0, :, :half], sum_q[1, :, :half]], axis=1)
    kv_grad = sum_q[0, :, half:] + sum_q[1, :, half:]
    key_grad, value_grad = kv_grad[:, :HD], kv_grad[:, HD:]
    output_grad = sum_o.reshape(2 * half, own_rows)
    flat = flat.reshape(-1)
    n_router = width * experts
    router_grad = flat[:n_router].reshape(width, experts)
    second_gain_grad = flat[n_router : n_router + width]
    tiny = tiny[0]
    first_gain_grad = tiny[:width]
    query_gain_grad = tiny[width : width + HD]
    key_gain_grad = tiny[width + HD :]
    return (
        block_out,
        tokens_grad,
        first_gain_grad,
        second_gain_grad,
        query_gain_grad,
        key_gain_grad,
        query_grad,
        key_grad,
        value_grad,
        output_grad,
        router_grad,
        gate_grad,
        up_grad,
        down_grad,
    )


def solution(mesh):
    both = ("exp", "tp")
    in_specs = (
        P(both, None),
        P(both, None),
        P(),
        P(),
        P(),
        P(),
        P("exp", "tp"),
        P("exp", "tp"),
        P("exp", "tp"),
        P("tp", "exp"),
        P(),
        P(both, None, None),
        P(both, None, None),
        P(both, None, None),
        P(both, None),
        P(both, None),
        P(),
    )
    out_specs = (
        P(both, None),
        P(both, None),
        P(),
        P(),
        P(),
        P(),
        P("exp", "tp"),
        P("exp", "tp"),
        P("exp", "tp"),
        P("tp", "exp"),
        P(),
        P(both, None, None),
        P(both, None, None),
        P(both, None, None),
    )
    return jax.shard_map(local, mesh=mesh, in_specs=in_specs, out_specs=out_specs, check_vma=False)
```

```python
import functools

import jax
import jax.numpy as jnp
from jax import lax
from jax.experimental import pallas as pl
from jax.experimental.pallas import tpu as pltpu
from jax.sharding import PartitionSpec as P

HD = 128
TOP = 8
IMG_LEN = 256
PLANE = 8

EPSILON = 1e-06
THETA = 1000000.0
NEGATIVE = -1e30

MESH = pl.DeviceIdType.MESH
f32 = jnp.float32
bf16 = jnp.bfloat16
VMEM_LIMIT = 60 << 20


def rms_scale(values):
    return lax.rsqrt(jnp.mean(values * values, axis=-1, keepdims=True) + EPSILON)


def rotary_tables(positions, width):
    half = width // 2
    freqs = THETA ** (-(jnp.arange(half, dtype=f32) * 2.0 / width))
    angles = positions.astype(f32)[:, None] * freqs[None, :]
    return (jnp.cos(angles), jnp.sin(angles))


def rotate(values, cosine, sine):
    half = values.shape[-1] // 2
    first = values[..., :half]
    second = values[..., half:]
    return jnp.concatenate(
        [first * cosine - second * sine, second * cosine + first * sine], axis=-1
    )


def unrotate(values, cosine, sine):
    half = values.shape[-1] // 2
    first = values[..., :half]
    second = values[..., half:]
    return jnp.concatenate(
        [first * cosine + second * sine, second * cosine - first * sine], axis=-1
    )


def piece_ids(positions, starts):
    inside = (positions[:, None] >= starts[None, :]) & (
        positions[:, None] < starts[None, :] + IMG_LEN
    )
    labels = jnp.arange(1, starts.shape[0] + 1, dtype=jnp.int32)
    return jnp.sum(jnp.where(inside, labels[None, :], 0), axis=1)


def allowed_mask(query_pos, key_pos, query_piece, key_piece):
    causal = key_pos[None, :] <= query_pos[:, None]
    same = (query_piece[:, None] == key_piece[None, :]) & (query_piece[:, None] > 0)
    return causal | same


def norm_back(grad_norm, hat, rms, gain):
    scaled = grad_norm * gain
    inner_mean = jnp.mean(scaled * hat, axis=-1, keepdims=True)
    lead_axes = tuple(range(grad_norm.ndim - 1))
    return (rms * (scaled - hat * inner_mean), jnp.sum(grad_norm * hat, axis=lead_axes))


class Place:
    def __init__(self):
        self.e = lax.axis_index("exp")
        self.t = lax.axis_index("tp")
        self.z = self.e // 2
        self.y = self.e % 2
        self.x = self.t // 2
        self.c = self.t % 2
        self.p = self.y * 4 + self.t

    def at(self, z, p):
        return (z * 2 + p // 4, p % 4)

    def flip(self, dy=0, dx=0, dc=0):
        y = 1 - self.y if dy else self.y
        x = 1 - self.x if dx else self.x
        c = 1 - self.c if dc else self.c
        return y * 4 + x * 2 + c

    def peer(self, dy=0, dx=0, dc=0):
        return self.at(self.z, self.flip(dy, dx, dc))

    def by(self, k):
        return self.flip((k >> 2) & 1, (k >> 1) & 1, k & 1)


class Sends:
    def __init__(self):
        self.kept = []

    def start(self, src, dst, send_sem, recv_sem, device, when=None):
        def make():
            return pltpu.make_async_remote_copy(
                src_ref=src,
                dst_ref=dst,
                send_sem=send_sem,
                recv_sem=recv_sem,
                device_id=device,
                device_id_type=MESH,
            )

        def go():
            make().start()

        if when is None:
            go()
        else:
            pl.when(when)(go)
        self.kept.append((make, when))

    def finish(self):
        for make, when in self.kept:
            if when is None:
                make().wait_send()
            else:
                pl.when(when)(lambda make=make: make().wait_send())
        self.kept = []


def arrived(dst, recv_sem, when=None):
    def go():
        pltpu.make_async_copy(dst, dst, recv_sem).wait()

    if when is None:
        go()
    else:
        pl.when(when)(go)


def greet(place, zn, ends=False, everyone=True, planes=True):
    bar = pltpu.get_barrier_semaphore()
    count = 0
    if planes:
        for k in range(1, PLANE):
            pl.semaphore_signal(
                bar, inc=1, device_id=place.at(place.z, place.by(k)), device_id_type=MESH
            )
        count += PLANE - 1
    if everyone:
        for k in range(1, zn):
            pl.semaphore_signal(
                bar,
                inc=1,
                device_id=place.at((place.z + k) % zn, place.p),
                device_id_type=MESH,
            )
        count += zn - 1
    pl.semaphore_wait(bar, count)
    if ends:
        bar2 = 0
        del bar2


class PlaneGather:
    sems = 8

    def __init__(self, place, sends, buf, ss, rs):
        self.place, self.sends, self.buf, self.ss, self.rs = place, sends, buf, ss, rs
        half = buf.shape[2] // 2
        self.cols_a = pl.ds(0, half)
        self.cols_b = pl.ds(half, half)

    def _send(self, block, which, device, cols=None):
        ref = self.buf.at[block] if cols is None else self.buf.at[block, :, cols]
        self.sends.start(ref, ref, self.ss.at[which], self.rs.at[which], device)

    def _wait(self, block, which, cols=None):
        ref = self.buf.at[block] if cols is None else self.buf.at[block, :, cols]
        arrived(ref, self.rs.at[which])

    def first(self):
        pc = self.place
        self._send(pc.p, 0, pc.peer(dy=1))
        self._send(pc.p, 1, pc.peer(dx=1))
        self._send(pc.p, 2, pc.peer(dc=1))

    def second(self):
        pc = self.place
        px, py = pc.flip(dx=1), pc.flip(dy=1)
        self._wait(px, 1)
        self._send(px, 3, pc.peer(dy=1), self.cols_a)
        self._send(px, 4, pc.peer(dc=1))
        self._wait(py, 0)
        self._send(py, 5, pc.peer(dx=1), self.cols_b)
        self._send(py, 6, pc.peer(dc=1))

    def third(self):
        pc = self.place
        pd = pc.flip(dy=1, dx=1)
        self._wait(pd, 3, self.cols_a)
        self._wait(pd, 5, self.cols_b)
        self._send(pd, 7, pc.peer(dc=1))

    def last(self):
        pc = self.place
        self._wait(pc.flip(dc=1), 2)
        self._wait(pc.flip(dc=1, dx=1), 4)
        self._wait(pc.flip(dc=1, dy=1), 6)
        self._wait(pc.flip(dc=1, dy=1, dx=1), 7)


def add_rows(dst, first, second, rows, step=32):
    def body(i, carry):
        at = pl.ds(pl.multiple_of(i * step, step), step)
        dst(at, first(at).astype(f32) + second(at).astype(f32))
        return carry

    lax.fori_loop(0, rows // step, body, 0)


class PlaneReduce:
    sems = 4 + 4 + 2

    @staticmethod
    def scratch(rows, width):
        return [
            pltpu.VMEM((4, rows, width), bf16),
            pltpu.VMEM((4, rows, width), bf16),
            pltpu.VMEM((2, rows, width // 2), bf16),
            pltpu.VMEM((2, rows, width // 2), bf16),
            pltpu.VMEM((2, rows, width // 2), bf16),
        ]

    def __init__(self, place, sends, part, out, scratch, ss, rs):
        self.place, self.sends, self.part, self.out = place, sends, part, out
        self.c1, self.s1, self.ra, self.rb, self.last = scratch
        self.ss, self.rs = ss, rs
        self.rows = part.shape[1]
        half = part.shape[2] // 2
        self.half = half
        self.cols_a = pl.ds(0, half)
        self.cols_b = pl.ds(half, half)
        pc = place
        self.chips = [(1, 1), (0, 1), (1, 0), (0, 0)]

    def _chip(self, dy, dx):
        pc = self.place
        y = 1 - pc.y if dy else pc.y
        x = 1 - pc.x if dx else pc.x
        return y, x, y * 2 + x

    def first(self, k):
        pc = self.place
        y, x, j = self._chip(*self.chips[k])
        block = y * 4 + x * 2 + (1 - pc.c)
        self.sends.start(
            self.part.at[block], self.c1.at[j], self.ss.at[k], self.rs.at[k], pc.peer(dc=1)
        )

    def second(self, k):
        pc = self.place
        y, x, j = self._chip(*self.chips[k])
        arrived(self.c1.at[j], self.rs.at[k])
        mine = y * 4 + x * 2 + pc.c

        def put(at, v):
            self.s1[j, at, :] = v.astype(bf16)

        add_rows(put, lambda at: self.part[mine, at, :], lambda at: self.c1[j, at, :], self.rows)
        dy, dx = self.chips[k]
        if dx:
            self.sends.start(
                self.s1.at[j, :, self.cols_a],
                self.ra.at[y],
                self.ss.at[4 + (0 if dy else 1)],
                self.rs.at[4 + (0 if dy else 1)],
                pc.peer(dx=1),
            )
        if dy:
            self.sends.start(
                self.s1.at[j, :, self.cols_b],
                self.rb.at[x],
                self.ss.at[6 + (0 if dx else 1)],
                self.rs.at[6 + (0 if dx else 1)],
                pc.peer(dy=1),
            )

    def third(self):
        pc = self.place
        other_y, other_x = 1 - pc.y, 1 - pc.x
        arrived(self.ra.at[other_y], self.rs.at[4])
        j = other_y * 2 + pc.x

        def put_a(at, v):
            self.ra[other_y, at, :] = v.astype(bf16)

        add_rows(
            put_a,
            lambda at: self.s1[j, at, self.cols_a],
            lambda at: self.ra[other_y, at, :],
            self.rows,
        )
        self.sends.start(
            self.ra.at[other_y], self.last.at[0], self.ss.at[8], self.rs.at[8], pc.peer(dy=1)
        )
        arrived(self.rb.at[other_x], self.rs.at[6])
        i = pc.y * 2 + other_x

        def put_b(at, v):
            self.rb[other_x, at, :] = v.astype(bf16)

        add_rows(
            put_b,
            lambda at: self.s1[i, at, self.cols_b],
            lambda at: self.rb[other_x, at, :],
            self.rows,
        )
        self.sends.start(
            self.rb.at[other_x], self.last.at[1], self.ss.at[9], self.rs.at[9], pc.peer(dx=1)
        )

    def finish(self):
        pc = self.place
        own = pc.y * 2 + pc.x
        arrived(self.ra.at[pc.y], self.rs.at[5])
        arrived(self.rb.at[pc.x], self.rs.at[7])

        def put_a(at, v):
            self.out[at, self.cols_a] = v + self.ra[pc.y, at, :].astype(f32)

        def put_b(at, v):
            self.out[at, self.cols_b] = v + self.rb[pc.x, at, :].astype(f32)

        arrived(self.last.at[0], self.rs.at[8])
        add_rows(
            put_a,
            lambda at: self.s1[own, at, self.cols_a],
            lambda at: self.last[0, at, :],
            self.rows,
        )
        arrived(self.last.at[1], self.rs.at[9])
        add_rows(
            put_b,
            lambda at: self.s1[own, at, self.cols_b],
            lambda at: self.last[1, at, :],
            self.rows,
        )


class ColumnGather:
    def __init__(self, place, sends, zn, pack, full, pair_ss, pair_rs, ss_r, ss_l, rs):
        self.place, self.sends, self.zn = place, sends, zn
        self.pack, self.full = pack, full
        self.pair_ss, self.pair_rs, self.ss_r, self.ss_l, self.rs = pair_ss, pair_rs, ss_r, ss_l, rs

    def _on(self, src, piece, right, left):
        pc = self.place
        if right is not None:
            self.sends.start(
                src,
                self.full.at[piece],
                self.ss_r.at[piece],
                self.rs.at[piece],
                pc.at(jnp.minimum(pc.z + 1, self.zn - 1), pc.p),
                right,
            )
        if left is not None:
            self.sends.start(
                src,
                self.full.at[piece],
                self.ss_l.at[piece],
                self.rs.at[piece],
                pc.at(jnp.maximum(pc.z - 1, 0), pc.p),
                left,
            )

    def pair(self):
        pc = self.place
        self.sends.start(
            self.pack.at[1 - pc.y],
            self.full.at[pc.e],
            self.pair_ss,
            self.pair_rs,
            pc.peer(dy=1),
        )

    def own(self):
        pc = self.place
        self._on(self.pack.at[pc.y], pc.e, pc.z < self.zn - 1, pc.z > 0)

    def keep(self):
        pc = self.place
        self.full[pc.e] = self.pack[pc.y]

    def partner(self):
        pc = self.place
        other = pc.z * 2 + 1 - pc.y
        arrived(self.full.at[other], self.pair_rs)
        self._on(self.full.at[other], other, pc.z < self.zn - 1, pc.z > 0)

    def step(self, k):
        pc = self.place
        for first in (True, False):
            y = pc.y if first else 1 - pc.y
            below = jnp.maximum(pc.z - k, 0) * 2 + y
            has = pc.z - k >= 0
            arrived(self.full.at[below], self.rs.at[below], has)
            self._on(
                self.full.at[below], below, jnp.logical_and(has, pc.z < self.zn - 1), None
            )
            above = jnp.minimum(pc.z + k, self.zn - 1) * 2 + y
            has = pc.z + k < self.zn
            arrived(self.full.at[above], self.rs.at[above], has)
            self._on(self.full.at[above], above, None, jnp.logical_and(has, pc.z > 0))


def dma_sems(*shape):
    return pltpu.SemaphoreType.DMA(shape)


VSPEC = pl.BlockSpec(memory_space=pltpu.VMEM)
ASPEC = pl.BlockSpec(memory_space=pl.ANY)


def params(cid):
    return pltpu.CompilerParams(
        collective_id=cid, has_side_effects=True, vmem_limit_bytes=VMEM_LIMIT
    )


class RowChain:
    def __init__(self, place, sends, zn, src, buf, chunk, ss_r, ss_l, rs):
        self.place, self.sends, self.zn = place, sends, zn
        self.src, self.buf, self.chunk = src, buf, chunk
        self.ss_r, self.ss_l, self.rs = ss_r, ss_l, rs

    def _on(self, src, c, origin, right, left):
        pc = self.place
        dst = self.buf.at[origin, :, pl.ds(c * self.chunk, self.chunk)]
        if right is not None:
            self.sends.start(
                src,
                dst,
                self.ss_r.at[c, origin],
                self.rs.at[c, origin],
                pc.at(jnp.minimum(pc.z + 1, self.zn - 1), pc.p),
                right,
            )
        if left is not None:
            self.sends.start(
                src,
                dst,
                self.ss_l.at[c, origin],
                self.rs.at[c, origin],
                pc.at(jnp.maximum(pc.z - 1, 0), pc.p),
                left,
            )

    def own(self, c):
        pc = self.place
        src = self.src.at[:, pl.ds(c * self.chunk, self.chunk)]
        self._on(src, c, pc.z, pc.z < self.zn - 1, pc.z > 0)

    def keep(self):
        self.buf[self.place.z] = self.src[...]

    def step(self, c, k):
        pc = self.place
        cols = pl.ds(c * self.chunk, self.chunk)
        below = jnp.maximum(pc.z - k, 0)
        has = pc.z - k >= 0
        ref = self.buf.at[below, :, cols]
        arrived(ref, self.rs.at[c, below], has)
        self._on(ref, c, below, jnp.logical_and(has, pc.z < self.zn - 1), None)
        above = jnp.minimum(pc.z + k, self.zn - 1)
        has = pc.z + k < self.zn
        ref = self.buf.at[above, :, cols]
        arrived(ref, self.rs.at[c, above], has)
        self._on(ref, c, above, None, jnp.logical_and(has, pc.z > 0))


def turned(values):
    return pltpu.roll(values, HD // 2, 1)


def nt_dot(a, b):
    return lax.dot_general(a, b, (((1,), (1,)), ((), ())), preferred_element_type=f32)


def tn_dot(a, b):
    return lax.dot_general(a, b, (((0,), (0,)), ((), ())), preferred_element_type=f32)


def nn_dot(a, b):
    return jnp.dot(a, b, preferred_element_type=f32)


QBLOCK = 256


def key_limit(i, length):
    return min(length, (i + 1) * QBLOCK + IMG_LEN)


def send_slots(place, sends, zn, src, dst, ss, rs):
    for k in range(1, zn):
        d = (place.z + k) % zn
        sends.start(src.at[d], dst.at[place.z], ss.at[k], rs.at[place.z], place.at(d, place.p))


def take_slots(place, zn, src, dst, rs):
    dst[place.z] = src[place.z]
    for k in range(1, zn):
        d = (place.z + k) % zn
        arrived(dst.at[d], rs.at[d])


def make_hot(zn, cap, tok, slots_ref, hot):
    row = lax.broadcasted_iota(jnp.int32, (zn * cap, tok), 0).astype(f32)

    def body(p, carry):
        for z in range(zn):
            have = slots_ref[z, pl.ds(p, 1), :]
            want = jnp.where(have < 0, -1.0, have + float(z * cap))
            hot[p, :, pl.ds(z * tok, tok)] = jnp.where(row == want, 1.0, 0.0).astype(bf16)
        return carry

    lax.fori_loop(0, PLANE, body, 0)


class PlaneSend:
    def __init__(self, place, sends, hot, rows, buf, out, chunk, ss, rs):
        self.place, self.sends = place, sends
        self.hot, self.rows, self.buf, self.out, self.chunk = hot, rows, buf, out, chunk
        self.ss, self.rs = ss, rs

    def send(self, c):
        pc = self.place
        cols = pl.ds(c * self.chunk, self.chunk)
        zn, tok, _ = self.rows.shape
        for k in (1, 2, 3, 4, 5, 6, 7, 0):
            p = pc.by(k) if k else pc.p
            got = nn_dot(self.hot[p], self.rows[:, :, cols].reshape(zn * tok, self.chunk))
            if k:
                self.buf[p, :, cols] = got.astype(bf16)
                self.sends.start(
                    self.buf.at[p, :, cols],
                    self.out.at[pc.p, :, cols],
                    self.ss.at[c, k],
                    self.rs.at[c, k],
                    pc.at(pc.z, p),
                )
            else:
                self.out[pc.p, :, cols] = got.astype(bf16)

    def take(self, c):
        cols = pl.ds(c * self.chunk, self.chunk)
        for k in range(1, PLANE):
            arrived(self.out.at[self.place.by(k), :, cols], self.rs.at[c, k])


def front_kernel(
    zn, cap, chunk, heads,
    tok_ref, gain_ref, pq_ref, po_ref, tab_ref, hg_ref, bias_ref, grad_ref, slot_ref,
    seq_ref, wq_ref, wo_ref, pre_ref, rot_ref, val_ref, lse_ref, ctx_ref, att_ref, ag_ref, so_ref,
    part, c1, s1, ra, rb, last, gb, sn, hot,
    gs, gr, ps, pr, sr, sl, rs, hs, hr, zsr, zsl, zr, ts, tr, xs, xr,
):
    place, sends = Place(), Sends()
    pc = place
    tok, width = tok_ref.shape
    length = PLANE * tok
    own_rows = pq_ref.shape[1]
    half = heads * HD
    chunks = width // chunk
    scale = HD ** (-0.5)
    greet(place, zn)
    q = ColumnGather(
        place, sends, zn, pq_ref, wq_ref, ps.at[0], pr.at[0], sr.at[0], sl.at[0], rs.at[0]
    )
    o = ColumnGather(
        place, sends, zn, po_ref, wo_ref, ps.at[1], pr.at[1], sr.at[1], sl.at[1], rs.at[1]
    )
    g = RowChain(place, sends, zn, grad_ref, gb, chunk, zsr, zsl, zr)
    q.pair()
    q.own()

    def first_norm(i, carry):
        at = pl.ds(pl.multiple_of(i * 32, 32), 32)
        v = tok_ref[at, :].astype(f32)
        seq_ref[pc.p, at, :] = (v * rms_scale(v) * gain_ref[...]).astype(bf16)
        return carry

    lax.fori_loop(0, tok // 32, first_norm, 0)
    rows = PlaneGather(place, sends, seq_ref, gs, gr)
    rows.first()
    send_slots(place, sends, zn, slot_ref, so_ref, ts, tr)
    q.keep()
    q.partner()
    rows.second()
    o.pair()
    o.keep()
    g.keep()
    rows.third()
    take_slots(place, zn, slot_ref, so_ref, tr)
    make_hot(zn, cap, tok, so_ref, hot)
    pre_ref[...] = jnp.zeros_like(pre_ref)

    def project(origin):
        cols = pl.ds(pl.multiple_of(origin * 2 * own_rows, 2 * own_rows), 2 * own_rows)
        weight = wq_ref.at[pl.ds(2 * origin, 2)]

        def body(i, carry):
            at = pl.ds(pl.multiple_of(i * 2 * tok, 2 * tok), 2 * tok)
            lhs = seq_ref[pl.ds(2 * i, 2), :, cols].reshape(2 * tok, 2 * own_rows)
            pre_ref[at, :] += nn_dot(lhs, weight[...].reshape(2 * own_rows, half + 2 * HD))
            return carry

        lax.fori_loop(0, PLANE // 2, body, 0)

    def project_step(k):
        pl.when(pc.z - k >= 0)(lambda: project(jnp.maximum(pc.z - k, 0)))
        pl.when(pc.z + k < zn)(lambda: project(jnp.minimum(pc.z + k, zn - 1)))

    for k in range(1, zn):
        q.step(k)
        if k == 1:
            rows.last()
            project(pc.z)
        if k == zn - 1:
            for c in range(chunks):
                g.own(c)
            o.own()
            o.partner()
        project_step(k)

    def turn(i, carry):
        at = pl.ds(pl.multiple_of(i * 128, 128), 128)
        cos, sin = tab_ref[0, at, :], tab_ref[1, at, :]
        for h in range(heads + 1):
            v = pre_ref[at, h * HD : (h + 1) * HD]
            gain = hg_ref[pl.ds(0 if h < heads else 1, 1), :]
            v = v * rms_scale(v) * gain
            rot_ref[h, at, :] = (v * cos + turned(v) * sin).astype(bf16)
        val_ref[at, :] = pre_ref[at, half + HD : half + 2 * HD].astype(bf16)
        return carry

    lax.fori_loop(0, length // 128, turn, 0)
    lane = lax.broadcasted_iota(jnp.int32, (QBLOCK, 128), 1)

    def attend(i):
        limit = key_limit(i, length)
        at = slice(i * QBLOCK, (i + 1) * QBLOCK)

        def body(h, carry):
            scores = nt_dot(rot_ref[h, at, :], rot_ref[heads, :limit, :]) * scale
            scores = scores + bias_ref[at, :limit].astype(f32)
            top = jnp.max(scores, axis=1, keepdims=True)
            expo = jnp.exp(scores - top)
            total = jnp.sum(expo, axis=1, keepdims=True)
            low = (expo * (1.0 / total)).astype(bf16)
            cols = pl.ds(pl.multiple_of(h * HD, HD), HD)
            ctx_ref[at, cols] = nn_dot(low, val_ref[:limit, :]).astype(bf16)
            lse_ref[at, :] = jnp.where(lane == h, top + jnp.log(total), lse_ref[at, :])
            return carry

        lax.fori_loop(0, heads, body, 0)

    lse_ref[...] = jnp.zeros_like(lse_ref)
    hops = [(c, k) for k in range(1, zn) for c in range(chunks)]
    blocks = length // QBLOCK
    ahead = min(len(hops), 2 * (blocks - 1))
    done = 0
    for i in range(blocks):
        attend(i)
        while i < blocks - 1 and done < ahead and done < 2 * (i + 1):
            g.step(*hops[done])
            done += 1

    def output(origin):
        cols = pl.ds(pl.multiple_of(origin * 2 * own_rows, 2 * own_rows), 2 * own_rows)
        weight = wo_ref.at[pl.ds(2 * origin, 2)]

        def body(i, carry):
            at = pl.ds(pl.multiple_of(i * 2 * tok, 2 * tok), 2 * tok)
            got = nt_dot(ctx_ref[at, :], weight[...].reshape(2 * own_rows, half))
            part[pl.ds(2 * i, 2), :, cols] = got.astype(bf16).reshape(2, tok, 2 * own_rows)
            return carry

        lax.fori_loop(0, PLANE // 2, body, 0)

    def output_step(k):
        pl.when(pc.z - k >= 0)(lambda: output(jnp.maximum(pc.z - k, 0)))
        pl.when(pc.z + k < zn)(lambda: output(jnp.minimum(pc.z + k, zn - 1)))

    output(pc.z)
    give = PlaneSend(place, sends, hot, gb, sn, ag_ref, chunk, xs, xr)
    for c, k in hops[done:]:
        g.step(c, k)
        if k == zn - 1:
            give.send(c)
    for k in range(1, zn):
        o.step(k)
        output_step(k)
    red = PlaneReduce(place, sends, part, att_ref, (c1, s1, ra, rb, last), hs, hr)
    for k in range(4):
        red.first(k)
    for k in range(4):
        red.second(k)
    red.third()
    red.finish()
    for c in range(chunks):
        give.take(c)
    sends.finish()


def front(zn, cap, heads, tokens, gain, pack_q, pack_o, tables, gains, bias, grad, slot, chunk=512):
    tok, width = tokens.shape
    length = PLANE * tok
    e = 2 * zn
    slots = zn * cap
    chunks = width // chunk
    half = heads * HD
    shape = jax.ShapeDtypeStruct
    return pl.pallas_call(
        functools.partial(front_kernel, zn, cap, chunk, heads),
        out_shape=(
            shape((PLANE, tok, width), bf16),
            shape((e,) + pack_q.shape[1:], bf16),
            shape((e,) + pack_o.shape[1:], bf16),
            shape((length, half + 2 * HD), f32),
            shape((heads + 1, length, HD), bf16),
            shape((length, HD), bf16),
            shape((length, 128), f32),
            shape((length, half), bf16),
            shape((tok, width), f32),
            shape((PLANE, slots, width), bf16),
            shape(slot.shape, f32),
        ),
        in_specs=[VSPEC] * 9,
        out_specs=(VSPEC,) * 11,
        scratch_shapes=[pltpu.VMEM((PLANE, tok, width), bf16)]
        + PlaneReduce.scratch(tok, width)
        + [
            pltpu.VMEM((zn, tok, width), bf16),
            pltpu.VMEM((PLANE, slots, width), bf16),
            pltpu.VMEM((PLANE, slots, zn * tok), bf16),
            dma_sems(8),
            dma_sems(8),
            dma_sems(2),
            dma_sems(2),
            dma_sems(2, e),
            dma_sems(2, e),
            dma_sems(2, e),
            dma_sems(10),
            dma_sems(10),
            dma_sems(chunks, zn),
            dma_sems(chunks, zn),
            dma_sems(chunks, zn),
            dma_sems(zn),
            dma_sems(zn),
            dma_sems(chunks, PLANE),
            dma_sems(chunks, PLANE),
        ],
        compiler_params=params(0),
        name="front",
    )(tokens, gain, pack_q, pack_o, tables, gains, bias, grad, slot)


class Flow:
    def __init__(self, stage, sems):
        self.stage, self.sems = stage, sems
        self.count = 0
        self.flight = [None, None]

    def slot(self):
        i = self.count % 2
        if self.flight[i] is not None:
            self.flight[i].wait()
            self.flight[i] = None
        return i

    def send(self, dst):
        i = self.count % 2
        copy = pltpu.make_async_copy(self.stage.at[i], dst, self.sems.at[i])
        copy.start()
        self.flight[i] = copy
        self.count += 1

    def finish(self):
        for i in range(2):
            if self.flight[i] is not None:
                self.flight[i].wait()
                self.flight[i] = None


def there_kernel(
    zn, cap, chunk, norm_ref, slots_ref, mix_ref, ag_hbm, gate_hbm, up_hbm, down_hbm,
    an_ref, mid_ref, dot_ref, hot_t_hbm, comb_hbm,
    nb, sn, hot, mo, mrow, mr, wg, wu, wd, ag, gate, up, unmixed, stage, loads, flows,
    zsr, zsl, zr, ts, tr, xs, xr, ys, yr,
):
    place, sends = Place(), Sends()
    pc = place
    greet(place, zn)
    tok, width = norm_ref.shape
    slots = zn * cap
    rows = PLANE * slots
    chunks = width // chunk
    hidden = wd.shape[0]
    fetch = [
        pltpu.make_async_copy(src, dst, loads.at[i])
        for i, (src, dst) in enumerate(((down_hbm, wd), (gate_hbm, wg), (up_hbm, wu)))
    ]
    parts = [
        pltpu.make_async_copy(
            ag_hbm.at[:, :, pl.ds(c * chunk, chunk)], ag.at[c % 2], loads.at[3 + c % 2]
        )
        for c in range(chunks)
    ]
    n = RowChain(place, sends, zn, norm_ref, nb, chunk, zsr, zsl, zr)
    for c in range(chunks):
        n.own(c)
    send_slots(place, sends, zn, mix_ref, mo, ts, tr)
    fetch[0].start()
    parts[0].start()
    if chunks > 1:
        parts[1].start()
    fetch[1].start()
    fetch[2].start()
    n.keep()
    make_hot(zn, cap, tok, slots_ref, hot)
    take_slots(place, zn, mix_ref, mo, tr)

    def mixes(p, carry):
        row = jnp.concatenate([mo[z, pl.ds(p, 1), :] for z in range(zn)], axis=1)
        high = row.astype(bf16)
        rest = row - high.astype(f32)
        middle = rest.astype(bf16)
        low = (rest - middle.astype(f32)).astype(bf16)
        zero = jnp.zeros((13, zn * tok), bf16)
        got = nt_dot(jnp.concatenate([high, middle, low, zero], axis=0), hot[p])
        mrow[p] = jnp.sum(got, axis=0, keepdims=True)
        return carry

    lax.fori_loop(0, PLANE, mixes, 0)
    for k in range(1, PLANE):
        p = pc.by(k)
        sends.start(mrow.at[p], mr.at[pc.p], ys.at[k], yr.at[k], pc.at(pc.z, p))
    mr[pc.p] = mrow[pc.p]
    fetch[0].wait()
    give = PlaneSend(place, sends, hot, nb, sn, an_ref, chunk, xs, xr)
    half = PLANE // 2

    def back_through(c):
        cols = pl.ds(c * chunk, chunk)
        parts[c].wait()

        def body(i, carry):
            at = pl.ds(i * half, half)
            got = nt_dot(ag[c % 2, at].reshape(half * slots, chunk), wd[:, cols])
            got = got.reshape(half, slots, hidden)
            unmixed[at] = got if c == 0 else unmixed[at] + got
            return carry

        lax.fori_loop(0, 2, body, 0)
        if c + 2 < chunks:
            parts[c + 2].start()

    for c in range(chunks):
        for k in range(1, zn):
            n.step(c, k)
        give.send(c)
        back_through(c)

    lane = lax.broadcasted_iota(jnp.int32, (tok, rows), 1).astype(f32)

    def tables(z, carry):
        zero = jnp.zeros((120, tok), f32)
        have = jnp.concatenate([slots_ref[z], zero], axis=0).T
        mixed = jnp.concatenate([mo[z], zero], axis=0).T
        one = jnp.zeros((tok, rows), f32)
        mix = jnp.zeros((tok, rows), f32)
        base = (z * cap).astype(f32)
        for p in range(PLANE):
            col = have[:, p : p + 1]
            hit = lane == jnp.where(col < 0, -1.0, col + base + float(p * slots))
            one = jnp.where(hit, 1.0, one)
            mix = jnp.where(hit, mixed[:, p : p + 1], mix)
        stage[0] = one.astype(bf16)
        stage[1] = mix.astype(bf16)
        at = pl.ds(pl.multiple_of(z * tok, tok), tok)
        out = [
            pltpu.make_async_copy(stage.at[i], dst.at[at, :], flows.at[i])
            for i, dst in enumerate((hot_t_hbm, comb_hbm))
        ]
        for copy in out:
            copy.start()
        for copy in out:
            copy.wait()
        return carry

    lax.fori_loop(0, zn, tables, 0)
    fetch[1].wait()
    fetch[2].wait()
    for c in range(chunks):
        cols = pl.ds(c * chunk, chunk)
        give.take(c)

        def into(i, carry):
            at = pl.ds(i * half, half)
            lhs = an_ref[at, :, cols].reshape(half * slots, chunk)
            for weight, acc in ((wg, gate), (wu, up)):
                got = nn_dot(lhs, weight[cols, :]).reshape(half, slots, hidden)
                acc[at] = got if c == 0 else acc[at] + got
            return carry

        lax.fori_loop(0, 2, into, 0)
    for k in range(1, PLANE):
        arrived(mr.at[pc.by(k)], yr.at[k])
    place_lane = lax.broadcasted_iota(jnp.int32, (slots, 128), 1)
    r = lax.broadcasted_iota(jnp.int32, (slots, slots), 0)
    s = lax.broadcasted_iota(jnp.int32, (slots, slots), 1)

    def acts(p, carry):
        mix = jnp.sum(jnp.where(r == s, mr[p], 0.0), axis=1, keepdims=True)
        g, u, d = gate[p], up[p], unmixed[p]
        sig = jax.nn.sigmoid(g)
        act = g * sig
        inner = (act * u).astype(bf16)
        mid_ref[0, p] = inner
        wide = inner.astype(f32)
        mid_ref[1, p] = (wide * mix).astype(bf16)
        dots = mix * jnp.sum(d * wide, axis=1, keepdims=True)
        high = dots.astype(bf16).astype(f32)
        dot = jnp.where(place_lane == pc.p, high, 0.0)
        dot = jnp.where(place_lane == pc.p + PLANE, dots - high, dot)
        dot_ref[p] = dot.astype(bf16)
        d = d * mix
        mid_ref[2, p] = (d * u * sig * (1.0 + g * (1.0 - sig))).astype(bf16)
        mid_ref[3, p] = (d * act).astype(bf16)
        return carry

    lax.fori_loop(0, PLANE, acts, 0)
    sends.finish()


def there(zn, cap, norm, slots_all, mix, ag, gate, up, down, chunk=512):
    tok, width = norm.shape
    slots = zn * cap
    hidden = down.shape[0]
    chunks = width // chunk
    shape = jax.ShapeDtypeStruct
    vmem = pltpu.VMEM
    return pl.pallas_call(
        functools.partial(there_kernel, zn, cap, chunk),
        out_shape=(
            shape((PLANE, slots, width), bf16),
            shape((4, PLANE, slots, hidden), bf16),
            shape((PLANE, slots, 128), bf16),
            shape((zn * tok, PLANE * slots), bf16),
            shape((zn * tok, PLANE * slots), bf16),
        ),
        in_specs=[VSPEC] * 3 + [ASPEC] * 4,
        out_specs=(VSPEC,) * 3 + (ASPEC,) * 2,
        scratch_shapes=[
            vmem((zn, tok, width), bf16),
            vmem((PLANE, slots, width), bf16),
            vmem((PLANE, slots, zn * tok), bf16),
            vmem(mix.shape, f32),
            vmem((PLANE, 1, slots), f32),
            vmem((PLANE, 1, slots), f32),
            vmem(gate.shape, bf16),
            vmem(up.shape, bf16),
            vmem(down.shape, bf16),
            vmem((2, PLANE, slots, chunk), bf16),
            vmem((PLANE, slots, hidden), f32),
            vmem((PLANE, slots, hidden), f32),
            vmem((PLANE, slots, hidden), f32),
            vmem((2, tok, PLANE * slots), bf16),
            dma_sems(5),
            dma_sems(2),
            dma_sems(chunks, zn),
            dma_sems(chunks, zn),
            dma_sems(chunks, zn),
            dma_sems(zn),
            dma_sems(zn),
            dma_sems(chunks, PLANE),
            dma_sems(chunks, PLANE),
            dma_sems(PLANE),
            dma_sems(PLANE),
        ],
        compiler_params=params(3),
        name="there",
    )(norm, slots_all, mix, ag, gate, up, down)


def back_kernel(
    zn, chunk, dot_ref, hot_ref, mid_hbm, an_hbm, ag_hbm, gate_hbm, up_hbm, down_hbm,
    dots_ref, ap_hbm, res_hbm, gg_hbm, ug_hbm, dg_hbm,
    mids, an, ag, wg, wu, wd, pb, rp, rd, zd, zp, wide, tall, flat,
    loads, flows, xs, xr, ds, dr, zs, zr, es, er, os,
):
    place, sends = Place(), Sends()
    pc = place
    fetch = [
        pltpu.make_async_copy(src, dst, loads.at[i])
        for i, (src, dst) in enumerate(
            (
                (gate_hbm, wg), (up_hbm, wu), (mid_hbm.at[2], mids.at[2]), (mid_hbm.at[3], mids.at[3]),
                (mid_hbm.at[0], mids.at[0]), (down_hbm, wd), (mid_hbm.at[1], mids.at[1]), (ag_hbm, ag),
                (an_hbm, an),
            )
        )
    ]
    for copy in fetch:
        copy.start()
    greet(place, zn)
    _, slots, width = pb.shape
    hidden = wd.shape[0]
    chunks = width // chunk
    tok = dots_ref.shape[1]
    far = [(pc.z + k) % zn for k in range(1, zn)]
    half = PLANE // 2
    for k in range(1, PLANE):
        p = pc.by(k)
        sends.start(dot_ref.at[p], rd.at[pc.p], ds.at[k], dr.at[k], pc.at(pc.z, p))
    for copy in fetch[:4]:
        copy.wait()
    for c in range(chunks):
        cols = pl.ds(c * chunk, chunk)

        def pair(i, carry):
            at = pl.ds(i * half, half)
            got = nt_dot(mids[2, at].reshape(half * slots, hidden), wg[cols, :])
            got = got + nt_dot(mids[3, at].reshape(half * slots, hidden), wu[cols, :])
            pb[at, :, cols] = got.astype(bf16).reshape(half, slots, chunk)
            return carry

        lax.fori_loop(0, 2, pair, 0)
        for k in range(1, PLANE):
            p = pc.by(k)
            sends.start(
                pb.at[p, :, cols], rp.at[pc.p, :, cols], xs.at[c, k], xr.at[c, k], pc.at(pc.z, p)
            )
        rp[pc.p, :, cols] = pb[pc.p, :, cols]
    rd[pc.p] = dot_ref[pc.p]
    for k in range(1, PLANE):
        arrived(rd.at[pc.by(k)], dr.at[k])
    zd[...] = nn_dot(hot_ref[...], rd[...].reshape(PLANE * slots, 128)).reshape(zn, tok, 128)
    for k, d in enumerate(far):
        sends.start(zd.at[d], dots_ref.at[pc.z], es.at[k], er.at[pc.z], pc.at(d, pc.p))
    dots_ref[pc.z] = zd[pc.z]

    flow_r, flow_g, flow_u, flow_d = (
        Flow(buf, flows.at[i]) for i, buf in enumerate((wide, tall.at[0], tall.at[1], flat))
    )
    keeps = []

    def result(c):
        cols = pl.ds(c * chunk, chunk)
        slot = flow_r.slot()

        def body(i, carry):
            at = pl.ds(i * half, half)
            got = nn_dot(mids[0, at].reshape(half * slots, hidden), wd[:, cols])
            wide[slot, at] = got.astype(bf16).reshape(half, slots, chunk)
            return carry

        lax.fori_loop(0, 2, body, 0)
        flow_r.send(res_hbm.at[:, :, cols])

    def down_grad(i):
        m = pl.ds(i * 128, 128)
        slot = flow_d.slot()
        lhs = mids[1, :, :, m].reshape(PLANE * slots, 128)

        def body(j, carry):
            cols = pl.ds(pl.multiple_of(j * chunk, chunk), chunk)
            flat[slot, :, cols] = tn_dot(lhs, ag[:, :, cols].reshape(PLANE * slots, chunk))
            return carry

        lax.fori_loop(0, chunks, body, 0)
        flow_d.send(dg_hbm.at[m, :])

    def gate_up_grad(i):
        m = pl.ds(i * 256, 256)
        lhs = an[:, :, m].reshape(PLANE * slots, 256)
        for which, flow, dst in ((0, flow_g, gg_hbm), (1, flow_u, ug_hbm)):
            slot = flow.slot()
            rhs = mids[2 + which].reshape(PLANE * slots, hidden)
            tall[which, slot] = tn_dot(lhs, rhs)
            flow.send(dst.at[m, :])

    def combine(c):
        cols = pl.ds(c * chunk, chunk)
        for k in range(1, PLANE):
            arrived(rp.at[pc.by(k), :, cols], xr.at[c, k])
        got = nn_dot(hot_ref[...], rp[:, :, cols].reshape(PLANE * slots, chunk))
        zp[:, :, cols] = got.astype(bf16).reshape(zn, tok, chunk)
        for k, d in enumerate(far):
            sends.start(
                zp.at[d, :, cols],
                ap_hbm.at[pc.z, :, cols],
                zs.at[c, k],
                zr.at[c, pc.z],
                pc.at(d, pc.p),
            )
        keep = pltpu.make_async_copy(zp.at[pc.z, :, cols], ap_hbm.at[pc.z, :, cols], os.at[c])
        keep.start()
        keeps.append(keep)

    for copy in fetch[4:6]:
        copy.wait()
    for c in range(chunks):
        result(c)
    for copy in fetch[6:]:
        copy.wait()
    work = [functools.partial(down_grad, i) for i in range(hidden // 128)]
    work += [functools.partial(gate_up_grad, i) for i in range(width // 256)]
    share = -(-len(work) // chunks)
    for c in range(chunks):
        for item in work[c * share : (c + 1) * share]:
            item()
        combine(c)
    for c in range(chunks):
        for d in far:
            arrived(ap_hbm.at[d, :, pl.ds(c * chunk, chunk)], zr.at[c, d])
    for keep in keeps:
        keep.wait()
    for d in far:
        arrived(dots_ref.at[d], er.at[d])
    for flow in (flow_r, flow_g, flow_u, flow_d):
        flow.finish()
    sends.finish()


def back_rows(zn, tok, dots, hot, mids, an, ag, gate, up, down, chunk=512):
    _, slots, width = an.shape
    hidden = down.shape[0]
    chunks = width // chunk
    shape = jax.ShapeDtypeStruct
    vmem = pltpu.VMEM
    return pl.pallas_call(
        functools.partial(back_kernel, zn, chunk),
        out_shape=(
            shape((zn, tok, 128), f32),
            shape((zn, tok, width), bf16),
            shape((PLANE, slots, width), bf16),
            shape(gate.shape, f32),
            shape(up.shape, f32),
            shape(down.shape, f32),
        ),
        in_specs=[VSPEC] * 2 + [ASPEC] * 6,
        out_specs=(VSPEC,) + (ASPEC,) * 5,
        scratch_shapes=[
            vmem((4, PLANE, slots, hidden), bf16),
            vmem((PLANE, slots, width), bf16),
            vmem((PLANE, slots, width), bf16),
            vmem(gate.shape, bf16),
            vmem(up.shape, bf16),
            vmem(down.shape, bf16),
            vmem((PLANE, slots, width), bf16),
            vmem((PLANE, slots, width), bf16),
            vmem((PLANE, slots, 128), bf16),
            vmem((zn, tok, 128), f32),
            vmem((zn, tok, width), bf16),
            vmem((2, PLANE, slots, chunk), bf16),
            vmem((2, 2, 256, hidden), f32),
            vmem((2, 128, width), f32),
            dma_sems(9),
            dma_sems(4, 2),
            dma_sems(chunks, PLANE),
            dma_sems(chunks, PLANE),
            dma_sems(PLANE),
            dma_sems(PLANE),
            dma_sems(chunks, zn),
            dma_sems(chunks, zn),
            dma_sems(zn),
            dma_sems(zn),
            dma_sems(chunks),
        ],
        compiler_params=params(4),
        name="back_rows",
    )(dots, hot, mids, an, ag, gate, up, down)


class ColumnReduce:
    def __init__(self, place, sends, zn, part, buf, ss_r, ss_l, rs_r, rs_l):
        self.place, self.sends, self.zn = place, sends, zn
        self.part, self.buf = part, buf
        self.ss_r, self.ss_l, self.rs_r, self.rs_l = ss_r, ss_l, rs_r, rs_l

    def _hop(self, slot, rs, ss, d, start, inner, device):
        rows = self.part.shape[1]

        def add():
            arrived(self.buf.at[slot], rs.at[d])

            def put(at, v):
                self.buf[slot, at, :] = v.astype(bf16)

            add_rows(put, lambda at: self.part[d, at, :], lambda at: self.buf[slot, at, :], rows)

        both = jnp.logical_and(start, inner)
        pl.when(both)(add)
        self.sends.start(
            self.buf.at[slot], self.buf.at[slot], ss.at[d], rs.at[d], device, both
        )
        self.sends.start(
            self.part.at[d],
            self.buf.at[slot],
            ss.at[d],
            rs.at[d],
            device,
            jnp.logical_and(start, jnp.logical_not(inner)),
        )

    def step(self, k):
        pc, zn = self.place, self.zn
        d = zn - 1 - k
        right = pc.at(jnp.minimum(pc.z + 1, zn - 1), pc.p)
        left = pc.at(jnp.maximum(pc.z - 1, 0), pc.p)
        self._hop(d + 1, self.rs_r, self.ss_r, d, pc.z < d, pc.z > 0, right)
        d = k
        self._hop(d, self.rs_l, self.ss_l, d, pc.z > d, pc.z < zn - 1, left)

    def own(self, use, step=32):
        pc, zn = self.place, self.zn
        lower, upper = pc.z > 0, pc.z < zn - 1
        arrived(self.buf.at[pc.z + 1], self.rs_r.at[pc.z], lower)
        arrived(self.buf.at[pc.z], self.rs_l.at[pc.z], upper)

        def body(i, carry):
            at = pl.ds(pl.multiple_of(i * step, step), step)
            v = self.part[pc.z, at, :].astype(f32)
            v = v + jnp.where(lower, self.buf[pc.z + 1, at, :].astype(f32), 0.0)
            v = v + jnp.where(upper, self.buf[pc.z, at, :].astype(f32), 0.0)
            use(at, v)
            return carry

        lax.fori_loop(0, self.part.shape[1] // step, body, 0)


class SmallSum:
    @staticmethod
    def scratch(zn, rows, lanes):
        return [
            pltpu.VMEM((PLANE, rows, lanes), f32),
            pltpu.VMEM((rows, lanes), f32),
            pltpu.VMEM((zn, rows, lanes), f32),
            dma_sems(PLANE),
            dma_sems(PLANE),
            dma_sems(zn),
            dma_sems(zn),
            dma_sems(PLANE),
            dma_sems(PLANE),
        ]

    def __init__(self, place, sends, zn, flat, out, scratch):
        self.place, self.sends, self.zn, self.flat, self.out = place, sends, zn, flat, out
        self.l1, self.mid, self.l2, self.a, self.ar, self.b, self.br, self.c, self.cr = scratch

    def first(self):
        pc = self.place
        for k in range(1, PLANE):
            p = pc.by(k)
            self.sends.start(
                self.flat.at[p], self.l1.at[pc.p], self.a.at[k], self.ar.at[k], pc.at(pc.z, p)
            )
        self.l1[pc.p] = self.flat[pc.p]

    def second(self):
        pc, zn = self.place, self.zn
        for k in range(1, PLANE):
            arrived(self.l1.at[pc.by(k)], self.ar.at[k])
        total = self.l1[0]
        for k in range(1, PLANE):
            total = total + self.l1[k]
        self.mid[...] = total
        self.l2[pc.z] = total
        for k in range(1, zn):
            d = (pc.z + k) % zn
            self.sends.start(
                self.mid, self.l2.at[pc.z], self.b.at[k], self.br.at[pc.z], pc.at(d, pc.p)
            )

    def _column(self):
        pc, zn = self.place, self.zn
        for k in range(1, zn):
            d = (pc.z + k) % zn
            arrived(self.l2.at[d], self.br.at[d])
        total = self.l2[0]
        for z in range(1, zn):
            total = total + self.l2[z]
        return total

    def third(self):
        pc = self.place
        self.out[pc.p] = self._column()
        for k in range(1, PLANE):
            p = pc.by(k)
            self.sends.start(
                self.out.at[pc.p], self.out.at[pc.p], self.c.at[k], self.cr.at[k], pc.at(pc.z, p)
            )

    def last(self):
        pc = self.place
        for k in range(1, PLANE):
            arrived(self.out.at[pc.by(k)], self.cr.at[k])


class TinySum:
    @staticmethod
    def scratch(zn, lanes):
        return [
            pltpu.VMEM((1, lanes), f32),
            pltpu.VMEM((PLANE, 1, lanes), f32),
            pltpu.VMEM((1, lanes), f32),
            pltpu.VMEM((zn, 1, lanes), f32),
            dma_sems(PLANE),
            dma_sems(PLANE),
            dma_sems(zn),
            dma_sems(zn),
        ]

    def __init__(self, place, sends, zn, out, scratch):
        self.place, self.sends, self.zn, self.out = place, sends, zn, out
        self.vec, self.l1, self.mid, self.l2, self.a, self.ar, self.b, self.br = scratch

    def first(self):
        pc = self.place
        for k in range(1, PLANE):
            p = pc.by(k)
            self.sends.start(
                self.vec, self.l1.at[pc.p], self.a.at[k], self.ar.at[k], pc.at(pc.z, p)
            )
        self.l1[pc.p] = self.vec[...]

    def second(self):
        pc, zn = self.place, self.zn
        for k in range(1, PLANE):
            arrived(self.l1.at[pc.by(k)], self.ar.at[k])
        total = self.l1[0]
        for k in range(1, PLANE):
            total = total + self.l1[k]
        self.mid[...] = total
        self.l2[pc.z] = total
        for k in range(1, zn):
            d = (pc.z + k) % zn
            self.sends.start(
                self.mid, self.l2.at[pc.z], self.b.at[k], self.br.at[pc.z], pc.at(d, pc.p)
            )

    def last(self):
        pc, zn = self.place, self.zn
        for k in range(1, zn):
            d = (pc.z + k) % zn
            arrived(self.l2.at[d], self.br.at[d])
        total = self.l2[0]
        for z in range(1, zn):
            total = total + self.l2[z]
        self.out[...] = total


class Result:
    def __init__(self, place, zn, res, comb, rr, am, rbuf, zbuf, chunk, xs, xr, zs, zr, ls, os):
        self.place, self.zn, self.res, self.comb = place, zn, res, comb
        self.rr, self.am, self.rbuf, self.zbuf, self.chunk = rr, am, rbuf, zbuf, chunk
        self.xs, self.xr, self.zs, self.zr, self.ls, self.os = xs, xr, zs, zr, ls, os
        self.flight = {}

    def first(self, sends, chunks):
        pc = self.place
        for c in range(chunks):
            cols = pl.ds(c * self.chunk, self.chunk)
            for k in range(1, PLANE):
                p = pc.by(k)
                sends.start(
                    self.res.at[p, :, cols],
                    self.rr.at[pc.p, :, cols],
                    self.xs.at[c, k],
                    self.xr.at[c, k],
                    pc.at(pc.z, p),
                )

    def mix(self, c):
        pc, zn = self.place, self.zn
        cols = pl.ds(c * self.chunk, self.chunk)
        own = pltpu.make_async_copy(self.res.at[pc.p, :, cols], self.rbuf.at[pc.p], self.ls.at[0])
        own.start()
        copies = []
        for k in range(1, PLANE):
            p = pc.by(k)
            arrived(self.rr.at[p, :, cols], self.xr.at[c, k])
            copy = pltpu.make_async_copy(self.rr.at[p, :, cols], self.rbuf.at[p], self.ls.at[k])
            copy.start()
            copies.append(copy)
        own.wait()
        for copy in copies:
            copy.wait()
        self.settle(c - 2)
        slot = c % 2
        _, slots, chunk = self.rbuf.shape
        tok = self.zbuf.shape[2]
        unit = min(512, zn * tok)
        per = unit // tok
        rows = self.rbuf[...].reshape(PLANE * slots, chunk)
        for i in range(zn * tok // unit):
            got = nn_dot(self.comb[i * unit : (i + 1) * unit, :], rows)
            self.zbuf[slot, i * per : (i + 1) * per] = got.astype(bf16).reshape(per, tok, chunk)
        flight = []
        for k in range(1, zn):
            d = (pc.z + k) % zn
            flight.append(
                pltpu.make_async_remote_copy(
                    src_ref=self.zbuf.at[slot, d],
                    dst_ref=self.am.at[pc.z, :, cols],
                    send_sem=self.zs.at[c, k],
                    recv_sem=self.zr.at[c, pc.z],
                    device_id=pc.at(d, pc.p),
                    device_id_type=MESH,
                )
            )
        for copy in flight:
            copy.start()
        keep = pltpu.make_async_copy(
            self.zbuf.at[slot, pc.z], self.am.at[pc.z, :, cols], self.os.at[c]
        )
        keep.start()
        self.flight[c] = (flight, keep)

    def settle(self, c):
        if c in self.flight:
            flight, keep = self.flight.pop(c)
            for copy in flight:
                copy.wait_send()
            keep.wait()

    def last(self, chunks):
        pc, zn = self.place, self.zn
        for c in range(chunks):
            self.settle(c)
            for k in range(1, zn):
                d = (pc.z + k) % zn
                arrived(self.am.at[d, :, pl.ds(c * self.chunk, self.chunk)], self.zr.at[c, d])


def rear_kernel(
    zn, chunk, heads,
    mid_ref, tok_ref, gain_ref, hg_ref, flat_ref, comb_ref,
    res_hbm, seq_hbm, wq_hbm, wo_hbm, pre_hbm, rot_hbm, val_hbm, lse_hbm, ctx_hbm, tab_hbm, bias_hbm,
    grad_ref, oq_ref, oo_ref, sum_ref, tiny_ref, am_hbm, rr_hbm,
    big, wq, wo, pre, rot, val, lse, ctx, tab, bias,
    lse_t, del_t, key_t, cback, aback, dk, dv, dgain,
    gq, bq, vq, tq, go, bo, vo, to,
    c1, s1, ra, rb, last, rbuf, zbuf,
    gs, gr, hs, hr, sr, sl, rr, rl, ps, pr, xs, xr, zs, zr, ls, os, loads,
    *rest,
):
    place, sends = Place(), Sends()
    pc = place
    small_scratch, tiny_scratch = rest[:9], rest[9:]
    tok, width = mid_ref.shape
    length = PLANE * tok
    half = heads * HD
    own_rows = wq.shape[1]
    chunks = width // chunk
    scale = HD ** (-0.5)
    greet(place, zn)
    pairs = (
        (wo_hbm, wo), (ctx_hbm, ctx), (rot_hbm, rot), (val_hbm, val), (lse_hbm, lse),
        (bias_hbm, bias), (pre_hbm, pre), (tab_hbm, tab), (wq_hbm, wq),
    )
    fetch = [pltpu.make_async_copy(a, b, loads.at[i]) for i, (a, b) in enumerate(pairs)]
    small = SmallSum(place, sends, zn, flat_ref, sum_ref, small_scratch)
    tiny = TinySum(place, sends, zn, tiny_ref, tiny_scratch)
    row_sends = Sends()
    rows = PlaneGather(place, row_sends, big, gs, gr)
    result = Result(
        place, zn, res_hbm, comb_ref, rr_hbm, am_hbm, rbuf, zbuf, chunk, xs, xr, zs, zr, ls, os
    )
    o = ColumnReduce(place, sends, zn, go, bo, sr.at[1], sl.at[1], rr.at[1], rl.at[1])
    q = ColumnReduce(place, sends, zn, gq, bq, sr.at[0], sl.at[0], rr.at[0], rl.at[0])

    def stage(i, carry):
        at = pl.ds(pl.multiple_of(i * 32, 32), 32)
        big[pc.p, at, :] = mid_ref[at, :].astype(bf16)
        return carry

    lax.fori_loop(0, tok // 32, stage, 0)
    rows.first()
    for copy in fetch:
        copy.start()
    small.first()
    rows.second()
    rows.third()
    for copy in fetch[:6]:
        copy.wait()
    key_t[...] = rot[heads].astype(f32).T.astype(bf16)
    lse_t[...] = lse[...].T
    small.second()
    rows.last()
    result.first(sends, chunks)

    order = []
    for k in range(zn):
        for d in (zn - 1 - k, k):
            if d not in order:
                order.append(d)

    def output_grad(d):
        cols = pl.ds(d * 2 * own_rows, 2 * own_rows)
        rhs = big[:, :, cols].reshape(length, 2 * own_rows)

        def body(i, carry):
            m = pl.ds(pl.multiple_of(i * 256, 256), 256)
            go[d, m, :] = tn_dot(ctx[:, m], rhs).astype(bf16)
            return carry

        lax.fori_loop(0, half // 256, body, 0)

    made = 0
    for k in range(1):
        while made < len(order) and not {zn - 1 - k, k} <= set(order[:made]):
            output_grad(order[made])
            made += 1
        o.step(k)

    def context_back(i, carry):
        at = pl.ds(pl.multiple_of(i * 2 * tok, 2 * tok), 2 * tok)
        lhs = big[pl.ds(2 * i, 2)].reshape(2 * tok, width)
        got = nn_dot(lhs, wo[...].reshape(width, half))
        cback[at, :] = got.astype(bf16)
        prod = got.astype(bf16).astype(f32) * ctx[at, :].astype(f32)
        for h in range(heads):
            s = jnp.sum(prod[:, h * HD : (h + 1) * HD], axis=1, keepdims=True)
            lse[at, h : h + 1] = s
        return carry

    lax.fori_loop(0, PLANE // 2, context_back, 0)
    while made < len(order):
        output_grad(order[made])
        made += 1
    del_t[...] = lse[...].T
    row_sends.finish()
    fill = pltpu.make_async_copy(seq_hbm, big, loads.at[len(pairs)])
    fill.start()
    small.third()
    dk[...] = jnp.zeros_like(dk)
    dv[...] = jnp.zeros_like(dv)
    dgain[...] = jnp.zeros_like(dgain)
    for copy in fetch[6:]:
        copy.wait()

    def norm_of(d, at, h, gain_row):
        d = d * tab[0, at, :] - turned(d) * tab[1, at, :]
        v = pre[at, pl.ds(h * HD if isinstance(h, int) else pl.multiple_of(h * HD, HD), HD)]
        r = rms_scale(v)
        hat = v * r
        s = d * hg_ref[pl.ds(gain_row, 1), :]
        got = r * (s - hat * jnp.mean(s * hat, axis=1, keepdims=True))
        dgain[pl.ds(gain_row, 1), :] += jnp.sum(d * hat, axis=0, keepdims=True)
        return got.astype(bf16)

    def attend(i):
        limit = key_limit(i, length)
        at = slice(i * QBLOCK, (i + 1) * QBLOCK)

        def body(h, carry):
            cols = pl.ds(pl.multiple_of(h * HD, HD), HD)
            query = rot[h, at, :]
            dctx = cback[at, cols]
            scores = nt_dot(rot[heads, :limit, :], query) * scale
            scores = scores + bias[:limit, at].astype(f32)
            probs = jnp.exp(scores - lse_t[pl.ds(h, 1), at])
            dprobs = nt_dot(val[:limit, :], dctx)
            dscores = (probs * (dprobs - del_t[pl.ds(h, 1), at])).astype(bf16)
            dv[:limit, :] += nn_dot(probs.astype(bf16), dctx)
            dk[:limit, :] += nn_dot(dscores, query)
            dq = nn_dot(key_t[:, :limit], dscores).T * scale
            aback[at, cols] = norm_of(dq, at, h, 0)
            return carry

        lax.fori_loop(0, heads, body, 0)

    blocks = length // QBLOCK
    hop = 1
    for i in range(blocks):
        attend(i)
        if i % 2 == 1 and hop < zn - 1:
            o.step(hop)
            hop += 1
        if i == 2:
            result.mix(0)
    while hop < zn - 1:
        o.step(hop)
        hop += 1

    def keys(i, carry):
        at = pl.ds(pl.multiple_of(i * 256, 256), 256)
        aback[at, half : half + HD] = norm_of(dk[at, :] * scale, at, heads, 1)
        aback[at, half + HD : half + 2 * HD] = dv[at, :].astype(bf16)
        return carry

    lax.fori_loop(0, length // 256, keys, 0)
    fill.wait()

    def query_grad(d):
        for h in range(2):
            cols = pl.ds((2 * d + h) * own_rows, own_rows) if own_rows % 128 == 0 else None
            if cols is None:
                lhs = big[:, :, pl.ds(2 * d * own_rows, 2 * own_rows)]
                lhs = lhs.reshape(length, 2 * own_rows)
                if h == 0:
                    gq[d] = tn_dot(lhs, aback[...]).astype(bf16)
            else:
                lhs = big[:, :, cols].reshape(length, own_rows)
                gq[d, h * own_rows : (h + 1) * own_rows, :] = tn_dot(lhs, aback[...]).astype(bf16)

    made = 0
    for k in range(zn - 1):
        while made < len(order) and not {zn - 1 - k, k} <= set(order[:made]):
            query_grad(order[made])
            made += 1
        if k == 0:
            q.step(0)
    while made < len(order):
        query_grad(order[made])
        made += 1

    red = PlaneReduce(place, sends, big, grad_ref, (c1, s1, ra, rb, last), hs, hr)

    def norm1_part(k):
        y, x, j = red._chip(*red.chips[k])
        lhs = aback[pl.ds(pl.multiple_of(j * 2 * tok, 2 * tok), 2 * tok), :]

        def body(i, carry):
            cols = pl.ds(pl.multiple_of(i * chunk, chunk), chunk)
            e = i * (chunk // own_rows)
            rhs = wq[pl.ds(e, chunk // own_rows)].reshape(chunk, half + 2 * HD)
            big[pl.ds(j * 2, 2), :, cols] = nt_dot(lhs, rhs).astype(bf16).reshape(2, tok, chunk)
            return carry

        lax.fori_loop(0, width // chunk, body, 0)

    for k in range(4):
        norm1_part(k)
        red.first(k)
    if zn > 2:
        q.step(1)
    for k in range(4):
        red.second(k)
    red.third()
    result.mix(1)
    for k in range(2, zn - 1):
        q.step(k)
    result.mix(2)
    red.finish()

    def tokens_back(i, carry):
        at = pl.ds(pl.multiple_of(i * 16, 16), 16)
        v = tok_ref[at, :].astype(f32)
        r = rms_scale(v)
        hat = v * r
        d = grad_ref[at, :]
        s = d * gain_ref[...]
        got = r * (s - hat * jnp.mean(s * hat, axis=1, keepdims=True))
        grad_ref[at, :] = mid_ref[at, :] + got
        return carry + jnp.sum(d * hat, axis=0, keepdims=True)

    total = lax.fori_loop(0, tok // 16, tokens_back, jnp.zeros((1, width), f32))
    tiny.vec[:, :width] = total
    tiny.vec[:, width : width + HD] = dgain[0:1, :]
    tiny.vec[:, width + HD : width + 2 * HD] = dgain[1:2, :]
    tiny.first()
    for c in range(3, chunks):
        result.mix(c)

    def split_o(at, v):
        first, second = v[:, :own_rows], v[:, own_rows:]
        low = pc.y == 0
        vo[at, :] = jnp.where(low, second, first).astype(bf16)
        oo_ref[pc.y, at, :] = jnp.where(low, first, second)

    o.own(split_o)
    sends.start(vo, to, ps.at[1], pr.at[1], pc.peer(dy=1))
    tiny.second()
    q_own(q, pc, zn, gq, bq, vq, oq_ref, own_rows)
    sends.start(vq, tq, ps.at[0], pr.at[0], pc.peer(dy=1))
    tiny.last()
    small.last()
    result.last(chunks)
    arrived(to, pr.at[1])
    oo_ref[1 - pc.y] = to[...].astype(f32)
    arrived(tq, pr.at[0])
    oq_ref[1 - pc.y] = tq[...].astype(f32)
    sends.finish()


def q_own(q, pc, zn, part, buf, give, out, rows, step=32):
    lower, upper = pc.z > 0, pc.z < zn - 1
    arrived(buf.at[pc.z + 1], q.rs_r.at[pc.z], lower)
    arrived(buf.at[pc.z], q.rs_l.at[pc.z], upper)

    def total(at):
        v = part[pc.z, at, :].astype(f32)
        v = v + jnp.where(lower, buf[pc.z + 1, at, :].astype(f32), 0.0)
        return v + jnp.where(upper, buf[pc.z, at, :].astype(f32), 0.0)

    def body(i, carry):
        at = pl.ds(pl.multiple_of(i * step, step), step)
        theirs = pl.ds(pl.multiple_of((1 - pc.y) * rows + i * step, step), step)
        mine = pl.ds(pl.multiple_of(pc.y * rows + i * step, step), step)
        give[at, :] = total(theirs).astype(bf16)
        out[pc.y, at, :] = total(mine)
        return carry

    lax.fori_loop(0, rows // step, body, 0)


def rear(
    zn, heads, middle, tokens, gain, gains, flat, comb, res, seq, full_q, full_o, pre, rot, val, lse,
    ctx, tables, bias, chunk=512,
):
    tok, width = tokens.shape
    length = PLANE * tok
    e, own_rows, wide = full_q.shape
    half = heads * HD
    chunks = width // chunk
    slots = res.shape[1]
    lanes = width + 2 * HD
    shape = jax.ShapeDtypeStruct
    vmem = pltpu.VMEM
    return pl.pallas_call(
        functools.partial(rear_kernel, zn, chunk, heads),
        out_shape=(
            shape((tok, width), f32),
            shape((2, own_rows, wide), f32),
            shape((2, half, own_rows), f32),
            shape(flat.shape, f32),
            shape((1, lanes), f32),
            shape((zn, tok, width), bf16),
            shape((PLANE, slots, width), bf16),
        ),
        in_specs=[VSPEC] * 6 + [ASPEC] * 11,
        out_specs=(VSPEC,) * 5 + (ASPEC,) * 2,
        scratch_shapes=[
            vmem((PLANE, tok, width), bf16),
            vmem((e, own_rows, wide), bf16),
            vmem((e, own_rows, half), bf16),
            vmem((length, wide), f32),
            vmem((heads + 1, length, HD), bf16),
            vmem((length, HD), bf16),
            vmem((length, 128), f32),
            vmem((length, half), bf16),
            vmem((2, length, HD), f32),
            vmem((length, length), bf16),
            vmem((128, length), f32),
            vmem((128, length), f32),
            vmem((HD, length), bf16),
            vmem((length, half), bf16),
            vmem((length, wide), bf16),
            vmem((length, HD), f32),
            vmem((length, HD), f32),
            vmem((8, HD), f32),
            vmem((zn, 2 * own_rows, wide), bf16),
            vmem((zn + 1, 2 * own_rows, wide), bf16),
            vmem((own_rows, wide), bf16),
            vmem((own_rows, wide), bf16),
            vmem((zn, half, 2 * own_rows), bf16),
            vmem((zn + 1, half, 2 * own_rows), bf16),
            vmem((half, own_rows), bf16),
            vmem((half, own_rows), bf16),
        ]
        + PlaneReduce.scratch(tok, width)
        + [
            vmem((PLANE, slots, chunk), bf16),
            vmem((2, zn, tok, chunk), bf16),
            dma_sems(8),
            dma_sems(8),
            dma_sems(10),
            dma_sems(10),
            dma_sems(2, zn),
            dma_sems(2, zn),
            dma_sems(2, zn),
            dma_sems(2, zn),
            dma_sems(2),
            dma_sems(2),
            dma_sems(chunks, PLANE),
            dma_sems(chunks, PLANE),
            dma_sems(chunks, zn),
            dma_sems(chunks, zn),
            dma_sems(PLANE),
            dma_sems(chunks),
            dma_sems(10),
        ]
        + SmallSum.scratch(zn, flat.shape[1], flat.shape[2])
        + TinySum.scratch(zn, lanes),
        compiler_params=params(5),
        name="rear",
    )(
        middle, tokens, gain, gains, flat, comb, res, seq, full_q, full_o, pre, rot, val, lse, ctx,
        tables, bias,
    )


def local(
    tokens,
    out_grad,
    first_gain,
    second_gain,
    query_gain,
    key_gain,
    query_weight,
    key_weight,
    value_weight,
    output_weight,
    router_weight,
    gate_weight,
    up_weight,
    down_weight,
    expert_ids,
    router_order,
    image_starts,
):
    tok, width = tokens.shape
    zn = lax.axis_size("exp") // 2
    experts = PLANE * zn
    cap = (9 * tok * TOP + 8 * experts - 1) // (8 * experts)
    slots = zn * cap
    length = PLANE * tok
    own_rows = query_weight.shape[0]
    half = query_weight.shape[1] // 2
    heads = half // HD
    scale = HD ** (-0.5)
    exp_index = lax.axis_index("exp")
    starts = lax.dynamic_slice_in_dim(image_starts, exp_index // 2, 1, 0)[0]

    expert_axis = jnp.arange(experts, dtype=jnp.int32)
    member = jnp.any(expert_ids[:, :, None] == expert_axis[None, None, :], axis=1)
    order_here = router_order[0]
    earlier = (order_here[None, :] < order_here[:, None]).astype(bf16)
    counts = jnp.dot(earlier, member.astype(bf16), preferred_element_type=f32)
    keep = member & (counts < cap)
    slot_of = jnp.where(keep, counts, -1.0)

    resid_in = tokens.astype(f32)
    first_rms = rms_scale(resid_in)
    first_hat = resid_in * first_rms
    first_norm = (first_hat * first_gain).astype(bf16)
    q_halves = query_weight.reshape(own_rows, 2, half).transpose(1, 0, 2)
    kv = jnp.concatenate([key_weight, value_weight], axis=1)
    pack_q = jnp.concatenate([q_halves, jnp.broadcast_to(kv[None], (2,) + kv.shape)], axis=2)
    pack_o = output_weight.reshape(2, half, own_rows).transpose(0, 2, 1)
    pos = jnp.arange(length, dtype=jnp.int32)
    cosine, sine = rotary_tables(pos, HD)
    tables = jnp.stack(
        [jnp.concatenate([cosine, cosine], axis=1), jnp.concatenate([-sine, sine], axis=1)]
    )
    pieces = piece_ids(pos, starts)
    mask = allowed_mask(pos, pos, pieces, pieces)
    bias = jnp.where(mask, 0.0, NEGATIVE).astype(bf16)
    slot_t = slot_of.T.reshape(zn, PLANE, tok)
    (
        seq_norm, full_q, full_o, pre, rot, value_rows, lse, context_rows, attention, rows_g, slots_all,
    ) = front(
        zn, cap, heads, tokens, first_gain[None], pack_q, pack_o, tables,
        jnp.stack([query_gain, key_gain]), bias, out_grad, slot_t,
    )
    resid_mid = resid_in + attention
    second_rms = rms_scale(resid_mid)
    second_hat = resid_mid * second_rms
    second_norm = (second_hat * second_gain).astype(bf16)
    logits = jnp.dot(second_norm, router_weight, preferred_element_type=f32)
    mix = jax.nn.softmax(jnp.where(member, logits, NEGATIVE), axis=-1)
    mix = jnp.where(member, mix, 0.0)
    keep_mix = jnp.where(keep, mix, 0.0)
    mix_t = keep_mix.T.reshape(zn, PLANE, tok)
    gate_w, up_w, down_w = gate_weight[0], up_weight[0], down_weight[0]
    rows_n, mids, dot_lanes, hot, comb = there(
        zn, cap, second_norm, slots_all, mix_t, rows_g, gate_w, up_w, down_w
    )
    dots_all, pairs, result, gate_grad, up_grad, down_grad = back_rows(
        zn, tok, dot_lanes, hot, mids, rows_n, rows_g, gate_w, up_w, down_w
    )
    pairs_sum = jnp.sum(pairs.astype(f32), axis=0)
    grad_out = out_grad.astype(f32)
    mix_dots = dots_all[:, :, :PLANE] + dots_all[:, :, PLANE : 2 * PLANE]
    mix_dots = mix_dots.transpose(1, 0, 2).reshape(tok, experts)
    chosen_grad = mix_dots - mix * jnp.sum(mix_dots, axis=1, keepdims=True)
    logit_grad = chosen_grad.astype(bf16)
    router_part = jnp.dot(second_norm.T, logit_grad, preferred_element_type=f32)
    norm2_back = pairs_sum + jnp.dot(logit_grad, router_weight.T, preferred_element_type=f32)
    mid_from_norm, second_gain_part = norm_back(norm2_back, second_hat, second_rms, second_gain)
    middle_grad = grad_out + mid_from_norm

    flat = jnp.concatenate([router_part.reshape(-1), second_gain_part])
    count = flat.shape[0]
    unit = PLANE * 8 * 128
    padded = -(-count // unit) * unit
    flat = jnp.pad(flat, (0, padded - count)).reshape(PLANE, padded // (PLANE * 128), 128)
    tokens_grad, sum_q, sum_o, flat, tiny, mixtures, _ = rear(
        zn, heads, middle_grad, tokens, first_gain[None], jnp.stack([query_gain, key_gain]), flat, comb,
        result, seq_norm, full_q, full_o, pre, rot, value_rows, lse,
        context_rows, tables, bias.T,
    )
    block_out = (resid_mid + jnp.sum(mixtures.astype(f32), axis=0)).astype(bf16)
    query_grad = jnp.concatenate([sum_q[0, :, :half], sum_q[1, :, :half]], axis=1)
    kv_grad = sum_q[0, :, half:] + sum_q[1, :, half:]
    key_grad, value_grad = kv_grad[:, :HD], kv_grad[:, HD:]
    output_grad = sum_o.reshape(2 * half, own_rows)
    flat = flat.reshape(-1)
    n_router = width * experts
    router_grad = flat[:n_router].reshape(width, experts)
    second_gain_grad = flat[n_router : n_router + width]
    tiny = tiny[0]
    first_gain_grad = tiny[:width]
    query_gain_grad = tiny[width : width + HD]
    key_gain_grad = tiny[width + HD :]
    return (
        block_out,
        tokens_grad,
        first_gain_grad,
        second_gain_grad,
        query_gain_grad,
        key_gain_grad,
        query_grad,
        key_grad,
        value_grad,
        output_grad,
        router_grad,
        gate_grad[None],
        up_grad[None],
        down_grad[None],
    )


def solution(mesh):
    both = ("exp", "tp")
    in_specs = (
        P(both, None),
        P(both, None),
        P(),
        P(),
        P(),
        P(),
        P("exp", "tp"),
        P("exp", "tp"),
        P("exp", "tp"),
        P("tp", "exp"),
        P(),
        P(both, None, None),
        P(both, None, None),
        P(both, None, None),
        P(both, None),
        P(both, None),
        P(),
    )
    out_specs = (
        P(both, None),
        P(both, None),
        P(),
        P(),
        P(),
        P(),
        P("exp", "tp"),
        P("exp", "tp"),
        P("exp", "tp"),
        P("tp", "exp"),
        P(),
        P(both, None, None),
        P(both, None, None),
        P(both, None, None),
    )
    return jax.shard_map(local, mesh=mesh, in_specs=in_specs, out_specs=out_specs, check_vma=False)
```

```python
import functools

import jax
import jax.numpy as jnp
import numpy as np
from jax import lax
from jax.experimental import pallas as pl
from jax.experimental.pallas import tpu as pltpu
from jax.sharding import PartitionSpec as P

HD = 128
TOP = 8
IMG_LEN = 256
PLANE = 8

EPSILON = 1e-06
THETA = 1000000.0
NEGATIVE = -1e30

MESH = pl.DeviceIdType.MESH
f32 = jnp.float32
bf16 = jnp.bfloat16
VMEM_LIMIT = 60 << 20


def rms_scale(values):
    return lax.rsqrt(jnp.mean(values * values, axis=-1, keepdims=True) + EPSILON)


def rotary_tables(length):
    freqs = np.float32(THETA) ** (-(np.arange(HD // 2, dtype=np.float32) * np.float32(2.0 / HD)))
    angles = np.arange(length, dtype=np.float32)[:, None] * freqs.astype(np.float32)[None, :]
    cosine, sine = np.cos(angles.astype(np.float64)), np.sin(angles.astype(np.float64))
    first = np.concatenate([cosine, cosine], axis=1)
    second = np.concatenate([-sine, sine], axis=1)
    return np.stack([first, second]).astype(np.float32)


def norm_back(grad_norm, hat, rms, gain):
    scaled = grad_norm * gain
    inner_mean = jnp.mean(scaled * hat, axis=-1, keepdims=True)
    lead_axes = tuple(range(grad_norm.ndim - 1))
    return (rms * (scaled - hat * inner_mean), jnp.sum(grad_norm * hat, axis=lead_axes))


class Place:
    def __init__(self):
        self.e = lax.axis_index("exp")
        self.t = lax.axis_index("tp")
        self.z = self.e // 2
        self.y = self.e % 2
        self.x = self.t // 2
        self.c = self.t % 2
        self.p = self.y * 4 + self.t

    def at(self, z, p):
        return (z * 2 + p // 4, p % 4)

    def flip(self, dy=0, dx=0, dc=0):
        y = 1 - self.y if dy else self.y
        x = 1 - self.x if dx else self.x
        c = 1 - self.c if dc else self.c
        return y * 4 + x * 2 + c

    def peer(self, dy=0, dx=0, dc=0):
        return self.at(self.z, self.flip(dy, dx, dc))

    def by(self, k):
        return self.flip((k >> 2) & 1, (k >> 1) & 1, k & 1)


class Sends:
    def __init__(self):
        self.kept = []

    def start(self, src, dst, send_sem, recv_sem, device, when=None):
        def make():
            return pltpu.make_async_remote_copy(
                src_ref=src,
                dst_ref=dst,
                send_sem=send_sem,
                recv_sem=recv_sem,
                device_id=device,
                device_id_type=MESH,
            )

        def go():
            make().start()

        if when is None:
            go()
        else:
            pl.when(when)(go)
        self.kept.append((make, when))

    def finish(self):
        for make, when in self.kept:
            if when is None:
                make().wait_send()
            else:
                pl.when(when)(lambda make=make: make().wait_send())
        self.kept = []


def arrived(dst, recv_sem, when=None):
    def go():
        pltpu.make_async_copy(dst, dst, recv_sem).wait()

    if when is None:
        go()
    else:
        pl.when(when)(go)


def greet(place, zn, cross=False):
    bar = pltpu.get_barrier_semaphore()
    met = [place.at(place.z, place.by(k)) for k in range(1, PLANE)]
    for k in range(1, zn):
        z = (place.z + k) % zn
        met.append(place.at(z, place.p))
        if cross:
            met.append(place.at(z, place.flip(dy=1)))
    for device in met:
        pl.semaphore_signal(bar, inc=1, device_id=device, device_id_type=MESH)
    pl.semaphore_wait(bar, len(met))


class PlaneGather:
    sems = 8

    def __init__(self, place, sends, buf, ss, rs):
        self.place, self.sends, self.buf, self.ss, self.rs = place, sends, buf, ss, rs
        half = buf.shape[2] // 2
        self.cols_a = pl.ds(0, half)
        self.cols_b = pl.ds(half, half)

    def _send(self, block, which, device, cols=None):
        ref = self.buf.at[block] if cols is None else self.buf.at[block, :, cols]
        self.sends.start(ref, ref, self.ss.at[which], self.rs.at[which], device)

    def _wait(self, block, which, cols=None):
        ref = self.buf.at[block] if cols is None else self.buf.at[block, :, cols]
        arrived(ref, self.rs.at[which])

    def first(self):
        pc = self.place
        self._send(pc.p, 1, pc.peer(dx=1))
        self._send(pc.p, 2, pc.peer(dc=1))

    def along(self):
        self._send(self.place.p, 0, self.place.peer(dy=1))

    def second(self):
        pc = self.place
        px, py = pc.flip(dx=1), pc.flip(dy=1)
        self._wait(px, 1)
        self._send(px, 3, pc.peer(dy=1), self.cols_a)
        self._send(px, 4, pc.peer(dc=1))
        self._wait(py, 0)
        self._send(py, 5, pc.peer(dx=1), self.cols_b)
        self._send(py, 6, pc.peer(dc=1))

    def third(self):
        pc = self.place
        pd = pc.flip(dy=1, dx=1)
        self._wait(pd, 3, self.cols_a)
        self._wait(pd, 5, self.cols_b)
        self._send(pd, 7, pc.peer(dc=1))

    def last(self):
        pc = self.place
        self._wait(pc.flip(dc=1), 2)
        self._wait(pc.flip(dc=1, dx=1), 4)
        self._wait(pc.flip(dc=1, dy=1), 6)
        self._wait(pc.flip(dc=1, dy=1, dx=1), 7)


def add_rows(dst, first, second, rows, step=32, when=None):
    if when is not None:
        pl.when(when)(lambda: add_rows(dst, first, second, rows, step))
        return

    def body(i, carry):
        at = pl.ds(pl.multiple_of(i * step, step), step)
        dst(at, first(at).astype(f32) + second(at).astype(f32))
        return carry

    lax.fori_loop(0, rows // step, body, 0)


class PlaneReduce:
    @staticmethod
    def scratch(rows, width, windows=1):
        return [
            pltpu.VMEM((windows, 4, rows, width), bf16),
            pltpu.VMEM((windows, 4, rows, width), bf16),
            pltpu.VMEM((windows, 2, rows // 2, width), bf16),
            pltpu.VMEM((windows, 2, rows // 2, width), bf16),
            pltpu.VMEM((windows, 2, rows // 2, width), bf16),
        ]

    def __init__(self, place, sends, part, out, scratch, ss, rs, cols, slot=0, when=None):
        self.place, self.sends, self.part, self.out = place, sends, part, out
        self.c1, self.s1, self.ra, self.rb, self.late = (ref.at[slot] for ref in scratch)
        self.ss, self.rs = ss.at[slot], rs.at[slot]
        self.cols, self.when = cols, when
        self.rows = part.shape[1]
        self.half = self.rows // 2
        self.chips = [(1, 1), (0, 1), (1, 0), (0, 0)]

    def chip(self, dy, dx):
        pc = self.place
        y = 1 - pc.y if dy else pc.y
        x = 1 - pc.x if dx else pc.x
        return y, x, y * 2 + x

    def _send(self, src, dst, i, device):
        self.sends.start(src, dst, self.ss.at[i], self.rs.at[i], device, self.when)

    def _take(self, dst, i):
        arrived(dst, self.rs.at[i], self.when)

    def _add(self, dst, first, second, rows):
        add_rows(dst, first, second, rows, when=self.when)

    def first(self, k):
        pc = self.place
        y, x, j = self.chip(*self.chips[k])
        block = y * 4 + x * 2 + (1 - pc.c)
        self._send(self.part.at[block, :, self.cols], self.c1.at[j], k, pc.peer(dc=1))

    def second(self, k):
        pc = self.place
        dy, dx = self.chips[k]
        y, x, j = self.chip(dy, dx)
        self._take(self.c1.at[j], k)
        mine = y * 4 + x * 2 + pc.c

        def put(at, v):
            self.s1[j, at, :] = v.astype(bf16)

        self._add(
            put, lambda at: self.part[mine, at, self.cols], lambda at: self.c1[j, at, :], self.rows
        )
        if dx:
            self._send(
                self.s1.at[j, pl.ds(0, self.half), :],
                self.ra.at[y],
                4 + (0 if dy else 1),
                pc.peer(dx=1),
            )
        if dy:
            self._send(
                self.s1.at[j, pl.ds(self.half, self.half), :],
                self.rb.at[x],
                6 + (0 if dx else 1),
                pc.peer(dy=1),
            )

    def third(self):
        pc = self.place
        for buf, slot, base, sem, other, out_sem in (
            (self.ra, 1 - pc.y, 0, 4, pc.peer(dy=1), 8),
            (self.rb, 1 - pc.x, self.half, 6, pc.peer(dx=1), 9),
        ):
            self._take(buf.at[slot], sem)
            j = (1 - pc.y) * 2 + pc.x if base == 0 else pc.y * 2 + 1 - pc.x

            def put(at, v, buf=buf, slot=slot):
                buf[slot, at, :] = v.astype(bf16)

            self._add(
                put,
                lambda at, j=j, base=base: self.s1[j, pl.ds(at.start + base, at.size), :],
                lambda at, buf=buf, slot=slot: buf[slot, at, :],
                self.half,
            )
            self._send(buf.at[slot], self.late.at[out_sem - 8], out_sem, other)

    def finish(self):
        pc = self.place
        own = pc.y * 2 + pc.x
        for i, (buf, slot, base, sem) in enumerate(
            ((self.ra, pc.y, 0, 5), (self.rb, pc.x, self.half, 7))
        ):
            self._take(buf.at[slot], sem)
            self._take(self.late.at[i], 8 + i)

            def put(at, v, buf=buf, slot=slot, base=base):
                to = pl.ds(at.start + base, at.size)
                self.out[to, self.cols] = v + buf[slot, at, :].astype(f32)

            self._add(
                put,
                lambda at, base=base: self.s1[own, pl.ds(at.start + base, at.size), :],
                lambda at, i=i: self.late[i, at, :],
                self.half,
            )


class ColumnGather:
    def __init__(self, place, sends, zn, pack, full, pair_ss, pair_rs, ss_r, ss_l, rs):
        self.place, self.sends, self.zn = place, sends, zn
        self.pack, self.full = pack, full
        self.pair_ss, self.pair_rs, self.ss_r, self.ss_l, self.rs = pair_ss, pair_rs, ss_r, ss_l, rs

    def _on(self, src, piece, right, left):
        pc = self.place
        if right is not None:
            self.sends.start(
                src,
                self.full.at[piece],
                self.ss_r.at[piece],
                self.rs.at[piece],
                pc.at(jnp.minimum(pc.z + 1, self.zn - 1), pc.p),
                right,
            )
        if left is not None:
            self.sends.start(
                src,
                self.full.at[piece],
                self.ss_l.at[piece],
                self.rs.at[piece],
                pc.at(jnp.maximum(pc.z - 1, 0), pc.p),
                left,
            )

    def pair(self):
        pc = self.place
        self.sends.start(
            self.pack.at[1 - pc.y],
            self.full.at[pc.e],
            self.pair_ss,
            self.pair_rs,
            pc.peer(dy=1),
        )

    def own(self):
        pc = self.place
        self._on(self.pack.at[pc.y], pc.e, pc.z < self.zn - 1, pc.z > 0)

    def keep(self):
        pc = self.place
        self.full[pc.e] = self.pack[pc.y]

    def partner(self):
        pc = self.place
        other = pc.z * 2 + 1 - pc.y
        arrived(self.full.at[other], self.pair_rs)
        self._on(self.full.at[other], other, pc.z < self.zn - 1, pc.z > 0)

    def step(self, k):
        pc = self.place
        for first in (True, False):
            y = pc.y if first else 1 - pc.y
            below = jnp.maximum(pc.z - k, 0) * 2 + y
            has = pc.z - k >= 0
            arrived(self.full.at[below], self.rs.at[below], has)
            self._on(
                self.full.at[below], below, jnp.logical_and(has, pc.z < self.zn - 1), None
            )
            above = jnp.minimum(pc.z + k, self.zn - 1) * 2 + y
            has = pc.z + k < self.zn
            arrived(self.full.at[above], self.rs.at[above], has)
            self._on(self.full.at[above], above, None, jnp.logical_and(has, pc.z > 0))


def dma_sems(*shape):
    return pltpu.SemaphoreType.DMA(shape)


VSPEC = pl.BlockSpec(memory_space=pltpu.VMEM)
ASPEC = pl.BlockSpec(memory_space=pl.ANY)
SSPEC = pl.BlockSpec(memory_space=pltpu.SMEM)


def params(cid):
    return pltpu.CompilerParams(
        collective_id=cid, has_side_effects=True, vmem_limit_bytes=VMEM_LIMIT
    )


class RowPush:
    def __init__(self, place, sends, zn, src, buf, chunk, ss, rs):
        self.place, self.sends, self.zn = place, sends, zn
        self.src, self.buf, self.chunk = src, buf, chunk
        self.ss, self.rs = ss, rs

    def own(self, c):
        pc = self.place
        cols = pl.ds(c * self.chunk, self.chunk)
        for k in range(1, self.zn):
            self.sends.start(
                self.src.at[:, cols],
                self.buf.at[pc.z, :, cols],
                self.ss.at[c, k],
                self.rs.at[c, pc.z],
                pc.at((pc.z + k) % self.zn, pc.p),
            )

    def keep(self):
        self.buf[self.place.z] = self.src[...]

    def take(self, c):
        pc = self.place
        for k in range(1, self.zn):
            d = (pc.z + k) % self.zn
            arrived(self.buf.at[d, :, pl.ds(c * self.chunk, self.chunk)], self.rs.at[c, d])


def turned(values):
    return pltpu.roll(values, HD // 2, 1)


def nt_dot(a, b):
    return lax.dot_general(a, b, (((1,), (1,)), ((), ())), preferred_element_type=f32)


def tn_dot(a, b):
    return lax.dot_general(a, b, (((0,), (0,)), ((), ())), preferred_element_type=f32)


def nn_dot(a, b):
    return jnp.dot(a, b, preferred_element_type=f32)


QBLOCK = 256


def key_limit(i, length):
    return min(length, (i + 1) * QBLOCK + IMG_LEN)


def bias_block(starts, at, length, turn):
    limit = length
    shape = (limit, QBLOCK) if turn else (QBLOCK, limit)
    query = lax.broadcasted_iota(jnp.int32, shape, 1 if turn else 0) + at
    key = lax.broadcasted_iota(jnp.int32, shape, 0 if turn else 1)
    allowed = key <= query
    for start in starts:
        low = (query >= start) & (query < start + IMG_LEN)
        allowed = allowed | (low & (key >= start) & (key < start + IMG_LEN))
    return jnp.where(allowed, 0.0, NEGATIVE)


def send_slots(place, sends, zn, src, dst, ss, rs):
    for k in range(1, zn):
        d = (place.z + k) % zn
        sends.start(src.at[d], dst.at[place.z], ss.at[k], rs.at[place.z], place.at(d, place.p))


def take_slots(place, zn, src, dst, rs):
    dst[place.z] = src[place.z]
    for k in range(1, zn):
        d = (place.z + k) % zn
        arrived(dst.at[d], rs.at[d])


def make_hot(zn, cap, tok, slots_ref, hot):
    row = lax.broadcasted_iota(jnp.int32, (zn * cap, tok), 0).astype(f32)

    def body(p, carry):
        for z in range(zn):
            have = slots_ref[z, pl.ds(p, 1), :]
            want = jnp.where(have < 0, -1.0, have + float(z * cap))
            hot[p, :, pl.ds(z * tok, tok)] = jnp.where(row == want, 1.0, 0.0).astype(bf16)
        return carry

    lax.fori_loop(0, PLANE, body, 0)


class PlaneSend:
    def __init__(self, place, sends, hot, rows, buf, out, chunk, ss, rs):
        self.place, self.sends = place, sends
        self.hot, self.rows, self.buf, self.out, self.chunk = hot, rows, buf, out, chunk
        self.ss, self.rs = ss, rs

    def send(self, c):
        pc = self.place
        cols = pl.ds(c * self.chunk, self.chunk)
        zn, tok, _ = self.rows.shape
        for k in (1, 2, 3, 4, 5, 6, 7, 0):
            p = pc.by(k) if k else pc.p
            got = nn_dot(self.hot[p], self.rows[:, :, cols].reshape(zn * tok, self.chunk))
            self.buf[p, :, cols] = got.astype(bf16)
            if k:
                self.sends.start(
                    self.buf.at[p, :, cols],
                    self.out.at[pc.p, :, cols],
                    self.ss.at[c, k],
                    self.rs.at[c, k],
                    pc.at(pc.z, p),
                )
            else:
                self._own(c).start()

    def _own(self, c):
        p = self.place.p
        cols = pl.ds(c * self.chunk, self.chunk)
        return pltpu.make_async_copy(self.buf.at[p, :, cols], self.out.at[p, :, cols], self.rs.at[c, 0])

    def take(self, c):
        cols = pl.ds(c * self.chunk, self.chunk)
        self._own(c).wait()
        for k in range(1, PLANE):
            arrived(self.out.at[self.place.by(k), :, cols], self.rs.at[c, k])


def front_kernel(
    zn, cap, chunk, heads, starts_ref,
    tok_ref, gain_ref, q_ref, k_ref, v_ref, o_ref, hg_ref, grad_ref, slot_ref, tab_hbm,
    lse_ref, att_ref, so_ref, seq_hbm, wq_hbm, wo_hbm, pre_hbm, rot_hbm, val_hbm, ctx_hbm, ag_hbm,
    seq, wq, wo, pre, rot, val, ctx, tab, bias, pq, po,
    part, c1, s1, ra, rb, last, gb, sn, hot,
    gs, gr, ps, pr, sr, sl, rs, hs, hr, zs, zr, ts, tr, xs, xr, out_sems,
):
    place, sends = Place(), Sends()
    pc = place
    tok, width = tok_ref.shape
    length = PLANE * tok
    own_rows = pq.shape[1]
    half = heads * HD
    chunks = width // chunk
    scale = HD ** (-0.5)
    table = pltpu.make_async_copy(tab_hbm, tab, out_sems.at[7])
    table.start()
    for y in range(2):
        pq[y, :, :half] = q_ref[:, y * half : (y + 1) * half]
        pq[y, :, half : half + HD] = k_ref[...]
        pq[y, :, half + HD :] = v_ref[...]
    greet(place, zn)
    q = ColumnGather(place, sends, zn, pq, wq, ps.at[0], pr.at[0], sr.at[0], sl.at[0], rs.at[0])
    o = ColumnGather(place, sends, zn, po, wo, ps.at[1], pr.at[1], sr.at[1], sl.at[1], rs.at[1])
    g = RowPush(place, sends, zn, grad_ref, gb, chunk, zs, zr)
    q.pair()
    q.own()

    def first_norm(i, carry):
        at = pl.ds(pl.multiple_of(i * 32, 32), 32)
        v = tok_ref[at, :].astype(f32)
        seq[pc.p, at, :] = (v * rms_scale(v) * gain_ref[...]).astype(bf16)
        return carry

    lax.fori_loop(0, tok // 32, first_norm, 0)
    rows = PlaneGather(place, sends, seq, gs, gr)
    rows.first()
    q.keep()
    q.partner()
    rows.along()
    send_slots(place, sends, zn, slot_ref, so_ref, ts, tr)
    for y in range(2):
        po[y] = o_ref[y * half : (y + 1) * half, :].astype(f32).T.astype(bf16)
    o.keep()
    g.keep()
    rows.second()
    o.pair()
    take_slots(place, zn, slot_ref, so_ref, tr)
    make_hot(zn, cap, tok, so_ref, hot)
    rows.third()
    pre[...] = jnp.zeros_like(pre)

    def project(origin):
        cols = pl.ds(pl.multiple_of(origin * 2 * own_rows, 2 * own_rows), 2 * own_rows)
        weight = wq.at[pl.ds(2 * origin, 2)]

        def body(i, carry):
            at = pl.ds(pl.multiple_of(i * 2 * tok, 2 * tok), 2 * tok)
            lhs = seq[pl.ds(2 * i, 2), :, cols].reshape(2 * tok, 2 * own_rows)
            pre[at, :] += nn_dot(lhs, weight[...].reshape(2 * own_rows, half + 2 * HD))
            return carry

        lax.fori_loop(0, PLANE // 2, body, 0)

    def project_step(k):
        pl.when(pc.z - k >= 0)(lambda: project(jnp.maximum(pc.z - k, 0)))
        pl.when(pc.z + k < zn)(lambda: project(jnp.minimum(pc.z + k, zn - 1)))

    kept = []

    def keep(i, src, dst):
        copy = pltpu.make_async_copy(src, dst, out_sems.at[i])
        copy.start()
        kept.append(copy)

    for k in range(1, zn):
        q.step(k)
        if k == max(1, zn - 2):
            g.own(0)
        if k == 1:
            rows.last()
            keep(0, seq, seq_hbm)
            project(pc.z)
        project_step(k)
    g.own(1)
    keep(1, wq, wq_hbm)
    keep(2, pre, pre_hbm)
    table.wait()

    def turn(i, carry):
        at = pl.ds(pl.multiple_of(i * 128, 128), 128)
        cos, sin = tab[0, at, :], tab[1, at, :]
        for h in range(heads + 1):
            v = pre[at, h * HD : (h + 1) * HD]
            gain = hg_ref[pl.ds(0 if h < heads else 1, 1), :]
            v = v * rms_scale(v) * gain
            rot[h, at, :] = (v * cos + turned(v) * sin).astype(bf16)
        val[at, :] = pre[at, half + HD : half + 2 * HD].astype(bf16)
        return carry

    lax.fori_loop(0, length // 128, turn, 0)
    keep(3, rot, rot_hbm)
    keep(4, val, val_hbm)
    lane = lax.broadcasted_iota(jnp.int32, (QBLOCK, 128), 1)
    starts = [starts_ref[pc.z, j] for j in range(starts_ref.shape[1])]

    def attend(i):
        limit = key_limit(i, length)
        at = slice(i * QBLOCK, (i + 1) * QBLOCK)
        bias[:, :limit] = bias_block(starts, i * QBLOCK, limit, False)

        def body(h, carry):
            scores = nt_dot(rot[h, at, :], rot[heads, :limit, :]) * scale + bias[:, :limit]
            top = jnp.max(scores, axis=1, keepdims=True)
            expo = jnp.exp(scores - top)
            total = jnp.sum(expo, axis=1, keepdims=True)
            low = (expo * (1.0 / total)).astype(bf16)
            cols = pl.ds(pl.multiple_of(h * HD, HD), HD)
            ctx[at, cols] = nn_dot(low, val[:limit, :]).astype(bf16)
            lse_ref[at, :] = jnp.where(lane == h, top + jnp.log(total), lse_ref[at, :])
            return carry

        lax.fori_loop(0, heads, body, 0, unroll=2)

    lse_ref[...] = jnp.zeros_like(lse_ref)
    give = PlaneSend(place, sends, hot, gb, sn, ag_hbm, chunk, xs, xr)
    blocks = length // QBLOCK
    given = 0
    for i in range(blocks):
        attend(i)
        if given < chunks - 1:
            g.take(given)
            if given < chunks - 3:
                g.own(given + 2)
            if given == max(chunks - 3, 0):
                o.own()
                o.partner()
            give.send(given)
            given += 1
    keep(5, ctx, ctx_hbm)

    def output(origin):
        cols = pl.ds(pl.multiple_of(origin * 2 * own_rows, 2 * own_rows), 2 * own_rows)
        weight = wo.at[pl.ds(2 * origin, 2)]

        def body(i, carry):
            at = pl.ds(pl.multiple_of(i * 2 * tok, 2 * tok), 2 * tok)
            got = nt_dot(ctx[at, :], weight[...].reshape(2 * own_rows, half))
            part[pl.ds(2 * i, 2), :, cols] = got.astype(bf16).reshape(2, tok, 2 * own_rows)
            return carry

        lax.fori_loop(0, PLANE // 2, body, 0)

    def visit(origin, when):
        cols = pl.ds(pl.multiple_of(origin * 2 * own_rows, 2 * own_rows), 2 * own_rows)
        red = PlaneReduce(
            place, sends, part, att_ref, (c1, s1, ra, rb, last), hs, hr, cols, origin, when
        )
        if when is None:
            output(origin)
        else:
            pl.when(when)(lambda: output(origin))
        for j in range(4):
            red.first(j)
        visits.append(red)

    def push_on():
        for lag, stage in ((2, 2), (3, 3), (4, 4)):
            if len(visits) >= lag:
                step_on(visits[-lag], stage)

    def step_on(red, stage):
        if stage == 2:
            for j in range(4):
                red.second(j)
        elif stage == 3:
            red.third()
        else:
            red.finish()

    visits = []
    visit(pc.z, None)
    for k in range(1, zn):
        o.step(k)
        if k == max(1, zn - 2):
            g.own(chunks - 1)
        visit(jnp.maximum(pc.z - k, 0), pc.z - k >= 0)
        push_on()
        visit(jnp.minimum(pc.z + k, zn - 1), pc.z + k < zn)
        push_on()
    keep(6, wo, wo_hbm)
    step_on(visits[-1], 2)
    while given < chunks:
        g.take(given)
        give.send(given)
        given += 1
    step_on(visits[-2], 3)
    step_on(visits[-1], 3)
    for red in visits[-3:]:
        step_on(red, 4)
    for c in range(chunks):
        give.take(c)
    for copy in kept:
        copy.wait()
    sends.finish()


def front(
    zn, cap, heads, starts, tokens, gain, query, key, value, output, gains, grad, slot, tables, chunk=512
):
    tok, width = tokens.shape
    length = PLANE * tok
    own_rows = query.shape[0]
    e = 2 * zn
    slots = zn * cap
    chunks = width // chunk
    half = heads * HD
    wide = half + 2 * HD
    shape = jax.ShapeDtypeStruct
    vmem = pltpu.VMEM
    return pl.pallas_call(
        functools.partial(front_kernel, zn, cap, chunk, heads),
        out_shape=(
            shape((length, 128), f32),
            shape((tok, width), f32),
            shape(slot.shape, f32),
            shape((PLANE, tok, width), bf16),
            shape((e, own_rows, wide), bf16),
            shape((e, own_rows, half), bf16),
            shape((length, wide), f32),
            shape((heads + 1, length, HD), bf16),
            shape((length, HD), bf16),
            shape((length, half), bf16),
            shape((PLANE, slots, width), bf16),
        ),
        in_specs=[SSPEC] + [VSPEC] * 9 + [ASPEC],
        out_specs=(VSPEC,) * 3 + (ASPEC,) * 8,
        scratch_shapes=[
            vmem((PLANE, tok, width), bf16),
            vmem((e, own_rows, wide), bf16),
            vmem((e, own_rows, half), bf16),
            vmem((length, wide), f32),
            vmem((heads + 1, length, HD), bf16),
            vmem((length, HD), bf16),
            vmem((length, half), bf16),
            vmem((2, length, HD), f32),
            vmem((QBLOCK, length), f32),
            vmem((2, own_rows, wide), bf16),
            vmem((2, own_rows, half), bf16),
            vmem((PLANE, tok, width), bf16),
        ]
        + PlaneReduce.scratch(tok, 2 * own_rows, zn)
        + [
            vmem((zn, tok, width), bf16),
            vmem((PLANE, slots, width), bf16),
            vmem((PLANE, slots, zn * tok), bf16),
            dma_sems(8),
            dma_sems(8),
            dma_sems(2),
            dma_sems(2),
            dma_sems(2, e),
            dma_sems(2, e),
            dma_sems(2, e),
            dma_sems(zn, 10),
            dma_sems(zn, 10),
            dma_sems(chunks, zn),
            dma_sems(chunks, zn),
            dma_sems(zn),
            dma_sems(zn),
            dma_sems(chunks, PLANE),
            dma_sems(chunks, PLANE),
            dma_sems(8),
        ],
        compiler_params=params(0),
        name="front",
    )(starts, tokens, gain, query, key, value, output, gains, grad, slot, tables)


class Flow:
    def __init__(self, stage, sems):
        self.stage, self.sems = stage, sems
        self.count = 0
        self.flight = [None, None]

    def slot(self):
        i = self.count % 2
        if self.flight[i] is not None:
            self.flight[i].wait()
            self.flight[i] = None
        return i

    def send(self, dst):
        i = self.count % 2
        copy = pltpu.make_async_copy(self.stage.at[i], dst, self.sems.at[i])
        copy.start()
        self.flight[i] = copy
        self.count += 1

    def finish(self):
        for i in range(2):
            if self.flight[i] is not None:
                self.flight[i].wait()
                self.flight[i] = None


def there_kernel(
    zn, cap, chunk, norm_ref, slots_ref, mix_ref, ag_hbm, gate_hbm, up_hbm, down_hbm,
    dot_ref, an_hbm, mid_hbm, hot_t_hbm, comb_hbm,
    an_ref, mid_ref, nb, sn, hot, mo, mrow, mr, wg, wu, wd, ag, gate, up, unmixed, stage, loads, flows, keeps,
    zs, zr, ts, tr, xs, xr, ys, yr,
):
    place, sends = Place(), Sends()
    pc = place
    greet(place, zn)
    tok, width = norm_ref.shape
    slots = zn * cap
    rows = PLANE * slots
    chunks = width // chunk
    hidden = wd.shape[0]
    fetch = [
        pltpu.make_async_copy(src, dst, loads.at[i])
        for i, (src, dst) in enumerate(((down_hbm, wd), (gate_hbm, wg), (up_hbm, wu)))
    ]
    parts = [
        pltpu.make_async_copy(
            ag_hbm.at[:, :, pl.ds(c * chunk, chunk)], ag.at[c % 2], loads.at[3 + c % 2]
        )
        for c in range(chunks)
    ]
    n = RowPush(place, sends, zn, norm_ref, nb, chunk, zs, zr)
    n.own(0)
    send_slots(place, sends, zn, mix_ref, mo, ts, tr)
    fetch[0].start()
    parts[0].start()
    if chunks > 1:
        parts[1].start()
    fetch[1].start()
    fetch[2].start()
    n.keep()
    make_hot(zn, cap, tok, slots_ref, hot)
    take_slots(place, zn, mix_ref, mo, tr)

    def mixes(p, carry):
        row = jnp.concatenate([mo[z, pl.ds(p, 1), :] for z in range(zn)], axis=1)
        high = row.astype(bf16)
        rest = row - high.astype(f32)
        middle = rest.astype(bf16)
        low = (rest - middle.astype(f32)).astype(bf16)
        zero = jnp.zeros((13, zn * tok), bf16)
        got = nt_dot(jnp.concatenate([high, middle, low, zero], axis=0), hot[p])
        mrow[p] = jnp.sum(got, axis=0, keepdims=True)
        return carry

    lax.fori_loop(0, PLANE, mixes, 0)
    for k in range(1, PLANE):
        p = pc.by(k)
        sends.start(mrow.at[p], mr.at[pc.p], ys.at[k], yr.at[k], pc.at(pc.z, p))
    mr[pc.p] = mrow[pc.p]
    if chunks > 1:
        n.own(1)
    fetch[0].wait()
    give = PlaneSend(place, sends, hot, nb, sn, an_ref, chunk, xs, xr)
    half = PLANE // 2

    def back_through(c):
        cols = pl.ds(c * chunk, chunk)
        parts[c].wait()

        def body(i, carry):
            at = pl.ds(i * half, half)
            got = nt_dot(ag[c % 2, at].reshape(half * slots, chunk), wd[:, cols])
            got = got.reshape(half, slots, hidden)
            unmixed[at] = got if c == 0 else unmixed[at] + got
            return carry

        lax.fori_loop(0, 2, body, 0)
        if c + 2 < chunks:
            parts[c + 2].start()

    for c in range(chunks):
        n.take(c)
        if c + 2 < chunks:
            n.own(c + 2)
        give.send(c)
        back_through(c)

    lane = lax.broadcasted_iota(jnp.int32, (tok, rows), 1).astype(f32)

    def tables(z, carry):
        zero = jnp.zeros((120, tok), f32)
        have = jnp.concatenate([slots_ref[z], zero], axis=0).T
        mixed = jnp.concatenate([mo[z], zero], axis=0).T
        one = jnp.zeros((tok, rows), f32)
        mix = jnp.zeros((tok, rows), f32)
        base = (z * cap).astype(f32)
        for p in range(PLANE):
            col = have[:, p : p + 1]
            hit = lane == jnp.where(col < 0, -1.0, col + base + float(p * slots))
            one = jnp.where(hit, 1.0, one)
            mix = jnp.where(hit, mixed[:, p : p + 1], mix)
        stage[0] = one.astype(bf16)
        stage[1] = mix.astype(bf16)
        at = pl.ds(pl.multiple_of(z * tok, tok), tok)
        out = [
            pltpu.make_async_copy(stage.at[i], dst.at[at, :], flows.at[i])
            for i, dst in enumerate((hot_t_hbm, comb_hbm))
        ]
        for copy in out:
            copy.start()
        for copy in out:
            copy.wait()
        return carry

    lax.fori_loop(0, zn, tables, 0)
    fetch[1].wait()
    fetch[2].wait()
    saves = []
    for c in range(chunks):
        cols = pl.ds(c * chunk, chunk)
        give.take(c)
        save = pltpu.make_async_copy(an_ref.at[:, :, cols], an_hbm.at[:, :, cols], keeps.at[PLANE + c])
        save.start()
        saves.append(save)

        def into(i, carry):
            at = pl.ds(i * half, half)
            lhs = an_ref[at, :, cols].reshape(half * slots, chunk)
            for weight, acc in ((wg, gate), (wu, up)):
                got = nn_dot(lhs, weight[cols, :]).reshape(half, slots, hidden)
                acc[at] = got if c == 0 else acc[at] + got
            return carry

        lax.fori_loop(0, 2, into, 0)
    for k in range(1, PLANE):
        arrived(mr.at[pc.by(k)], yr.at[k])
    place_lane = lax.broadcasted_iota(jnp.int32, (slots, 128), 1)
    r = lax.broadcasted_iota(jnp.int32, (slots, slots), 0)
    s = lax.broadcasted_iota(jnp.int32, (slots, slots), 1)

    def acts(p, carry):
        mix = jnp.sum(jnp.where(r == s, mr[p], 0.0), axis=1, keepdims=True)
        g, u, d = gate[p], up[p], unmixed[p]
        sig = jax.nn.sigmoid(g)
        act = g * sig
        inner = (act * u).astype(bf16)
        mid_ref[0, p] = inner
        wide = inner.astype(f32)
        mid_ref[1, p] = (wide * mix).astype(bf16)
        dots = mix * jnp.sum(d * wide, axis=1, keepdims=True)
        high = dots.astype(bf16).astype(f32)
        dot = jnp.where(place_lane == pc.p, high, 0.0)
        dot = jnp.where(place_lane == pc.p + PLANE, dots - high, dot)
        dot_ref[p] = dot.astype(bf16)
        d = d * mix
        mid_ref[2, p] = (d * u * sig * (1.0 + g * (1.0 - sig))).astype(bf16)
        mid_ref[3, p] = (d * act).astype(bf16)
        pltpu.make_async_copy(mid_ref.at[:, p], mid_hbm.at[:, p], keeps.at[p]).start()
        return carry

    lax.fori_loop(0, PLANE, acts, 0)
    for p in range(PLANE):
        saves.append(pltpu.make_async_copy(mid_ref.at[:, p], mid_hbm.at[:, p], keeps.at[p]))
    for save in saves:
        save.wait()
    sends.finish()


def there(zn, cap, norm, slots_all, mix, ag, gate, up, down, chunk=512):
    tok, width = norm.shape
    slots = zn * cap
    hidden = down.shape[0]
    chunks = width // chunk
    shape = jax.ShapeDtypeStruct
    vmem = pltpu.VMEM
    return pl.pallas_call(
        functools.partial(there_kernel, zn, cap, chunk),
        out_shape=(
            shape((PLANE, slots, 128), bf16),
            shape((PLANE, slots, width), bf16),
            shape((4, PLANE, slots, hidden), bf16),
            shape((zn * tok, PLANE * slots), bf16),
            shape((zn * tok, PLANE * slots), bf16),
        ),
        in_specs=[VSPEC] * 3 + [ASPEC] * 4,
        out_specs=(VSPEC,) + (ASPEC,) * 4,
        scratch_shapes=[
            vmem((PLANE, slots, width), bf16),
            vmem((4, PLANE, slots, hidden), bf16),
            vmem((zn, tok, width), bf16),
            vmem((PLANE, slots, width), bf16),
            vmem((PLANE, slots, zn * tok), bf16),
            vmem(mix.shape, f32),
            vmem((PLANE, 1, slots), f32),
            vmem((PLANE, 1, slots), f32),
            vmem(gate.shape, bf16),
            vmem(up.shape, bf16),
            vmem(down.shape, bf16),
            vmem((2, PLANE, slots, chunk), bf16),
            vmem((PLANE, slots, hidden), f32),
            vmem((PLANE, slots, hidden), f32),
            vmem((PLANE, slots, hidden), f32),
            vmem((2, tok, PLANE * slots), bf16),
            dma_sems(5),
            dma_sems(2),
            dma_sems(PLANE + chunks),
            dma_sems(chunks, zn),
            dma_sems(chunks, zn),
            dma_sems(zn),
            dma_sems(zn),
            dma_sems(chunks, PLANE),
            dma_sems(chunks, PLANE),
            dma_sems(PLANE),
            dma_sems(PLANE),
        ],
        compiler_params=params(3),
        name="there",
    )(norm, slots_all, mix, ag, gate, up, down)


def back_kernel(
    zn, chunk, dot_ref, hot_ref, mid_hbm, an_hbm, ag_hbm, gate_hbm, up_hbm, down_hbm,
    dots_ref, ap_hbm, res_hbm, gg_hbm, ug_hbm, dg_hbm, rr_hbm,
    mids, an, ag, wg, wu, wd, pb, rp, rd, zd, zp, wide, tall, flat,
    loads, flows, xs, xr, ds, dr, zs, zr, es, er, os, vs, vr,
):
    place, sends = Place(), Sends()
    pc = place
    fetch = [
        pltpu.make_async_copy(src, dst, loads.at[i])
        for i, (src, dst) in enumerate(
            (
                (gate_hbm, wg), (up_hbm, wu), (mid_hbm.at[2], mids.at[2]), (mid_hbm.at[3], mids.at[3]),
                (mid_hbm.at[0], mids.at[0]), (down_hbm, wd), (mid_hbm.at[1], mids.at[1]), (ag_hbm, ag),
                (an_hbm, an),
            )
        )
    ]
    for copy in fetch:
        copy.start()
    greet(place, zn)
    _, slots, width = pb.shape
    hidden = wd.shape[0]
    chunks = width // chunk
    tok = dots_ref.shape[1]
    far = [(pc.z + k) % zn for k in range(1, zn)]
    half = PLANE // 2
    for k in range(1, PLANE):
        p = pc.by(k)
        sends.start(dot_ref.at[p], rd.at[pc.p], ds.at[k], dr.at[k], pc.at(pc.z, p))
    for copy in fetch[:4]:
        copy.wait()
    def pair_chunk(c):
        cols = pl.ds(c * chunk, chunk)

        def pair(i, carry):
            at = pl.ds(i * half, half)
            got = nt_dot(mids[2, at].reshape(half * slots, hidden), wg[cols, :])
            got = got + nt_dot(mids[3, at].reshape(half * slots, hidden), wu[cols, :])
            pb[at, :, cols] = got.astype(bf16).reshape(half, slots, chunk)
            return carry

        lax.fori_loop(0, 2, pair, 0)
        rp[pc.p, :, cols] = pb[pc.p, :, cols]

    def pair_send(c):
        cols = pl.ds(c * chunk, chunk)
        for k in range(1, PLANE):
            p = pc.by(k)
            sends.start(
                pb.at[p, :, cols], rp.at[pc.p, :, cols], xs.at[c, k], xr.at[c, k], pc.at(pc.z, p)
            )

    for c in range(chunks):
        pair_chunk(c)
        if c < 2:
            pair_send(c)
    rd[pc.p] = dot_ref[pc.p]
    for k in range(1, PLANE):
        arrived(rd.at[pc.by(k)], dr.at[k])
    zd[...] = nn_dot(hot_ref[...], rd[...].reshape(PLANE * slots, 128)).reshape(zn, tok, 128)
    for k, d in enumerate(far):
        sends.start(zd.at[d], dots_ref.at[pc.z], es.at[k], er.at[pc.z], pc.at(d, pc.p))
    dots_ref[pc.z] = zd[pc.z]

    flow_r, flow_g, flow_u, flow_d = (
        Flow(buf, flows.at[i]) for i, buf in enumerate((wide, tall.at[0], tall.at[1], flat))
    )
    keeps = []

    def result(c):
        cols = pl.ds(c * chunk, chunk)
        slot = flow_r.slot()

        def body(i, carry):
            at = pl.ds(i * half, half)
            got = nn_dot(mids[0, at].reshape(half * slots, hidden), wd[:, cols])
            wide[slot, at] = got.astype(bf16).reshape(half, slots, chunk)
            return carry

        lax.fori_loop(0, 2, body, 0)
        flow_r.send(res_hbm.at[:, :, cols])

    def down_grad(i):
        m = pl.ds(i * 128, 128)
        slot = flow_d.slot()
        lhs = mids[1, :, :, m].reshape(PLANE * slots, 128)

        def body(j, carry):
            cols = pl.ds(pl.multiple_of(j * chunk, chunk), chunk)
            flat[slot, :, cols] = tn_dot(lhs, ag[:, :, cols].reshape(PLANE * slots, chunk))
            return carry

        lax.fori_loop(0, chunks, body, 0)
        flow_d.send(dg_hbm.at[m, :])

    def gate_up_grad(i):
        m = pl.ds(i * 256, 256)
        lhs = an[:, :, m].reshape(PLANE * slots, 256)
        for which, flow, dst in ((0, flow_g, gg_hbm), (1, flow_u, ug_hbm)):
            slot = flow.slot()
            rhs = mids[2 + which].reshape(PLANE * slots, hidden)
            tall[which, slot] = tn_dot(lhs, rhs)
            flow.send(dst.at[m, :])

    def combine(c):
        cols = pl.ds(c * chunk, chunk)
        for k in range(1, PLANE):
            arrived(rp.at[pc.by(k), :, cols], xr.at[c, k])
        if c + 2 < chunks:
            pair_send(c + 2)
        if c == chunks - 1:
            flow_r.finish()
            for k in range(1, PLANE):
                p = pc.by(k)
                sends.start(
                    res_hbm.at[p, :, pl.ds(0, chunk)],
                    rr_hbm.at[pc.p],
                    vs.at[k],
                    vr.at[k],
                    pc.at(pc.z, p),
                )
        got = nn_dot(hot_ref[...], rp[:, :, cols].reshape(PLANE * slots, chunk))
        zp[:, :, cols] = got.astype(bf16).reshape(zn, tok, chunk)
        for k, d in enumerate(far):
            sends.start(
                zp.at[d, :, cols],
                ap_hbm.at[pc.z, :, cols],
                zs.at[c, k],
                zr.at[c, pc.z],
                pc.at(d, pc.p),
            )
        keep = pltpu.make_async_copy(zp.at[pc.z, :, cols], ap_hbm.at[pc.z, :, cols], os.at[c])
        keep.start()
        keeps.append(keep)

    for copy in fetch[4:6]:
        copy.wait()
    for c in range(chunks):
        result(c)
    for copy in fetch[6:]:
        copy.wait()
    work = [functools.partial(down_grad, i) for i in range(hidden // 128)]
    work += [functools.partial(gate_up_grad, i) for i in range(width // 256)]
    share = -(-len(work) // chunks)
    for c in range(chunks):
        for item in work[c * share : (c + 1) * share]:
            item()
        combine(c)
    for c in range(chunks):
        for d in far:
            arrived(ap_hbm.at[d, :, pl.ds(c * chunk, chunk)], zr.at[c, d])
    for keep in keeps:
        keep.wait()
    for k in range(1, PLANE):
        arrived(rr_hbm.at[pc.by(k)], vr.at[k])
    for d in far:
        arrived(dots_ref.at[d], er.at[d])
    for flow in (flow_r, flow_g, flow_u, flow_d):
        flow.finish()
    sends.finish()


def back_rows(zn, tok, dots, hot, mids, an, ag, gate, up, down, chunk=512):
    _, slots, width = an.shape
    hidden = down.shape[0]
    chunks = width // chunk
    shape = jax.ShapeDtypeStruct
    vmem = pltpu.VMEM
    return pl.pallas_call(
        functools.partial(back_kernel, zn, chunk),
        out_shape=(
            shape((zn, tok, 128), f32),
            shape((zn, tok, width), bf16),
            shape((PLANE, slots, width), bf16),
            shape(gate.shape, f32),
            shape(up.shape, f32),
            shape(down.shape, f32),
            shape((PLANE, slots, chunk), bf16),
        ),
        in_specs=[VSPEC] * 2 + [ASPEC] * 6,
        out_specs=(VSPEC,) + (ASPEC,) * 6,
        scratch_shapes=[
            vmem((4, PLANE, slots, hidden), bf16),
            vmem((PLANE, slots, width), bf16),
            vmem((PLANE, slots, width), bf16),
            vmem(gate.shape, bf16),
            vmem(up.shape, bf16),
            vmem(down.shape, bf16),
            vmem((PLANE, slots, width), bf16),
            vmem((PLANE, slots, width), bf16),
            vmem((PLANE, slots, 128), bf16),
            vmem((zn, tok, 128), f32),
            vmem((zn, tok, width), bf16),
            vmem((2, PLANE, slots, chunk), bf16),
            vmem((2, 2, 256, hidden), f32),
            vmem((2, 128, width), f32),
            dma_sems(9),
            dma_sems(4, 2),
            dma_sems(chunks, PLANE),
            dma_sems(chunks, PLANE),
            dma_sems(PLANE),
            dma_sems(PLANE),
            dma_sems(chunks, zn),
            dma_sems(chunks, zn),
            dma_sems(zn),
            dma_sems(zn),
            dma_sems(chunks),
            dma_sems(PLANE),
            dma_sems(PLANE),
        ],
        compiler_params=params(4),
        name="back_rows",
    )(dots, hot, mids, an, ag, gate, up, down)


class ColumnReduce:
    def __init__(self, place, sends, zn, part, buf, ss_r, ss_l, rs_r, rs_l):
        self.place, self.sends, self.zn = place, sends, zn
        self.part, self.buf = part, buf
        self.ss_r, self.ss_l, self.rs_r, self.rs_l = ss_r, ss_l, rs_r, rs_l

    def _hop(self, slot, rs, ss, d, start, inner, device):
        rows = self.part.shape[1]

        def add():
            arrived(self.buf.at[slot], rs.at[d])

            def put(at, v):
                self.buf[slot, at, :] = v.astype(bf16)

            add_rows(put, lambda at: self.part[d, at, :], lambda at: self.buf[slot, at, :], rows)

        both = jnp.logical_and(start, inner)
        pl.when(both)(add)
        self.sends.start(
            self.buf.at[slot], self.buf.at[slot], ss.at[d], rs.at[d], device, both
        )
        self.sends.start(
            self.part.at[d],
            self.buf.at[slot],
            ss.at[d],
            rs.at[d],
            device,
            jnp.logical_and(start, jnp.logical_not(inner)),
        )

    def step(self, k):
        pc, zn = self.place, self.zn
        d = zn - 1 - k
        right = pc.at(jnp.minimum(pc.z + 1, zn - 1), pc.p)
        left = pc.at(jnp.maximum(pc.z - 1, 0), pc.p)
        self._hop(d + 1, self.rs_r, self.ss_r, d, pc.z < d, pc.z > 0, right)
        d = k
        self._hop(d, self.rs_l, self.ss_l, d, pc.z > d, pc.z < zn - 1, left)

    def own(self, use, step=32):
        pc, zn = self.place, self.zn
        lower, upper = pc.z > 0, pc.z < zn - 1
        arrived(self.buf.at[pc.z + 1], self.rs_r.at[pc.z], lower)
        arrived(self.buf.at[pc.z], self.rs_l.at[pc.z], upper)

        def body(i, carry):
            at = pl.ds(pl.multiple_of(i * step, step), step)
            v = self.part[pc.z, at, :].astype(f32)
            v = v + jnp.where(lower, self.buf[pc.z + 1, at, :].astype(f32), 0.0)
            v = v + jnp.where(upper, self.buf[pc.z, at, :].astype(f32), 0.0)
            use(at, v)
            return carry

        lax.fori_loop(0, self.part.shape[1] // step, body, 0)


class SmallSum:
    @staticmethod
    def scratch(zn, rows, lanes):
        return [
            pltpu.VMEM((PLANE, rows, lanes), f32),
            pltpu.VMEM((rows, lanes), f32),
            pltpu.VMEM((zn, rows, lanes), f32),
            dma_sems(PLANE),
            dma_sems(PLANE),
            dma_sems(zn),
            dma_sems(zn),
            dma_sems(PLANE),
            dma_sems(PLANE),
        ]

    def __init__(self, place, sends, zn, flat, out, scratch):
        self.place, self.sends, self.zn, self.flat, self.out = place, sends, zn, flat, out
        self.l1, self.mid, self.l2, self.a, self.ar, self.b, self.br, self.c, self.cr = scratch

    def first(self):
        pc = self.place
        for k in range(1, PLANE):
            p = pc.by(k)
            self.sends.start(
                self.flat.at[p], self.l1.at[pc.p], self.a.at[k], self.ar.at[k], pc.at(pc.z, p)
            )
        self.l1[pc.p] = self.flat[pc.p]

    def second(self):
        pc, zn = self.place, self.zn
        for k in range(1, PLANE):
            arrived(self.l1.at[pc.by(k)], self.ar.at[k])
        total = self.l1[0]
        for k in range(1, PLANE):
            total = total + self.l1[k]
        self.mid[...] = total
        self.l2[pc.z] = total
        for k in range(1, zn):
            d = (pc.z + k) % zn
            self.sends.start(
                self.mid, self.l2.at[pc.z], self.b.at[k], self.br.at[pc.z], pc.at(d, pc.p)
            )

    def _column(self):
        pc, zn = self.place, self.zn
        for k in range(1, zn):
            d = (pc.z + k) % zn
            arrived(self.l2.at[d], self.br.at[d])
        total = self.l2[0]
        for z in range(1, zn):
            total = total + self.l2[z]
        return total

    def third(self):
        pc = self.place
        self.out[pc.p] = self._column()
        for k in range(1, PLANE):
            p = pc.by(k)
            self.sends.start(
                self.out.at[pc.p], self.out.at[pc.p], self.c.at[k], self.cr.at[k], pc.at(pc.z, p)
            )

    def last(self):
        pc = self.place
        for k in range(1, PLANE):
            arrived(self.out.at[pc.by(k)], self.cr.at[k])


class TinySum:
    @staticmethod
    def scratch(zn, lanes):
        return [
            pltpu.VMEM((1, lanes), f32),
            pltpu.VMEM((PLANE, 1, lanes), f32),
            pltpu.VMEM((1, lanes), f32),
            pltpu.VMEM((zn, 1, lanes), f32),
            dma_sems(PLANE),
            dma_sems(PLANE),
            dma_sems(zn),
            dma_sems(zn),
        ]

    def __init__(self, place, sends, zn, out, scratch):
        self.place, self.sends, self.zn, self.out = place, sends, zn, out
        self.vec, self.l1, self.mid, self.l2, self.a, self.ar, self.b, self.br = scratch

    def first(self):
        pc = self.place
        for k in range(1, PLANE):
            p = pc.by(k)
            self.sends.start(
                self.vec, self.l1.at[pc.p], self.a.at[k], self.ar.at[k], pc.at(pc.z, p)
            )
        self.l1[pc.p] = self.vec[...]

    def second(self):
        pc, zn = self.place, self.zn
        for k in range(1, PLANE):
            arrived(self.l1.at[pc.by(k)], self.ar.at[k])
        total = self.l1[0]
        for k in range(1, PLANE):
            total = total + self.l1[k]
        self.mid[...] = total
        self.l2[pc.z] = total
        for k in range(1, zn):
            d = (pc.z + k) % zn
            self.sends.start(
                self.mid, self.l2.at[pc.z], self.b.at[k], self.br.at[pc.z], pc.at(d, pc.p)
            )

    def last(self):
        pc, zn = self.place, self.zn
        for k in range(1, zn):
            d = (pc.z + k) % zn
            arrived(self.l2.at[d], self.br.at[d])
        total = self.l2[0]
        for z in range(1, zn):
            total = total + self.l2[z]
        self.out[...] = total


class Result:
    def __init__(self, place, sends, zn, res, first, comb, rr, am, rbuf, zbuf, chunk, xs, xr, zs, zr, ls, os):
        self.place, self.sends, self.zn, self.res, self.comb = place, sends, zn, res, comb
        self.rr, self.am, self.rbuf, self.zbuf, self.chunk = rr, am, rbuf, zbuf, chunk
        self.xs, self.xr, self.zs, self.zr, self.ls, self.os = xs, xr, zs, zr, ls, os
        self.early = first
        self.flight = {}

    def first(self, c):
        pc = self.place
        cols = pl.ds(c * self.chunk, self.chunk)
        for k in range(1, PLANE):
            p = pc.by(k)
            self.sends.start(
                self.res.at[p, :, cols],
                self.rr.at[pc.p, :, cols],
                self.xs.at[c, k],
                self.xr.at[c, k],
                pc.at(pc.z, p),
            )

    def mix(self, c, chunks):
        pc, zn = self.place, self.zn
        cols = pl.ds(c * self.chunk, self.chunk)
        own = pltpu.make_async_copy(self.res.at[pc.p, :, cols], self.rbuf.at[pc.p], self.ls.at[0])
        own.start()
        copies = []
        for k in range(1, PLANE):
            p = pc.by(k)
            if c:
                arrived(self.rr.at[p, :, cols], self.xr.at[c, k])
            src = self.rr.at[p, :, cols] if c else self.early.at[p]
            copy = pltpu.make_async_copy(src, self.rbuf.at[p], self.ls.at[k])
            copy.start()
            copies.append(copy)
        if c and c + 2 < chunks:
            self.first(c + 2)
        own.wait()
        for copy in copies:
            copy.wait()
        self.settle(c - 2)
        slot = c % 2
        _, slots, chunk = self.rbuf.shape
        tok = self.zbuf.shape[2]
        unit = min(512, zn * tok)
        per = unit // tok
        rows = self.rbuf[...].reshape(PLANE * slots, chunk)
        for i in range(zn * tok // unit):
            got = nn_dot(self.comb[i * unit : (i + 1) * unit, :], rows)
            self.zbuf[slot, i * per : (i + 1) * per] = got.astype(bf16).reshape(per, tok, chunk)
        flight = []
        for k in range(1, zn):
            d = (pc.z + k) % zn
            flight.append(
                pltpu.make_async_remote_copy(
                    src_ref=self.zbuf.at[slot, d],
                    dst_ref=self.am.at[pc.z, :, cols],
                    send_sem=self.zs.at[c, k],
                    recv_sem=self.zr.at[c, pc.z],
                    device_id=pc.at(d, pc.p),
                    device_id_type=MESH,
                )
            )
        for copy in flight:
            copy.start()
        keep = pltpu.make_async_copy(
            self.zbuf.at[slot, pc.z], self.am.at[pc.z, :, cols], self.os.at[c]
        )
        keep.start()
        self.flight[c] = (flight, keep)

    def settle(self, c):
        if c in self.flight:
            flight, keep = self.flight.pop(c)
            for copy in flight:
                copy.wait_send()
            keep.wait()

    def last(self, chunks):
        pc, zn = self.place, self.zn
        for c in range(chunks):
            self.settle(c)
            for k in range(1, zn):
                d = (pc.z + k) % zn
                arrived(self.am.at[d, :, pl.ds(c * self.chunk, self.chunk)], self.zr.at[c, d])


def rear_kernel(
    zn, chunk, heads, starts_ref,
    mid_ref, tok_ref, gain_ref, hg_ref, flat_ref, comb_ref,
    res_hbm, early_hbm, seq_hbm, wq_hbm, wo_hbm, pre_hbm, rot_hbm, val_hbm, lse_hbm, ctx_hbm, tab_hbm,
    grad_ref, oq_ref, oo_ref, sum_ref, tiny_ref, am_hbm, rr_hbm,
    big, wq, wo, pre, rot, val, lse, ctx, tab, bias,
    lse_t, del_t, key_t, cback, aback, dk, dv, dgain,
    gq, bq, vq, tq, go, bo, vo, to,
    c1, s1, ra, rb, last, rbuf, zbuf,
    gs, gr, hs, hr, sr, sl, rr, rl, ps, pr, xs, xr, zs, zr, ls, os, loads,
    *rest,
):
    place, sends = Place(), Sends()
    pc = place
    small_scratch, tiny_scratch = rest[:9], rest[9:]
    tok, width = mid_ref.shape
    length = PLANE * tok
    half = heads * HD
    own_rows = wq.shape[1]
    chunks = width // chunk
    scale = HD ** (-0.5)
    greet(place, zn)
    pairs = (
        (wo_hbm, wo), (ctx_hbm, ctx), (rot_hbm, rot), (val_hbm, val), (lse_hbm, lse),
        (pre_hbm, pre), (tab_hbm, tab), (wq_hbm, wq),
    )
    fetch = [pltpu.make_async_copy(a, b, loads.at[i]) for i, (a, b) in enumerate(pairs)]
    small = SmallSum(place, sends, zn, flat_ref, sum_ref, small_scratch)
    tiny = TinySum(place, sends, zn, tiny_ref, tiny_scratch)
    row_sends = Sends()
    rows = PlaneGather(place, row_sends, big, gs, gr)
    result = Result(
        place, sends, zn, res_hbm, early_hbm, comb_ref, rr_hbm, am_hbm, rbuf, zbuf, chunk, xs, xr, zs, zr, ls, os
    )
    o = ColumnReduce(place, sends, zn, go, bo, sr.at[1], sl.at[1], rr.at[1], rl.at[1])
    q = ColumnReduce(place, sends, zn, gq, bq, sr.at[0], sl.at[0], rr.at[0], rl.at[0])

    def stage(i, carry):
        at = pl.ds(pl.multiple_of(i * 32, 32), 32)
        big[pc.p, at, :] = mid_ref[at, :].astype(bf16)
        return carry

    lax.fori_loop(0, tok // 32, stage, 0)
    rows.first()
    rows.along()
    for copy in fetch:
        copy.start()
    small.first()
    rows.second()
    rows.third()
    result.mix(0, chunks)
    for copy in fetch[:5]:
        copy.wait()
    key_t[...] = rot[heads].astype(f32).T.astype(bf16)
    lse_t[...] = lse[...].T
    small.second()
    rows.last()
    for c in range(1, min(3, chunks)):
        result.first(c)

    order = []
    for k in range(zn):
        for d in (zn - 1 - k, k):
            if d not in order:
                order.append(d)

    def output_grad(d):
        cols = pl.ds(d * 2 * own_rows, 2 * own_rows)
        rhs = big[:, :, cols].reshape(length, 2 * own_rows)

        def body(i, carry):
            m = pl.ds(pl.multiple_of(i * 256, 256), 256)
            go[d, m, :] = tn_dot(ctx[:, m], rhs).astype(bf16)
            return carry

        lax.fori_loop(0, half // 256, body, 0)

    made = 0
    for k in range(1):
        while made < len(order) and not {zn - 1 - k, k} <= set(order[:made]):
            output_grad(order[made])
            made += 1
        o.step(k)

    def context_back(i, carry):
        at = pl.ds(pl.multiple_of(i * 2 * tok, 2 * tok), 2 * tok)
        lhs = big[pl.ds(2 * i, 2)].reshape(2 * tok, width)
        got = nn_dot(lhs, wo[...].reshape(width, half))
        cback[at, :] = got.astype(bf16)
        prod = got.astype(bf16).astype(f32) * ctx[at, :].astype(f32)
        for h in range(heads):
            s = jnp.sum(prod[:, h * HD : (h + 1) * HD], axis=1, keepdims=True)
            lse[at, h : h + 1] = s
        return carry

    lax.fori_loop(0, PLANE // 2, context_back, 0)
    while made < len(order):
        output_grad(order[made])
        made += 1
    del_t[...] = lse[...].T
    row_sends.finish()
    fill = pltpu.make_async_copy(seq_hbm, big, loads.at[len(pairs)])
    fill.start()
    small.third()
    dk[...] = jnp.zeros_like(dk)
    dv[...] = jnp.zeros_like(dv)
    dgain[...] = jnp.zeros_like(dgain)
    for copy in fetch[5:]:
        copy.wait()

    def norm_of(d, at, h, gain_row):
        d = d * tab[0, at, :] - turned(d) * tab[1, at, :]
        v = pre[at, pl.ds(h * HD if isinstance(h, int) else pl.multiple_of(h * HD, HD), HD)]
        r = rms_scale(v)
        hat = v * r
        s = d * hg_ref[pl.ds(gain_row, 1), :]
        got = r * (s - hat * jnp.mean(s * hat, axis=1, keepdims=True))
        dgain[pl.ds(gain_row, 1), :] += jnp.sum(d * hat, axis=0, keepdims=True)
        return got.astype(bf16)

    starts = [starts_ref[pc.z, j] for j in range(starts_ref.shape[1])]

    def attend(i):
        limit = key_limit(i, length)
        at = slice(i * QBLOCK, (i + 1) * QBLOCK)
        bias[:limit, :] = bias_block(starts, i * QBLOCK, limit, True)

        def body(h, carry):
            cols = pl.ds(pl.multiple_of(h * HD, HD), HD)
            query = rot[h, at, :]
            dctx = cback[at, cols]
            scores = nt_dot(rot[heads, :limit, :], query) * scale
            scores = scores + bias[:limit, :]
            probs = jnp.exp(scores - lse_t[pl.ds(h, 1), at])
            dprobs = nt_dot(val[:limit, :], dctx)
            dscores = (probs * (dprobs - del_t[pl.ds(h, 1), at])).astype(bf16)
            dv[:limit, :] += nn_dot(probs.astype(bf16), dctx)
            dk[:limit, :] += nn_dot(dscores, query)
            dq = nn_dot(key_t[:, :limit], dscores).T * scale
            aback[at, cols] = norm_of(dq, at, h, 0)
            return carry

        lax.fori_loop(0, heads, body, 0, unroll=2)

    for i in range(length // QBLOCK):
        attend(i)

    def keys(i, carry):
        at = pl.ds(pl.multiple_of(i * 256, 256), 256)
        aback[at, half : half + HD] = norm_of(dk[at, :] * scale, at, heads, 1)
        aback[at, half + HD : half + 2 * HD] = dv[at, :].astype(bf16)
        return carry

    lax.fori_loop(0, length // 256, keys, 0)
    fill.wait()

    def query_grad(d):
        for h in range(2):
            cols = pl.ds((2 * d + h) * own_rows, own_rows) if own_rows % 128 == 0 else None
            if cols is None:
                lhs = big[:, :, pl.ds(2 * d * own_rows, 2 * own_rows)]
                lhs = lhs.reshape(length, 2 * own_rows)
                if h == 0:
                    gq[d] = tn_dot(lhs, aback[...]).astype(bf16)
            else:
                lhs = big[:, :, cols].reshape(length, own_rows)
                gq[d, h * own_rows : (h + 1) * own_rows, :] = tn_dot(lhs, aback[...]).astype(bf16)

    made = 0
    for k in range(zn - 1):
        while made < len(order) and not {zn - 1 - k, k} <= set(order[:made]):
            query_grad(order[made])
            made += 1
        if k == 0:
            q.step(0)
            if zn > 2:
                o.step(1)
    while made < len(order):
        query_grad(order[made])
        made += 1

    mixed = 1
    red = PlaneReduce(
        place, sends, big, grad_ref, (c1, s1, ra, rb, last), hs, hr, pl.ds(0, width)
    )

    def norm1_part(k):
        y, x, j = red.chip(*red.chips[k])
        lhs = aback[pl.ds(pl.multiple_of(j * 2 * tok, 2 * tok), 2 * tok), :]

        def body(i, carry):
            cols = pl.ds(pl.multiple_of(i * chunk, chunk), chunk)
            e = i * (chunk // own_rows)
            rhs = wq[pl.ds(e, chunk // own_rows)].reshape(chunk, half + 2 * HD)
            big[pl.ds(j * 2, 2), :, cols] = nt_dot(lhs, rhs).astype(bf16).reshape(2, tok, chunk)
            return carry

        lax.fori_loop(0, width // chunk, body, 0)

    for k in range(4):
        norm1_part(k)
        red.first(k)
    if mixed < chunks:
        result.mix(mixed, chunks)
        mixed += 1
    for j in range(4):
        red.second(j)
    for k in range(1, zn - 1):
        q.step(k)
        if k + 1 < zn - 1:
            o.step(k + 1)
        if k == 1:
            red.third()
        if mixed < chunks:
            result.mix(mixed, chunks)
            mixed += 1
    def split_o(at, v):
        first, second = v[:, :own_rows], v[:, own_rows:]
        low = pc.y == 0
        vo[at, :] = jnp.where(low, second, first).astype(bf16)
        oo_ref[pc.y, at, :] = jnp.where(low, first, second)

    o.own(split_o)
    sends.start(vo, to, ps.at[1], pr.at[1], pc.peer(dy=1))
    if zn <= 2:
        red.third()
    red.finish()

    def tokens_back(i, carry):
        at = pl.ds(pl.multiple_of(i * 16, 16), 16)
        v = tok_ref[at, :].astype(f32)
        r = rms_scale(v)
        hat = v * r
        d = grad_ref[at, :]
        s = d * gain_ref[...]
        got = r * (s - hat * jnp.mean(s * hat, axis=1, keepdims=True))
        grad_ref[at, :] = mid_ref[at, :] + got
        return carry + jnp.sum(d * hat, axis=0, keepdims=True)

    total = lax.fori_loop(0, tok // 16, tokens_back, jnp.zeros((1, width), f32))
    tiny.vec[:, :width] = total
    tiny.vec[:, width : width + HD] = dgain[0:1, :]
    tiny.vec[:, width + HD : width + 2 * HD] = dgain[1:2, :]
    tiny.first()
    while mixed < chunks:
        result.mix(mixed, chunks)
        mixed += 1

    tiny.second()
    q_own(q, pc, zn, gq, bq, vq, oq_ref, own_rows)
    sends.start(vq, tq, ps.at[0], pr.at[0], pc.peer(dy=1))
    tiny.last()
    small.last()
    result.last(chunks)
    arrived(to, pr.at[1])
    oo_ref[1 - pc.y] = to[...].astype(f32)
    arrived(tq, pr.at[0])
    oq_ref[1 - pc.y] = tq[...].astype(f32)
    sends.finish()


def q_own(q, pc, zn, part, buf, give, out, rows, step=32):
    lower, upper = pc.z > 0, pc.z < zn - 1
    arrived(buf.at[pc.z + 1], q.rs_r.at[pc.z], lower)
    arrived(buf.at[pc.z], q.rs_l.at[pc.z], upper)

    def total(at):
        v = part[pc.z, at, :].astype(f32)
        v = v + jnp.where(lower, buf[pc.z + 1, at, :].astype(f32), 0.0)
        return v + jnp.where(upper, buf[pc.z, at, :].astype(f32), 0.0)

    def body(i, carry):
        at = pl.ds(pl.multiple_of(i * step, step), step)
        theirs = pl.ds(pl.multiple_of((1 - pc.y) * rows + i * step, step), step)
        mine = pl.ds(pl.multiple_of(pc.y * rows + i * step, step), step)
        give[at, :] = total(theirs).astype(bf16)
        out[pc.y, at, :] = total(mine)
        return carry

    lax.fori_loop(0, rows // step, body, 0)


def rear(
    zn, heads, starts, middle, tokens, gain, gains, flat, comb, res, early, seq, full_q, full_o, pre, rot, val, lse,
    ctx, tables, chunk=512,
):
    tok, width = tokens.shape
    length = PLANE * tok
    e, own_rows, wide = full_q.shape
    half = heads * HD
    chunks = width // chunk
    slots = res.shape[1]
    lanes = width + 2 * HD
    shape = jax.ShapeDtypeStruct
    vmem = pltpu.VMEM
    return pl.pallas_call(
        functools.partial(rear_kernel, zn, chunk, heads),
        out_shape=(
            shape((tok, width), f32),
            shape((2, own_rows, wide), f32),
            shape((2, half, own_rows), f32),
            shape(flat.shape, f32),
            shape((1, lanes), f32),
            shape((zn, tok, width), bf16),
            shape((PLANE, slots, width), bf16),
        ),
        in_specs=[SSPEC] + [VSPEC] * 6 + [ASPEC] * 11,
        out_specs=(VSPEC,) * 5 + (ASPEC,) * 2,
        scratch_shapes=[
            vmem((PLANE, tok, width), bf16),
            vmem((e, own_rows, wide), bf16),
            vmem((e, own_rows, half), bf16),
            vmem((length, wide), f32),
            vmem((heads + 1, length, HD), bf16),
            vmem((length, HD), bf16),
            vmem((length, 128), f32),
            vmem((length, half), bf16),
            vmem((2, length, HD), f32),
            vmem((length, QBLOCK), f32),
            vmem((128, length), f32),
            vmem((128, length), f32),
            vmem((HD, length), bf16),
            vmem((length, half), bf16),
            vmem((length, wide), bf16),
            vmem((length, HD), f32),
            vmem((length, HD), f32),
            vmem((8, HD), f32),
            vmem((zn, 2 * own_rows, wide), bf16),
            vmem((zn + 1, 2 * own_rows, wide), bf16),
            vmem((own_rows, wide), bf16),
            vmem((own_rows, wide), bf16),
            vmem((zn, half, 2 * own_rows), bf16),
            vmem((zn + 1, half, 2 * own_rows), bf16),
            vmem((half, own_rows), bf16),
            vmem((half, own_rows), bf16),
        ]
        + PlaneReduce.scratch(tok, width)
        + [
            vmem((PLANE, slots, chunk), bf16),
            vmem((2, zn, tok, chunk), bf16),
            dma_sems(8),
            dma_sems(8),
            dma_sems(1, 10),
            dma_sems(1, 10),
            dma_sems(2, zn),
            dma_sems(2, zn),
            dma_sems(2, zn),
            dma_sems(2, zn),
            dma_sems(2),
            dma_sems(2),
            dma_sems(chunks, PLANE),
            dma_sems(chunks, PLANE),
            dma_sems(chunks, zn),
            dma_sems(chunks, zn),
            dma_sems(PLANE),
            dma_sems(chunks),
            dma_sems(10),
        ]
        + SmallSum.scratch(zn, flat.shape[1], flat.shape[2])
        + TinySum.scratch(zn, lanes),
        compiler_params=params(5),
        name="rear",
    )(
        starts, middle, tokens, gain, gains, flat, comb, res, early, seq, full_q, full_o, pre, rot, val, lse,
        ctx, tables,
    )


def local(
    tokens,
    out_grad,
    first_gain,
    second_gain,
    query_gain,
    key_gain,
    query_weight,
    key_weight,
    value_weight,
    output_weight,
    router_weight,
    gate_weight,
    up_weight,
    down_weight,
    expert_ids,
    router_order,
    image_starts,
):
    tok, width = tokens.shape
    zn = lax.axis_size("exp") // 2
    experts = PLANE * zn
    cap = (9 * tok * TOP + 8 * experts - 1) // (8 * experts)
    slots = zn * cap
    length = PLANE * tok
    own_rows = query_weight.shape[0]
    half = query_weight.shape[1] // 2
    heads = half // HD
    expert_axis = jnp.arange(experts, dtype=jnp.int32)
    member = jnp.any(expert_ids[:, :, None] == expert_axis[None, None, :], axis=1)
    order_here = router_order[0]
    earlier = (order_here[None, :] < order_here[:, None]).astype(bf16)
    counts = jnp.dot(earlier, member.astype(bf16), preferred_element_type=f32)
    keep = member & (counts < cap)
    slot_of = jnp.where(keep, counts, -1.0)

    resid_in = tokens.astype(f32)
    tables = jnp.asarray(rotary_tables(length))
    slot_t = slot_of.T.reshape(zn, PLANE, tok)
    gains = jnp.stack([query_gain, key_gain])
    (
        lse, attention, slots_all, seq_norm, full_q, full_o, pre, rot, value_rows, context_rows, rows_g,
    ) = front(
        zn, cap, heads, image_starts, tokens, first_gain[None], query_weight, key_weight, value_weight,
        output_weight, gains, out_grad, slot_t, tables,
    )
    resid_mid = resid_in + attention
    second_rms = rms_scale(resid_mid)
    second_hat = resid_mid * second_rms
    second_norm = (second_hat * second_gain).astype(bf16)
    logits = jnp.dot(second_norm, router_weight, preferred_element_type=f32)
    mix = jax.nn.softmax(jnp.where(member, logits, NEGATIVE), axis=-1)
    mix = jnp.where(member, mix, 0.0)
    keep_mix = jnp.where(keep, mix, 0.0)
    mix_t = keep_mix.T.reshape(zn, PLANE, tok)
    gate_w, up_w, down_w = gate_weight[0], up_weight[0], down_weight[0]
    dot_lanes, rows_n, mids, hot, comb = there(
        zn, cap, second_norm, slots_all, mix_t, rows_g, gate_w, up_w, down_w
    )
    dots_all, pairs, result, gate_grad, up_grad, down_grad, result_first = back_rows(
        zn, tok, dot_lanes, hot, mids, rows_n, rows_g, gate_w, up_w, down_w
    )
    pairs_sum = jnp.sum(pairs.astype(f32), axis=0)
    grad_out = out_grad.astype(f32)
    mix_dots = dots_all[:, :, :PLANE] + dots_all[:, :, PLANE : 2 * PLANE]
    mix_dots = mix_dots.transpose(1, 0, 2).reshape(tok, experts)
    chosen_grad = mix_dots - mix * jnp.sum(mix_dots, axis=1, keepdims=True)
    logit_grad = chosen_grad.astype(bf16)
    router_part = jnp.dot(second_norm.T, logit_grad, preferred_element_type=f32)
    norm2_back = pairs_sum + jnp.dot(logit_grad, router_weight.T, preferred_element_type=f32)
    mid_from_norm, second_gain_part = norm_back(norm2_back, second_hat, second_rms, second_gain)
    middle_grad = grad_out + mid_from_norm

    flat = jnp.concatenate([router_part.reshape(-1), second_gain_part])
    count = flat.shape[0]
    unit = PLANE * 8 * 128
    padded = -(-count // unit) * unit
    flat = jnp.pad(flat, (0, padded - count)).reshape(PLANE, padded // (PLANE * 128), 128)
    tokens_grad, sum_q, sum_o, flat, tiny, mixtures, _ = rear(
        zn, heads, image_starts, middle_grad, tokens, first_gain[None], gains, flat, comb,
        result, result_first, seq_norm, full_q, full_o, pre, rot, value_rows, lse,
        context_rows, tables,
    )
    block_out = (resid_mid + jnp.sum(mixtures.astype(f32), axis=0)).astype(bf16)
    query_grad = jnp.concatenate([sum_q[0, :, :half], sum_q[1, :, :half]], axis=1)
    kv_grad = sum_q[0, :, half:] + sum_q[1, :, half:]
    key_grad, value_grad = kv_grad[:, :HD], kv_grad[:, HD:]
    output_grad = sum_o.reshape(2 * half, own_rows)
    flat = flat.reshape(-1)
    n_router = width * experts
    router_grad = flat[:n_router].reshape(width, experts)
    second_gain_grad = flat[n_router : n_router + width]
    tiny = tiny[0]
    first_gain_grad = tiny[:width]
    query_gain_grad = tiny[width : width + HD]
    key_gain_grad = tiny[width + HD :]
    return (
        block_out,
        tokens_grad,
        first_gain_grad,
        second_gain_grad,
        query_gain_grad,
        key_gain_grad,
        query_grad,
        key_grad,
        value_grad,
        output_grad,
        router_grad,
        gate_grad[None],
        up_grad[None],
        down_grad[None],
    )


def solution(mesh):
    both = ("exp", "tp")
    in_specs = (
        P(both, None),
        P(both, None),
        P(),
        P(),
        P(),
        P(),
        P("exp", "tp"),
        P("exp", "tp"),
        P("exp", "tp"),
        P("tp", "exp"),
        P(),
        P(both, None, None),
        P(both, None, None),
        P(both, None, None),
        P(both, None),
        P(both, None),
        P(),
    )
    out_specs = (
        P(both, None),
        P(both, None),
        P(),
        P(),
        P(),
        P(),
        P("exp", "tp"),
        P("exp", "tp"),
        P("exp", "tp"),
        P("tp", "exp"),
        P(),
        P(both, None, None),
        P(both, None, None),
        P(both, None, None),
    )
    return jax.shard_map(local, mesh=mesh, in_specs=in_specs, out_specs=out_specs, check_vma=False)
```

```python
import functools

import jax
import jax.numpy as jnp
import numpy as np
from jax import lax
from jax.experimental import pallas as pl
from jax.experimental.pallas import tpu as pltpu
from jax.sharding import PartitionSpec as P

HD = 128
TOP = 8
IMG_LEN = 256
PLANE = 8

EPSILON = 1e-06
THETA = 1000000.0
NEGATIVE = -1e30

MESH = pl.DeviceIdType.MESH
f32 = jnp.float32
bf16 = jnp.bfloat16
VMEM_LIMIT = 60 << 20


def rms_scale(values):
    return lax.rsqrt(jnp.mean(values * values, axis=-1, keepdims=True) + EPSILON)


def rotary_tables(length):
    freqs = np.float32(THETA) ** (-(np.arange(HD // 2, dtype=np.float32) * np.float32(2.0 / HD)))
    angles = np.arange(length, dtype=np.float32)[:, None] * freqs.astype(np.float32)[None, :]
    cosine, sine = np.cos(angles.astype(np.float64)), np.sin(angles.astype(np.float64))
    first = np.concatenate([cosine, cosine], axis=1)
    second = np.concatenate([-sine, sine], axis=1)
    return np.stack([first, second]).astype(np.float32)


def norm_back(grad_norm, hat, rms, gain):
    scaled = grad_norm * gain
    inner_mean = jnp.mean(scaled * hat, axis=-1, keepdims=True)
    lead_axes = tuple(range(grad_norm.ndim - 1))
    return (rms * (scaled - hat * inner_mean), jnp.sum(grad_norm * hat, axis=lead_axes))


class Place:
    def __init__(self):
        self.e = lax.axis_index("exp")
        self.t = lax.axis_index("tp")
        self.z = self.e // 2
        self.y = self.e % 2
        self.x = self.t // 2
        self.c = self.t % 2
        self.p = self.y * 4 + self.t

    def at(self, z, p):
        return (z * 2 + p // 4, p % 4)

    def flip(self, dy=0, dx=0, dc=0):
        y = 1 - self.y if dy else self.y
        x = 1 - self.x if dx else self.x
        c = 1 - self.c if dc else self.c
        return y * 4 + x * 2 + c

    def peer(self, dy=0, dx=0, dc=0):
        return self.at(self.z, self.flip(dy, dx, dc))

    def by(self, k):
        return self.flip((k >> 2) & 1, (k >> 1) & 1, k & 1)


class Sends:
    def __init__(self):
        self.kept = []

    def start(self, src, dst, send_sem, recv_sem, device, when=None):
        def make():
            return pltpu.make_async_remote_copy(
                src_ref=src,
                dst_ref=dst,
                send_sem=send_sem,
                recv_sem=recv_sem,
                device_id=device,
                device_id_type=MESH,
            )

        def go():
            make().start()

        if when is None:
            go()
        else:
            pl.when(when)(go)
        self.kept.append((make, when))

    def finish(self):
        for make, when in self.kept:
            if when is None:
                make().wait_send()
            else:
                pl.when(when)(lambda make=make: make().wait_send())
        self.kept = []


def arrived(dst, recv_sem, when=None):
    def go():
        pltpu.make_async_copy(dst, dst, recv_sem).wait()

    if when is None:
        go()
    else:
        pl.when(when)(go)


def greet(place, zn, cross=False):
    bar = pltpu.get_barrier_semaphore()
    met = [place.at(place.z, place.by(k)) for k in range(1, PLANE)]
    for k in range(1, zn):
        z = (place.z + k) % zn
        met.append(place.at(z, place.p))
        if cross:
            met.append(place.at(z, place.flip(dy=1)))
    for device in met:
        pl.semaphore_signal(bar, inc=1, device_id=device, device_id_type=MESH)
    pl.semaphore_wait(bar, len(met))


class PlaneGather:
    sems = 8

    def __init__(self, place, sends, buf, ss, rs):
        self.place, self.sends, self.buf, self.ss, self.rs = place, sends, buf, ss, rs
        half = buf.shape[2] // 2
        self.cols_a = pl.ds(0, half)
        self.cols_b = pl.ds(half, half)

    def _send(self, block, which, device, cols=None):
        ref = self.buf.at[block] if cols is None else self.buf.at[block, :, cols]
        self.sends.start(ref, ref, self.ss.at[which], self.rs.at[which], device)

    def _wait(self, block, which, cols=None):
        ref = self.buf.at[block] if cols is None else self.buf.at[block, :, cols]
        arrived(ref, self.rs.at[which])

    def first(self):
        pc = self.place
        self._send(pc.p, 1, pc.peer(dx=1))
        self._send(pc.p, 2, pc.peer(dc=1))

    def along(self):
        self._send(self.place.p, 0, self.place.peer(dy=1))

    def second(self):
        pc = self.place
        px, py = pc.flip(dx=1), pc.flip(dy=1)
        self._wait(px, 1)
        self._send(px, 3, pc.peer(dy=1), self.cols_a)
        self._send(px, 4, pc.peer(dc=1))
        self._wait(py, 0)
        self._send(py, 5, pc.peer(dx=1), self.cols_b)
        self._send(py, 6, pc.peer(dc=1))

    def third(self):
        pc = self.place
        pd = pc.flip(dy=1, dx=1)
        self._wait(pd, 3, self.cols_a)
        self._wait(pd, 5, self.cols_b)
        self._send(pd, 7, pc.peer(dc=1))

    def last(self):
        pc = self.place
        self._wait(pc.flip(dc=1), 2)
        self._wait(pc.flip(dc=1, dx=1), 4)
        self._wait(pc.flip(dc=1, dy=1), 6)
        self._wait(pc.flip(dc=1, dy=1, dx=1), 7)


def add_rows(dst, first, second, rows, step=32, when=None):
    if when is not None:
        pl.when(when)(lambda: add_rows(dst, first, second, rows, step))
        return

    def body(i, carry):
        at = pl.ds(pl.multiple_of(i * step, step), step)
        dst(at, first(at).astype(f32) + second(at).astype(f32))
        return carry

    lax.fori_loop(0, rows // step, body, 0)


class PlaneReduce:
    @staticmethod
    def scratch(rows, width, windows=1):
        return [
            pltpu.VMEM((windows, 4, rows, width), bf16),
            pltpu.VMEM((windows, 4, rows, width), bf16),
            pltpu.VMEM((windows, 2, rows // 2, width), bf16),
            pltpu.VMEM((windows, 2, rows // 2, width), bf16),
            pltpu.VMEM((windows, 2, rows // 2, width), bf16),
        ]

    def __init__(self, place, sends, part, out, scratch, ss, rs, cols, slot=0, when=None):
        self.place, self.sends, self.part, self.out = place, sends, part, out
        self.c1, self.s1, self.ra, self.rb, self.late = (ref.at[slot] for ref in scratch)
        self.ss, self.rs = ss.at[slot], rs.at[slot]
        self.cols, self.when = cols, when
        self.rows = part.shape[1]
        self.half = self.rows // 2
        self.chips = [(1, 1), (0, 1), (1, 0), (0, 0)]

    def chip(self, dy, dx):
        pc = self.place
        y = 1 - pc.y if dy else pc.y
        x = 1 - pc.x if dx else pc.x
        return y, x, y * 2 + x

    def _send(self, src, dst, i, device):
        self.sends.start(src, dst, self.ss.at[i], self.rs.at[i], device, self.when)

    def _take(self, dst, i):
        arrived(dst, self.rs.at[i], self.when)

    def _add(self, dst, first, second, rows):
        add_rows(dst, first, second, rows, when=self.when)

    def first(self, k):
        pc = self.place
        y, x, j = self.chip(*self.chips[k])
        block = y * 4 + x * 2 + (1 - pc.c)
        self._send(self.part.at[block, :, self.cols], self.c1.at[j], k, pc.peer(dc=1))

    def second(self, k):
        pc = self.place
        dy, dx = self.chips[k]
        y, x, j = self.chip(dy, dx)
        self._take(self.c1.at[j], k)
        mine = y * 4 + x * 2 + pc.c

        def put(at, v):
            self.s1[j, at, :] = v.astype(bf16)

        self._add(
            put, lambda at: self.part[mine, at, self.cols], lambda at: self.c1[j, at, :], self.rows
        )
        if dx:
            self._send(
                self.s1.at[j, pl.ds(0, self.half), :],
                self.ra.at[y],
                4 + (0 if dy else 1),
                pc.peer(dx=1),
            )
        if dy:
            self._send(
                self.s1.at[j, pl.ds(self.half, self.half), :],
                self.rb.at[x],
                6 + (0 if dx else 1),
                pc.peer(dy=1),
            )

    def third(self):
        pc = self.place
        for buf, slot, base, sem, other, out_sem in (
            (self.ra, 1 - pc.y, 0, 4, pc.peer(dy=1), 8),
            (self.rb, 1 - pc.x, self.half, 6, pc.peer(dx=1), 9),
        ):
            self._take(buf.at[slot], sem)
            j = (1 - pc.y) * 2 + pc.x if base == 0 else pc.y * 2 + 1 - pc.x

            def put(at, v, buf=buf, slot=slot):
                buf[slot, at, :] = v.astype(bf16)

            self._add(
                put,
                lambda at, j=j, base=base: self.s1[j, pl.ds(at.start + base, at.size), :],
                lambda at, buf=buf, slot=slot: buf[slot, at, :],
                self.half,
            )
            self._send(buf.at[slot], self.late.at[out_sem - 8], out_sem, other)

    def finish(self):
        pc = self.place
        own = pc.y * 2 + pc.x
        for i, (buf, slot, base, sem) in enumerate(
            ((self.ra, pc.y, 0, 5), (self.rb, pc.x, self.half, 7))
        ):
            self._take(buf.at[slot], sem)
            self._take(self.late.at[i], 8 + i)

            def put(at, v, buf=buf, slot=slot, base=base):
                to = pl.ds(at.start + base, at.size)
                self.out[to, self.cols] = v + buf[slot, at, :].astype(f32)

            self._add(
                put,
                lambda at, base=base: self.s1[own, pl.ds(at.start + base, at.size), :],
                lambda at, i=i: self.late[i, at, :],
                self.half,
            )


class ColumnGather:
    def __init__(self, place, sends, zn, pack, full, pair_ss, pair_rs, ss_r, ss_l, rs):
        self.place, self.sends, self.zn = place, sends, zn
        self.pack, self.full = pack, full
        self.pair_ss, self.pair_rs, self.ss_r, self.ss_l, self.rs = pair_ss, pair_rs, ss_r, ss_l, rs

    def _on(self, src, piece, right, left):
        pc = self.place
        if right is not None:
            self.sends.start(
                src,
                self.full.at[piece],
                self.ss_r.at[piece],
                self.rs.at[piece],
                pc.at(jnp.minimum(pc.z + 1, self.zn - 1), pc.p),
                right,
            )
        if left is not None:
            self.sends.start(
                src,
                self.full.at[piece],
                self.ss_l.at[piece],
                self.rs.at[piece],
                pc.at(jnp.maximum(pc.z - 1, 0), pc.p),
                left,
            )

    def pair(self):
        pc = self.place
        self.sends.start(
            self.pack.at[1 - pc.y],
            self.full.at[pc.e],
            self.pair_ss,
            self.pair_rs,
            pc.peer(dy=1),
        )

    def own(self):
        pc = self.place
        self._on(self.pack.at[pc.y], pc.e, pc.z < self.zn - 1, pc.z > 0)

    def keep(self):
        pc = self.place
        self.full[pc.e] = self.pack[pc.y]

    def partner(self):
        pc = self.place
        other = pc.z * 2 + 1 - pc.y
        arrived(self.full.at[other], self.pair_rs)
        self._on(self.full.at[other], other, pc.z < self.zn - 1, pc.z > 0)

    def step(self, k):
        pc = self.place
        for first in (True, False):
            y = pc.y if first else 1 - pc.y
            below = jnp.maximum(pc.z - k, 0) * 2 + y
            has = pc.z - k >= 0
            arrived(self.full.at[below], self.rs.at[below], has)
            self._on(
                self.full.at[below], below, jnp.logical_and(has, pc.z < self.zn - 1), None
            )
            above = jnp.minimum(pc.z + k, self.zn - 1) * 2 + y
            has = pc.z + k < self.zn
            arrived(self.full.at[above], self.rs.at[above], has)
            self._on(self.full.at[above], above, None, jnp.logical_and(has, pc.z > 0))


def dma_sems(*shape):
    return pltpu.SemaphoreType.DMA(shape)


VSPEC = pl.BlockSpec(memory_space=pltpu.VMEM)
ASPEC = pl.BlockSpec(memory_space=pl.ANY)
SSPEC = pl.BlockSpec(memory_space=pltpu.SMEM)


def params(cid):
    return pltpu.CompilerParams(
        collective_id=cid, has_side_effects=True, vmem_limit_bytes=VMEM_LIMIT
    )


class RowPush:
    def __init__(self, place, sends, zn, src, buf, chunk, ss, rs):
        self.place, self.sends, self.zn = place, sends, zn
        self.src, self.buf, self.chunk = src, buf, chunk
        self.ss, self.rs = ss, rs

    def own(self, c):
        pc = self.place
        cols = pl.ds(c * self.chunk, self.chunk)
        for k in range(1, self.zn):
            self.sends.start(
                self.src.at[:, cols],
                self.buf.at[pc.z, :, cols],
                self.ss.at[c, k],
                self.rs.at[c, pc.z],
                pc.at((pc.z + k) % self.zn, pc.p),
            )

    def keep(self):
        self.buf[self.place.z] = self.src[...]

    def take(self, c):
        pc = self.place
        for k in range(1, self.zn):
            d = (pc.z + k) % self.zn
            arrived(self.buf.at[d, :, pl.ds(c * self.chunk, self.chunk)], self.rs.at[c, d])


def turned(values):
    return pltpu.roll(values, HD // 2, 1)


def nt_dot(a, b):
    return lax.dot_general(a, b, (((1,), (1,)), ((), ())), preferred_element_type=f32)


def tn_dot(a, b):
    return lax.dot_general(a, b, (((0,), (0,)), ((), ())), preferred_element_type=f32)


def nn_dot(a, b):
    return jnp.dot(a, b, preferred_element_type=f32)


QBLOCK = 256


def key_limit(i, length):
    return min(length, (i + 1) * QBLOCK + IMG_LEN)


def bias_block(starts, at, length, turn):
    limit = length
    shape = (limit, QBLOCK) if turn else (QBLOCK, limit)
    query = lax.broadcasted_iota(jnp.int32, shape, 1 if turn else 0) + at
    key = lax.broadcasted_iota(jnp.int32, shape, 0 if turn else 1)
    allowed = key <= query
    for start in starts:
        low = (query >= start) & (query < start + IMG_LEN)
        allowed = allowed | (low & (key >= start) & (key < start + IMG_LEN))
    return jnp.where(allowed, 0.0, NEGATIVE)


def send_slots(place, sends, zn, src, dst, ss, rs):
    for k in range(1, zn):
        d = (place.z + k) % zn
        sends.start(src.at[d], dst.at[place.z], ss.at[k], rs.at[place.z], place.at(d, place.p))


def take_slots(place, zn, src, dst, rs):
    dst[place.z] = src[place.z]
    for k in range(1, zn):
        d = (place.z + k) % zn
        arrived(dst.at[d], rs.at[d])


def make_hot(zn, cap, tok, slots_ref, hot):
    row = lax.broadcasted_iota(jnp.int32, (zn * cap, tok), 0).astype(f32)

    def body(p, carry):
        for z in range(zn):
            have = slots_ref[z, pl.ds(p, 1), :]
            want = jnp.where(have < 0, -1.0, have + float(z * cap))
            hot[p, :, pl.ds(z * tok, tok)] = jnp.where(row == want, 1.0, 0.0).astype(bf16)
        return carry

    lax.fori_loop(0, PLANE, body, 0)


class PlaneSend:
    def __init__(self, place, sends, hot, rows, buf, out, chunk, ss, rs):
        self.place, self.sends = place, sends
        self.hot, self.rows, self.buf, self.out, self.chunk = hot, rows, buf, out, chunk
        self.ss, self.rs = ss, rs

    def send(self, c):
        pc = self.place
        cols = pl.ds(c * self.chunk, self.chunk)
        zn, tok, _ = self.rows.shape
        for k in (1, 2, 3, 4, 5, 6, 7, 0):
            p = pc.by(k) if k else pc.p
            got = nn_dot(self.hot[p], self.rows[:, :, cols].reshape(zn * tok, self.chunk))
            self.buf[p, :, cols] = got.astype(bf16)
            if k:
                self.sends.start(
                    self.buf.at[p, :, cols],
                    self.out.at[pc.p, :, cols],
                    self.ss.at[c, k],
                    self.rs.at[c, k],
                    pc.at(pc.z, p),
                )
            else:
                self._own(c).start()

    def _own(self, c):
        p = self.place.p
        cols = pl.ds(c * self.chunk, self.chunk)
        return pltpu.make_async_copy(self.buf.at[p, :, cols], self.out.at[p, :, cols], self.rs.at[c, 0])

    def take(self, c):
        cols = pl.ds(c * self.chunk, self.chunk)
        self._own(c).wait()
        for k in range(1, PLANE):
            arrived(self.out.at[self.place.by(k), :, cols], self.rs.at[c, k])


def front_kernel(
    zn, cap, chunk, heads, starts_ref,
    tok_ref, gain_ref, q_ref, k_ref, v_ref, o_ref, hg_ref, grad_ref, slot_ref, tab_hbm,
    lse_ref, att_ref, so_ref, seq_hbm, wq_hbm, wo_hbm, pre_hbm, rot_hbm, val_hbm, ctx_hbm, ag_hbm,
    seq, wq, wo, pre, rot, val, ctx, tab, bias, pq, po,
    part, c1, s1, ra, rb, last, gb, sn, hot,
    gs, gr, ps, pr, sr, sl, rs, hs, hr, zs, zr, ts, tr, xs, xr, out_sems,
):
    place, sends = Place(), Sends()
    pc = place
    tok, width = tok_ref.shape
    length = PLANE * tok
    own_rows = pq.shape[1]
    half = heads * HD
    chunks = width // chunk
    scale = HD ** (-0.5)
    table = pltpu.make_async_copy(tab_hbm, tab, out_sems.at[7])
    table.start()
    for y in range(2):
        pq[y, :, :half] = q_ref[:, y * half : (y + 1) * half]
        pq[y, :, half : half + HD] = k_ref[...]
        pq[y, :, half + HD :] = v_ref[...]
    greet(place, zn)
    q = ColumnGather(place, sends, zn, pq, wq, ps.at[0], pr.at[0], sr.at[0], sl.at[0], rs.at[0])
    o = ColumnGather(place, sends, zn, po, wo, ps.at[1], pr.at[1], sr.at[1], sl.at[1], rs.at[1])
    g = RowPush(place, sends, zn, grad_ref, gb, chunk, zs, zr)
    q.pair()
    q.own()

    def first_norm(i, carry):
        at = pl.ds(pl.multiple_of(i * 32, 32), 32)
        v = tok_ref[at, :].astype(f32)
        seq[pc.p, at, :] = (v * rms_scale(v) * gain_ref[...]).astype(bf16)
        return carry

    lax.fori_loop(0, tok // 32, first_norm, 0)
    rows = PlaneGather(place, sends, seq, gs, gr)
    rows.first()
    q.keep()
    q.partner()
    rows.along()
    send_slots(place, sends, zn, slot_ref, so_ref, ts, tr)
    for y in range(2):
        po[y] = o_ref[y * half : (y + 1) * half, :].astype(f32).T.astype(bf16)
    o.keep()
    g.keep()
    rows.second()
    o.pair()
    take_slots(place, zn, slot_ref, so_ref, tr)
    make_hot(zn, cap, tok, so_ref, hot)
    rows.third()
    pre[...] = jnp.zeros_like(pre)

    def project(origin):
        cols = pl.ds(pl.multiple_of(origin * 2 * own_rows, 2 * own_rows), 2 * own_rows)
        weight = wq.at[pl.ds(2 * origin, 2)]

        def body(i, carry):
            at = pl.ds(pl.multiple_of(i * 2 * tok, 2 * tok), 2 * tok)
            lhs = seq[pl.ds(2 * i, 2), :, cols].reshape(2 * tok, 2 * own_rows)
            pre[at, :] += nn_dot(lhs, weight[...].reshape(2 * own_rows, half + 2 * HD))
            return carry

        lax.fori_loop(0, PLANE // 2, body, 0)

    def project_step(k):
        pl.when(pc.z - k >= 0)(lambda: project(jnp.maximum(pc.z - k, 0)))
        pl.when(pc.z + k < zn)(lambda: project(jnp.minimum(pc.z + k, zn - 1)))

    kept = []

    def keep(i, src, dst):
        copy = pltpu.make_async_copy(src, dst, out_sems.at[i])
        copy.start()
        kept.append(copy)

    for k in range(1, zn):
        q.step(k)
        if k == max(1, zn - 2):
            g.own(0)
        if k == 1:
            rows.last()
            keep(0, seq, seq_hbm)
            project(pc.z)
        project_step(k)
    g.own(1)
    keep(1, wq, wq_hbm)
    keep(2, pre, pre_hbm)
    table.wait()

    def turn(i, carry):
        at = pl.ds(pl.multiple_of(i * 128, 128), 128)
        cos, sin = tab[0, at, :], tab[1, at, :]
        for h in range(heads + 1):
            v = pre[at, h * HD : (h + 1) * HD]
            gain = hg_ref[pl.ds(0 if h < heads else 1, 1), :]
            v = v * rms_scale(v) * gain
            rot[h, at, :] = (v * cos + turned(v) * sin).astype(bf16)
        val[at, :] = pre[at, half + HD : half + 2 * HD].astype(bf16)
        return carry

    lax.fori_loop(0, length // 128, turn, 0)
    keep(3, rot, rot_hbm)
    keep(4, val, val_hbm)
    lane = lax.broadcasted_iota(jnp.int32, (QBLOCK, 128), 1)
    starts = [starts_ref[pc.z, j] for j in range(starts_ref.shape[1])]

    def attend(i):
        limit = key_limit(i, length)
        at = slice(i * QBLOCK, (i + 1) * QBLOCK)
        bias[:, :limit] = bias_block(starts, i * QBLOCK, limit, False)

        def body(h, carry):
            scores = nt_dot(rot[h, at, :], rot[heads, :limit, :]) * scale + bias[:, :limit]
            top = jnp.max(scores, axis=1, keepdims=True)
            expo = jnp.exp(scores - top)
            total = jnp.sum(expo, axis=1, keepdims=True)
            low = (expo * (1.0 / total)).astype(bf16)
            cols = pl.ds(pl.multiple_of(h * HD, HD), HD)
            ctx[at, cols] = nn_dot(low, val[:limit, :]).astype(bf16)
            lse_ref[at, :] = jnp.where(lane == h, top + jnp.log(total), lse_ref[at, :])
            return carry

        lax.fori_loop(0, heads, body, 0, unroll=2)

    lse_ref[...] = jnp.zeros_like(lse_ref)
    give = PlaneSend(place, sends, hot, gb, sn, ag_hbm, chunk, xs, xr)
    blocks = length // QBLOCK
    given = 0
    for i in range(blocks):
        attend(i)
        if given < chunks - 1:
            g.take(given)
            if given < chunks - 3:
                g.own(given + 2)
            if given == max(chunks - 3, 0):
                o.own()
                o.partner()
            give.send(given)
            given += 1
    keep(5, ctx, ctx_hbm)

    def output(origin):
        cols = pl.ds(pl.multiple_of(origin * 2 * own_rows, 2 * own_rows), 2 * own_rows)
        weight = wo.at[pl.ds(2 * origin, 2)]

        def body(i, carry):
            at = pl.ds(pl.multiple_of(i * 2 * tok, 2 * tok), 2 * tok)
            got = nt_dot(ctx[at, :], weight[...].reshape(2 * own_rows, half))
            part[pl.ds(2 * i, 2), :, cols] = got.astype(bf16).reshape(2, tok, 2 * own_rows)
            return carry

        lax.fori_loop(0, PLANE // 2, body, 0)

    def visit(origin, when):
        cols = pl.ds(pl.multiple_of(origin * 2 * own_rows, 2 * own_rows), 2 * own_rows)
        red = PlaneReduce(
            place, sends, part, att_ref, (c1, s1, ra, rb, last), hs, hr, cols, origin, when
        )
        if when is None:
            output(origin)
        else:
            pl.when(when)(lambda: output(origin))
        for j in range(4):
            red.first(j)
        visits.append(red)

    def push_on():
        for lag, stage in ((2, 2), (3, 3), (4, 4)):
            if len(visits) >= lag:
                step_on(visits[-lag], stage)

    def step_on(red, stage):
        if stage == 2:
            for j in range(4):
                red.second(j)
        elif stage == 3:
            red.third()
        else:
            red.finish()

    visits = []
    visit(pc.z, None)
    for k in range(1, zn):
        o.step(k)
        if k == max(1, zn - 2):
            g.own(chunks - 1)
        visit(jnp.maximum(pc.z - k, 0), pc.z - k >= 0)
        push_on()
        visit(jnp.minimum(pc.z + k, zn - 1), pc.z + k < zn)
        push_on()
    keep(6, wo, wo_hbm)
    step_on(visits[-1], 2)
    while given < chunks:
        g.take(given)
        give.send(given)
        given += 1
    step_on(visits[-2], 3)
    step_on(visits[-1], 3)
    for red in visits[-3:]:
        step_on(red, 4)
    for c in range(chunks):
        give.take(c)
    for copy in kept:
        copy.wait()
    sends.finish()


def front(
    zn, cap, heads, starts, tokens, gain, query, key, value, output, gains, grad, slot, tables, chunk=512
):
    tok, width = tokens.shape
    length = PLANE * tok
    own_rows = query.shape[0]
    e = 2 * zn
    slots = zn * cap
    chunks = width // chunk
    half = heads * HD
    wide = half + 2 * HD
    shape = jax.ShapeDtypeStruct
    vmem = pltpu.VMEM
    return pl.pallas_call(
        functools.partial(front_kernel, zn, cap, chunk, heads),
        out_shape=(
            shape((length, 128), f32),
            shape((tok, width), f32),
            shape(slot.shape, f32),
            shape((PLANE, tok, width), bf16),
            shape((e, own_rows, wide), bf16),
            shape((e, own_rows, half), bf16),
            shape((length, wide), f32),
            shape((heads + 1, length, HD), bf16),
            shape((length, HD), bf16),
            shape((length, half), bf16),
            shape((PLANE, slots, width), bf16),
        ),
        in_specs=[SSPEC] + [VSPEC] * 9 + [ASPEC],
        out_specs=(VSPEC,) * 3 + (ASPEC,) * 8,
        scratch_shapes=[
            vmem((PLANE, tok, width), bf16),
            vmem((e, own_rows, wide), bf16),
            vmem((e, own_rows, half), bf16),
            vmem((length, wide), f32),
            vmem((heads + 1, length, HD), bf16),
            vmem((length, HD), bf16),
            vmem((length, half), bf16),
            vmem((2, length, HD), f32),
            vmem((QBLOCK, length), f32),
            vmem((2, own_rows, wide), bf16),
            vmem((2, own_rows, half), bf16),
            vmem((PLANE, tok, width), bf16),
        ]
        + PlaneReduce.scratch(tok, 2 * own_rows, zn)
        + [
            vmem((zn, tok, width), bf16),
            vmem((PLANE, slots, width), bf16),
            vmem((PLANE, slots, zn * tok), bf16),
            dma_sems(8),
            dma_sems(8),
            dma_sems(2),
            dma_sems(2),
            dma_sems(2, e),
            dma_sems(2, e),
            dma_sems(2, e),
            dma_sems(zn, 10),
            dma_sems(zn, 10),
            dma_sems(chunks, zn),
            dma_sems(chunks, zn),
            dma_sems(zn),
            dma_sems(zn),
            dma_sems(chunks, PLANE),
            dma_sems(chunks, PLANE),
            dma_sems(8),
        ],
        compiler_params=params(0),
        name="front",
    )(starts, tokens, gain, query, key, value, output, gains, grad, slot, tables)


class Flow:
    def __init__(self, stage, sems):
        self.stage, self.sems = stage, sems
        self.count = 0
        self.flight = [None, None]

    def slot(self):
        i = self.count % 2
        if self.flight[i] is not None:
            self.flight[i].wait()
            self.flight[i] = None
        return i

    def send(self, dst):
        i = self.count % 2
        copy = pltpu.make_async_copy(self.stage.at[i], dst, self.sems.at[i])
        copy.start()
        self.flight[i] = copy
        self.count += 1

    def finish(self):
        for i in range(2):
            if self.flight[i] is not None:
                self.flight[i].wait()
                self.flight[i] = None


def there_kernel(
    zn, cap, chunk, norm_ref, slots_ref, mix_ref, ag_hbm, gate_hbm, up_hbm, down_hbm,
    dot_ref, an_hbm, mid_hbm, hot_t_hbm, comb_hbm,
    an_ref, mid_ref, nb, sn, hot, mo, mrow, mr, wg, wu, wd, ag, gate, up, unmixed, stage, loads, flows, keeps,
    zs, zr, ts, tr, xs, xr, ys, yr,
):
    place, sends = Place(), Sends()
    pc = place
    greet(place, zn)
    tok, width = norm_ref.shape
    slots = zn * cap
    rows = PLANE * slots
    chunks = width // chunk
    hidden = wd.shape[0]
    fetch = [
        pltpu.make_async_copy(src, dst, loads.at[i])
        for i, (src, dst) in enumerate(((down_hbm, wd), (gate_hbm, wg), (up_hbm, wu)))
    ]
    parts = [
        pltpu.make_async_copy(
            ag_hbm.at[:, :, pl.ds(c * chunk, chunk)], ag.at[c % 2], loads.at[3 + c % 2]
        )
        for c in range(chunks)
    ]
    n = RowPush(place, sends, zn, norm_ref, nb, chunk, zs, zr)
    n.own(0)
    send_slots(place, sends, zn, mix_ref, mo, ts, tr)
    fetch[0].start()
    parts[0].start()
    if chunks > 1:
        parts[1].start()
    fetch[1].start()
    fetch[2].start()
    n.keep()
    make_hot(zn, cap, tok, slots_ref, hot)
    take_slots(place, zn, mix_ref, mo, tr)

    def mixes(p, carry):
        row = jnp.concatenate([mo[z, pl.ds(p, 1), :] for z in range(zn)], axis=1)
        high = row.astype(bf16)
        rest = row - high.astype(f32)
        middle = rest.astype(bf16)
        low = (rest - middle.astype(f32)).astype(bf16)
        zero = jnp.zeros((13, zn * tok), bf16)
        got = nt_dot(jnp.concatenate([high, middle, low, zero], axis=0), hot[p])
        mrow[p] = jnp.sum(got, axis=0, keepdims=True)
        return carry

    lax.fori_loop(0, PLANE, mixes, 0)
    for k in range(1, PLANE):
        p = pc.by(k)
        sends.start(mrow.at[p], mr.at[pc.p], ys.at[k], yr.at[k], pc.at(pc.z, p))
    mr[pc.p] = mrow[pc.p]
    if chunks > 1:
        n.own(1)
    fetch[0].wait()
    give = PlaneSend(place, sends, hot, nb, sn, an_ref, chunk, xs, xr)
    half = PLANE // 2

    def back_through(c):
        cols = pl.ds(c * chunk, chunk)
        parts[c].wait()

        def body(i, carry):
            at = pl.ds(i * half, half)
            got = nt_dot(ag[c % 2, at].reshape(half * slots, chunk), wd[:, cols])
            got = got.reshape(half, slots, hidden)
            unmixed[at] = got if c == 0 else unmixed[at] + got
            return carry

        lax.fori_loop(0, 2, body, 0)
        if c + 2 < chunks:
            parts[c + 2].start()

    for c in range(chunks):
        n.take(c)
        if c + 2 < chunks:
            n.own(c + 2)
        give.send(c)
        back_through(c)

    lane = lax.broadcasted_iota(jnp.int32, (tok, rows), 1).astype(f32)

    def tables(z, carry):
        zero = jnp.zeros((120, tok), f32)
        have = jnp.concatenate([slots_ref[z], zero], axis=0).T
        mixed = jnp.concatenate([mo[z], zero], axis=0).T
        one = jnp.zeros((tok, rows), f32)
        mix = jnp.zeros((tok, rows), f32)
        base = (z * cap).astype(f32)
        for p in range(PLANE):
            col = have[:, p : p + 1]
            hit = lane == jnp.where(col < 0, -1.0, col + base + float(p * slots))
            one = jnp.where(hit, 1.0, one)
            mix = jnp.where(hit, mixed[:, p : p + 1], mix)
        stage[0] = one.astype(bf16)
        stage[1] = mix.astype(bf16)
        at = pl.ds(pl.multiple_of(z * tok, tok), tok)
        out = [
            pltpu.make_async_copy(stage.at[i], dst.at[at, :], flows.at[i])
            for i, dst in enumerate((hot_t_hbm, comb_hbm))
        ]
        for copy in out:
            copy.start()
        for copy in out:
            copy.wait()
        return carry

    lax.fori_loop(0, zn, tables, 0)
    fetch[1].wait()
    fetch[2].wait()
    saves = []
    for c in range(chunks):
        cols = pl.ds(c * chunk, chunk)
        give.take(c)
        save = pltpu.make_async_copy(an_ref.at[:, :, cols], an_hbm.at[:, :, cols], keeps.at[PLANE + c])
        save.start()
        saves.append(save)

        def into(i, carry):
            at = pl.ds(i * half, half)
            lhs = an_ref[at, :, cols].reshape(half * slots, chunk)
            for weight, acc in ((wg, gate), (wu, up)):
                got = nn_dot(lhs, weight[cols, :]).reshape(half, slots, hidden)
                acc[at] = got if c == 0 else acc[at] + got
            return carry

        lax.fori_loop(0, 2, into, 0)
    for k in range(1, PLANE):
        arrived(mr.at[pc.by(k)], yr.at[k])
    place_lane = lax.broadcasted_iota(jnp.int32, (slots, 128), 1)
    r = lax.broadcasted_iota(jnp.int32, (slots, slots), 0)
    s = lax.broadcasted_iota(jnp.int32, (slots, slots), 1)

    def acts(p, carry):
        mix = jnp.sum(jnp.where(r == s, mr[p], 0.0), axis=1, keepdims=True)
        g, u, d = gate[p], up[p], unmixed[p]
        sig = jax.nn.sigmoid(g)
        act = g * sig
        inner = (act * u).astype(bf16)
        mid_ref[0, p] = inner
        wide = inner.astype(f32)
        mid_ref[1, p] = (wide * mix).astype(bf16)
        dots = mix * jnp.sum(d * wide, axis=1, keepdims=True)
        high = dots.astype(bf16).astype(f32)
        dot = jnp.where(place_lane == pc.p, high, 0.0)
        dot = jnp.where(place_lane == pc.p + PLANE, dots - high, dot)
        dot_ref[p] = dot.astype(bf16)
        d = d * mix
        mid_ref[2, p] = (d * u * sig * (1.0 + g * (1.0 - sig))).astype(bf16)
        mid_ref[3, p] = (d * act).astype(bf16)
        pltpu.make_async_copy(mid_ref.at[:, p], mid_hbm.at[:, p], keeps.at[p]).start()
        return carry

    lax.fori_loop(0, PLANE, acts, 0)
    for p in range(PLANE):
        saves.append(pltpu.make_async_copy(mid_ref.at[:, p], mid_hbm.at[:, p], keeps.at[p]))
    for save in saves:
        save.wait()
    sends.finish()


def there(zn, cap, norm, slots_all, mix, ag, gate, up, down, chunk=512):
    tok, width = norm.shape
    slots = zn * cap
    hidden = down.shape[0]
    chunks = width // chunk
    shape = jax.ShapeDtypeStruct
    vmem = pltpu.VMEM
    return pl.pallas_call(
        functools.partial(there_kernel, zn, cap, chunk),
        out_shape=(
            shape((PLANE, slots, 128), bf16),
            shape((PLANE, slots, width), bf16),
            shape((4, PLANE, slots, hidden), bf16),
            shape((zn * tok, PLANE * slots), bf16),
            shape((zn * tok, PLANE * slots), bf16),
        ),
        in_specs=[VSPEC] * 3 + [ASPEC] * 4,
        out_specs=(VSPEC,) + (ASPEC,) * 4,
        scratch_shapes=[
            vmem((PLANE, slots, width), bf16),
            vmem((4, PLANE, slots, hidden), bf16),
            vmem((zn, tok, width), bf16),
            vmem((PLANE, slots, width), bf16),
            vmem((PLANE, slots, zn * tok), bf16),
            vmem(mix.shape, f32),
            vmem((PLANE, 1, slots), f32),
            vmem((PLANE, 1, slots), f32),
            vmem(gate.shape, bf16),
            vmem(up.shape, bf16),
            vmem(down.shape, bf16),
            vmem((2, PLANE, slots, chunk), bf16),
            vmem((PLANE, slots, hidden), f32),
            vmem((PLANE, slots, hidden), f32),
            vmem((PLANE, slots, hidden), f32),
            vmem((2, tok, PLANE * slots), bf16),
            dma_sems(5),
            dma_sems(2),
            dma_sems(PLANE + chunks),
            dma_sems(chunks, zn),
            dma_sems(chunks, zn),
            dma_sems(zn),
            dma_sems(zn),
            dma_sems(chunks, PLANE),
            dma_sems(chunks, PLANE),
            dma_sems(PLANE),
            dma_sems(PLANE),
        ],
        compiler_params=params(3),
        name="there",
    )(norm, slots_all, mix, ag, gate, up, down)


def back_kernel(
    zn, chunk, dot_ref, hot_ref, mid_hbm, an_hbm, ag_hbm, gate_hbm, up_hbm, down_hbm,
    dots_ref, ap_hbm, res_hbm, gg_hbm, ug_hbm, dg_hbm, rr_hbm,
    mids, an, ag, wg, wu, wd, pb, rp, rd, zd, zp, wide, tall, flat,
    loads, flows, xs, xr, ds, dr, zs, zr, es, er, os, vs, vr,
):
    place, sends = Place(), Sends()
    pc = place
    fetch = [
        pltpu.make_async_copy(src, dst, loads.at[i])
        for i, (src, dst) in enumerate(
            (
                (gate_hbm, wg), (up_hbm, wu), (mid_hbm.at[2], mids.at[2]), (mid_hbm.at[3], mids.at[3]),
                (mid_hbm.at[0], mids.at[0]), (down_hbm, wd), (mid_hbm.at[1], mids.at[1]), (ag_hbm, ag),
                (an_hbm, an),
            )
        )
    ]
    for copy in fetch:
        copy.start()
    greet(place, zn)
    _, slots, width = pb.shape
    hidden = wd.shape[0]
    chunks = width // chunk
    tok = dots_ref.shape[1]
    far = [(pc.z + k) % zn for k in range(1, zn)]
    half = PLANE // 2
    for k in range(1, PLANE):
        p = pc.by(k)
        sends.start(dot_ref.at[p], rd.at[pc.p], ds.at[k], dr.at[k], pc.at(pc.z, p))
    for copy in fetch[:4]:
        copy.wait()
    def pair_chunk(c):
        cols = pl.ds(c * chunk, chunk)

        def pair(i, carry):
            at = pl.ds(i * half, half)
            got = nt_dot(mids[2, at].reshape(half * slots, hidden), wg[cols, :])
            got = got + nt_dot(mids[3, at].reshape(half * slots, hidden), wu[cols, :])
            pb[at, :, cols] = got.astype(bf16).reshape(half, slots, chunk)
            return carry

        lax.fori_loop(0, 2, pair, 0)
        rp[pc.p, :, cols] = pb[pc.p, :, cols]

    def pair_send(c):
        cols = pl.ds(c * chunk, chunk)
        for k in range(1, PLANE):
            p = pc.by(k)
            sends.start(
                pb.at[p, :, cols], rp.at[pc.p, :, cols], xs.at[c, k], xr.at[c, k], pc.at(pc.z, p)
            )

    for c in range(chunks):
        pair_chunk(c)
        if c < 2:
            pair_send(c)
    rd[pc.p] = dot_ref[pc.p]
    for k in range(1, PLANE):
        arrived(rd.at[pc.by(k)], dr.at[k])
    zd[...] = nn_dot(hot_ref[...], rd[...].reshape(PLANE * slots, 128)).reshape(zn, tok, 128)
    for k, d in enumerate(far):
        sends.start(zd.at[d], dots_ref.at[pc.z], es.at[k], er.at[pc.z], pc.at(d, pc.p))
    dots_ref[pc.z] = zd[pc.z]

    flow_r, flow_g, flow_u, flow_d = (
        Flow(buf, flows.at[i]) for i, buf in enumerate((wide, tall.at[0], tall.at[1], flat))
    )
    keeps = []

    def result(c):
        cols = pl.ds(c * chunk, chunk)
        slot = flow_r.slot()

        def body(i, carry):
            at = pl.ds(i * half, half)
            got = nn_dot(mids[0, at].reshape(half * slots, hidden), wd[:, cols])
            wide[slot, at] = got.astype(bf16).reshape(half, slots, chunk)
            return carry

        lax.fori_loop(0, 2, body, 0)
        flow_r.send(res_hbm.at[:, :, cols])

    def down_grad(i):
        m = pl.ds(i * 128, 128)
        slot = flow_d.slot()
        lhs = mids[1, :, :, m].reshape(PLANE * slots, 128)

        def body(j, carry):
            cols = pl.ds(pl.multiple_of(j * chunk, chunk), chunk)
            got = tn_dot(lhs, ag[:, :, cols].reshape(PLANE * slots, chunk))
            flat[slot, :, cols] = got.astype(bf16)
            return carry

        lax.fori_loop(0, chunks, body, 0)
        flow_d.send(dg_hbm.at[m, :])

    def gate_up_grad(i):
        m = pl.ds(i * 256, 256)
        lhs = an[:, :, m].reshape(PLANE * slots, 256)
        for which, flow, dst in ((0, flow_g, gg_hbm), (1, flow_u, ug_hbm)):
            slot = flow.slot()
            rhs = mids[2 + which].reshape(PLANE * slots, hidden)
            tall[which, slot] = tn_dot(lhs, rhs).astype(bf16)
            flow.send(dst.at[m, :])

    def combine(c):
        cols = pl.ds(c * chunk, chunk)
        for k in range(1, PLANE):
            arrived(rp.at[pc.by(k), :, cols], xr.at[c, k])
        if c + 2 < chunks:
            pair_send(c + 2)
        if c == chunks - 1:
            flow_r.finish()
            for k in range(1, PLANE):
                p = pc.by(k)
                sends.start(
                    res_hbm.at[p, :, pl.ds(0, chunk)],
                    rr_hbm.at[pc.p],
                    vs.at[k],
                    vr.at[k],
                    pc.at(pc.z, p),
                )
        got = nn_dot(hot_ref[...], rp[:, :, cols].reshape(PLANE * slots, chunk))
        zp[:, :, cols] = got.astype(bf16).reshape(zn, tok, chunk)
        for k, d in enumerate(far):
            sends.start(
                zp.at[d, :, cols],
                ap_hbm.at[pc.z, :, cols],
                zs.at[c, k],
                zr.at[c, pc.z],
                pc.at(d, pc.p),
            )
        keep = pltpu.make_async_copy(zp.at[pc.z, :, cols], ap_hbm.at[pc.z, :, cols], os.at[c])
        keep.start()
        keeps.append(keep)

    for copy in fetch[4:6]:
        copy.wait()
    for c in range(chunks):
        result(c)
    for copy in fetch[6:]:
        copy.wait()
    work = [functools.partial(down_grad, i) for i in range(hidden // 128)]
    work += [functools.partial(gate_up_grad, i) for i in range(width // 256)]
    share = -(-len(work) // chunks)
    for c in range(chunks):
        for item in work[c * share : (c + 1) * share]:
            item()
        combine(c)
    for c in range(chunks):
        for d in far:
            arrived(ap_hbm.at[d, :, pl.ds(c * chunk, chunk)], zr.at[c, d])
    for keep in keeps:
        keep.wait()
    for k in range(1, PLANE):
        arrived(rr_hbm.at[pc.by(k)], vr.at[k])
    for d in far:
        arrived(dots_ref.at[d], er.at[d])
    for flow in (flow_r, flow_g, flow_u, flow_d):
        flow.finish()
    sends.finish()


def back_rows(zn, tok, dots, hot, mids, an, ag, gate, up, down, chunk=512):
    _, slots, width = an.shape
    hidden = down.shape[0]
    chunks = width // chunk
    shape = jax.ShapeDtypeStruct
    vmem = pltpu.VMEM
    return pl.pallas_call(
        functools.partial(back_kernel, zn, chunk),
        out_shape=(
            shape((zn, tok, 128), f32),
            shape((zn, tok, width), bf16),
            shape((PLANE, slots, width), bf16),
            shape(gate.shape, bf16),
            shape(up.shape, bf16),
            shape(down.shape, bf16),
            shape((PLANE, slots, chunk), bf16),
        ),
        in_specs=[VSPEC] * 2 + [ASPEC] * 6,
        out_specs=(VSPEC,) + (ASPEC,) * 6,
        scratch_shapes=[
            vmem((4, PLANE, slots, hidden), bf16),
            vmem((PLANE, slots, width), bf16),
            vmem((PLANE, slots, width), bf16),
            vmem(gate.shape, bf16),
            vmem(up.shape, bf16),
            vmem(down.shape, bf16),
            vmem((PLANE, slots, width), bf16),
            vmem((PLANE, slots, width), bf16),
            vmem((PLANE, slots, 128), bf16),
            vmem((zn, tok, 128), f32),
            vmem((zn, tok, width), bf16),
            vmem((2, PLANE, slots, chunk), bf16),
            vmem((2, 2, 256, hidden), bf16),
            vmem((2, 128, width), bf16),
            dma_sems(9),
            dma_sems(4, 2),
            dma_sems(chunks, PLANE),
            dma_sems(chunks, PLANE),
            dma_sems(PLANE),
            dma_sems(PLANE),
            dma_sems(chunks, zn),
            dma_sems(chunks, zn),
            dma_sems(zn),
            dma_sems(zn),
            dma_sems(chunks),
            dma_sems(PLANE),
            dma_sems(PLANE),
        ],
        compiler_params=params(4),
        name="back_rows",
    )(dots, hot, mids, an, ag, gate, up, down)


class ColumnReduce:
    def __init__(self, place, sends, zn, part, buf, ss_r, ss_l, rs_r, rs_l):
        self.place, self.sends, self.zn = place, sends, zn
        self.part, self.buf = part, buf
        self.ss_r, self.ss_l, self.rs_r, self.rs_l = ss_r, ss_l, rs_r, rs_l

    def _hop(self, slot, rs, ss, d, start, inner, device):
        rows = self.part.shape[1]

        def add():
            arrived(self.buf.at[slot], rs.at[d])

            def put(at, v):
                self.buf[slot, at, :] = v.astype(bf16)

            add_rows(put, lambda at: self.part[d, at, :], lambda at: self.buf[slot, at, :], rows)

        both = jnp.logical_and(start, inner)
        pl.when(both)(add)
        self.sends.start(
            self.buf.at[slot], self.buf.at[slot], ss.at[d], rs.at[d], device, both
        )
        self.sends.start(
            self.part.at[d],
            self.buf.at[slot],
            ss.at[d],
            rs.at[d],
            device,
            jnp.logical_and(start, jnp.logical_not(inner)),
        )

    def step(self, k):
        pc, zn = self.place, self.zn
        d = zn - 1 - k
        right = pc.at(jnp.minimum(pc.z + 1, zn - 1), pc.p)
        left = pc.at(jnp.maximum(pc.z - 1, 0), pc.p)
        self._hop(d + 1, self.rs_r, self.ss_r, d, pc.z < d, pc.z > 0, right)
        d = k
        self._hop(d, self.rs_l, self.ss_l, d, pc.z > d, pc.z < zn - 1, left)

    def own(self, use, step=32):
        pc, zn = self.place, self.zn
        lower, upper = pc.z > 0, pc.z < zn - 1
        arrived(self.buf.at[pc.z + 1], self.rs_r.at[pc.z], lower)
        arrived(self.buf.at[pc.z], self.rs_l.at[pc.z], upper)

        def body(i, carry):
            at = pl.ds(pl.multiple_of(i * step, step), step)
            v = self.part[pc.z, at, :].astype(f32)
            v = v + jnp.where(lower, self.buf[pc.z + 1, at, :].astype(f32), 0.0)
            v = v + jnp.where(upper, self.buf[pc.z, at, :].astype(f32), 0.0)
            use(at, v)
            return carry

        lax.fori_loop(0, self.part.shape[1] // step, body, 0)


class SmallSum:
    @staticmethod
    def scratch(zn, rows, lanes):
        return [
            pltpu.VMEM((PLANE, rows, lanes), f32),
            pltpu.VMEM((rows, lanes), f32),
            pltpu.VMEM((zn, rows, lanes), f32),
            dma_sems(PLANE),
            dma_sems(PLANE),
            dma_sems(zn),
            dma_sems(zn),
            dma_sems(PLANE),
            dma_sems(PLANE),
        ]

    def __init__(self, place, sends, zn, flat, out, scratch):
        self.place, self.sends, self.zn, self.flat, self.out = place, sends, zn, flat, out
        self.l1, self.mid, self.l2, self.a, self.ar, self.b, self.br, self.c, self.cr = scratch

    def first(self):
        pc = self.place
        for k in range(1, PLANE):
            p = pc.by(k)
            self.sends.start(
                self.flat.at[p], self.l1.at[pc.p], self.a.at[k], self.ar.at[k], pc.at(pc.z, p)
            )
        self.l1[pc.p] = self.flat[pc.p]

    def second(self):
        pc, zn = self.place, self.zn
        for k in range(1, PLANE):
            arrived(self.l1.at[pc.by(k)], self.ar.at[k])
        total = self.l1[0]
        for k in range(1, PLANE):
            total = total + self.l1[k]
        self.mid[...] = total
        self.l2[pc.z] = total
        for k in range(1, zn):
            d = (pc.z + k) % zn
            self.sends.start(
                self.mid, self.l2.at[pc.z], self.b.at[k], self.br.at[pc.z], pc.at(d, pc.p)
            )

    def _column(self):
        pc, zn = self.place, self.zn
        for k in range(1, zn):
            d = (pc.z + k) % zn
            arrived(self.l2.at[d], self.br.at[d])
        total = self.l2[0]
        for z in range(1, zn):
            total = total + self.l2[z]
        return total

    def third(self):
        pc = self.place
        self.out[pc.p] = self._column()
        for k in range(1, PLANE):
            p = pc.by(k)
            self.sends.start(
                self.out.at[pc.p], self.out.at[pc.p], self.c.at[k], self.cr.at[k], pc.at(pc.z, p)
            )

    def last(self):
        pc = self.place
        for k in range(1, PLANE):
            arrived(self.out.at[pc.by(k)], self.cr.at[k])


class TinySum:
    @staticmethod
    def scratch(zn, lanes):
        return [
            pltpu.VMEM((1, lanes), f32),
            pltpu.VMEM((PLANE, 1, lanes), f32),
            pltpu.VMEM((1, lanes), f32),
            pltpu.VMEM((zn, 1, lanes), f32),
            dma_sems(PLANE),
            dma_sems(PLANE),
            dma_sems(zn),
            dma_sems(zn),
        ]

    def __init__(self, place, sends, zn, out, scratch):
        self.place, self.sends, self.zn, self.out = place, sends, zn, out
        self.vec, self.l1, self.mid, self.l2, self.a, self.ar, self.b, self.br = scratch

    def first(self):
        pc = self.place
        for k in range(1, PLANE):
            p = pc.by(k)
            self.sends.start(
                self.vec, self.l1.at[pc.p], self.a.at[k], self.ar.at[k], pc.at(pc.z, p)
            )
        self.l1[pc.p] = self.vec[...]

    def second(self):
        pc, zn = self.place, self.zn
        for k in range(1, PLANE):
            arrived(self.l1.at[pc.by(k)], self.ar.at[k])
        total = self.l1[0]
        for k in range(1, PLANE):
            total = total + self.l1[k]
        self.mid[...] = total
        self.l2[pc.z] = total
        for k in range(1, zn):
            d = (pc.z + k) % zn
            self.sends.start(
                self.mid, self.l2.at[pc.z], self.b.at[k], self.br.at[pc.z], pc.at(d, pc.p)
            )

    def last(self):
        pc, zn = self.place, self.zn
        for k in range(1, zn):
            d = (pc.z + k) % zn
            arrived(self.l2.at[d], self.br.at[d])
        total = self.l2[0]
        for z in range(1, zn):
            total = total + self.l2[z]
        self.out[...] = total


class Result:
    def __init__(self, place, sends, zn, res, first, comb, rr, am, rbuf, zbuf, chunk, xs, xr, zs, zr, ls, os):
        self.place, self.sends, self.zn, self.res, self.comb = place, sends, zn, res, comb
        self.rr, self.am, self.rbuf, self.zbuf, self.chunk = rr, am, rbuf, zbuf, chunk
        self.xs, self.xr, self.zs, self.zr, self.ls, self.os = xs, xr, zs, zr, ls, os
        self.early = first
        self.flight = {}

    def first(self, c):
        pc = self.place
        cols = pl.ds(c * self.chunk, self.chunk)
        for k in range(1, PLANE):
            p = pc.by(k)
            self.sends.start(
                self.res.at[p, :, cols],
                self.rr.at[pc.p, :, cols],
                self.xs.at[c, k],
                self.xr.at[c, k],
                pc.at(pc.z, p),
            )

    def mix(self, c, chunks):
        pc, zn = self.place, self.zn
        cols = pl.ds(c * self.chunk, self.chunk)
        own = pltpu.make_async_copy(self.res.at[pc.p, :, cols], self.rbuf.at[pc.p], self.ls.at[0])
        own.start()
        copies = []
        for k in range(1, PLANE):
            p = pc.by(k)
            if c:
                arrived(self.rr.at[p, :, cols], self.xr.at[c, k])
            src = self.rr.at[p, :, cols] if c else self.early.at[p]
            copy = pltpu.make_async_copy(src, self.rbuf.at[p], self.ls.at[k])
            copy.start()
            copies.append(copy)
        if c == 1:
            for later in range(2, chunks):
                self.first(later)
        own.wait()
        for copy in copies:
            copy.wait()
        self.settle(c - 2)
        slot = c % 2
        _, slots, chunk = self.rbuf.shape
        tok = self.zbuf.shape[2]
        unit = min(512, zn * tok)
        per = unit // tok
        rows = self.rbuf[...].reshape(PLANE * slots, chunk)
        for i in range(zn * tok // unit):
            got = nn_dot(self.comb[i * unit : (i + 1) * unit, :], rows)
            self.zbuf[slot, i * per : (i + 1) * per] = got.astype(bf16).reshape(per, tok, chunk)
        flight = []
        for k in range(1, zn):
            d = (pc.z + k) % zn
            flight.append(
                pltpu.make_async_remote_copy(
                    src_ref=self.zbuf.at[slot, d],
                    dst_ref=self.am.at[pc.z, :, cols],
                    send_sem=self.zs.at[c, k],
                    recv_sem=self.zr.at[c, pc.z],
                    device_id=pc.at(d, pc.p),
                    device_id_type=MESH,
                )
            )
        for copy in flight:
            copy.start()
        keep = pltpu.make_async_copy(
            self.zbuf.at[slot, pc.z], self.am.at[pc.z, :, cols], self.os.at[c]
        )
        keep.start()
        self.flight[c] = (flight, keep)

    def settle(self, c):
        if c in self.flight:
            flight, keep = self.flight.pop(c)
            for copy in flight:
                copy.wait_send()
            keep.wait()

    def last(self, chunks):
        pc, zn = self.place, self.zn
        for c in range(chunks):
            self.settle(c)
            for k in range(1, zn):
                d = (pc.z + k) % zn
                arrived(self.am.at[d, :, pl.ds(c * self.chunk, self.chunk)], self.zr.at[c, d])


def rear_kernel(
    zn, chunk, heads, starts_ref,
    mid_ref, tok_ref, gain_ref, hg_ref, flat_ref, comb_ref,
    res_hbm, early_hbm, seq_hbm, wq_hbm, wo_hbm, pre_hbm, rot_hbm, val_hbm, lse_hbm, ctx_hbm, tab_hbm,
    grad_ref, oq_ref, oo_ref, sum_ref, tiny_ref, am_hbm, rr_hbm,
    big, wq, wo, pre, rot, val, lse, ctx, tab, bias,
    lse_t, del_t, key_t, cback, aback, dk, dv, dgain,
    gq, bq, vq, tq, go, bo, vo, to,
    c1, s1, ra, rb, last, rbuf, zbuf,
    gs, gr, hs, hr, sr, sl, rr, rl, ps, pr, xs, xr, zs, zr, ls, os, loads,
    *rest,
):
    place, sends = Place(), Sends()
    pc = place
    small_scratch, tiny_scratch = rest[:9], rest[9:]
    tok, width = mid_ref.shape
    length = PLANE * tok
    half = heads * HD
    own_rows = wq.shape[1]
    chunks = width // chunk
    scale = HD ** (-0.5)
    greet(place, zn)
    pairs = (
        (wo_hbm, wo), (ctx_hbm, ctx), (rot_hbm, rot), (val_hbm, val), (lse_hbm, lse),
        (pre_hbm, pre), (tab_hbm, tab), (wq_hbm, wq),
    )
    fetch = [pltpu.make_async_copy(a, b, loads.at[i]) for i, (a, b) in enumerate(pairs)]
    small = SmallSum(place, sends, zn, flat_ref, sum_ref, small_scratch)
    tiny = TinySum(place, sends, zn, tiny_ref, tiny_scratch)
    row_sends = Sends()
    rows = PlaneGather(place, row_sends, big, gs, gr)
    result = Result(
        place, sends, zn, res_hbm, early_hbm, comb_ref, rr_hbm, am_hbm, rbuf, zbuf, chunk, xs, xr, zs, zr, ls, os
    )
    o = ColumnReduce(place, sends, zn, go, bo, sr.at[1], sl.at[1], rr.at[1], rl.at[1])
    q = ColumnReduce(place, sends, zn, gq, bq, sr.at[0], sl.at[0], rr.at[0], rl.at[0])

    def stage(i, carry):
        at = pl.ds(pl.multiple_of(i * 32, 32), 32)
        big[pc.p, at, :] = mid_ref[at, :].astype(bf16)
        return carry

    lax.fori_loop(0, tok // 32, stage, 0)
    rows.first()
    rows.along()
    for copy in fetch:
        copy.start()
    small.first()
    rows.second()
    rows.third()
    result.mix(0, chunks)
    for copy in fetch[:5]:
        copy.wait()
    key_t[...] = rot[heads].astype(f32).T.astype(bf16)
    lse_t[...] = lse[...].T
    small.second()
    rows.last()
    if chunks > 1:
        result.first(1)

    order = []
    for k in range(zn):
        for d in (zn - 1 - k, k):
            if d not in order:
                order.append(d)

    def output_grad(d):
        cols = pl.ds(d * 2 * own_rows, 2 * own_rows)
        rhs = big[:, :, cols].reshape(length, 2 * own_rows)

        def body(i, carry):
            m = pl.ds(pl.multiple_of(i * 256, 256), 256)
            go[d, m, :] = tn_dot(ctx[:, m], rhs).astype(bf16)
            return carry

        lax.fori_loop(0, half // 256, body, 0)

    made = 0
    for k in range(1):
        while made < len(order) and not {zn - 1 - k, k} <= set(order[:made]):
            output_grad(order[made])
            made += 1
        o.step(k)

    def context_back(i, carry):
        at = pl.ds(pl.multiple_of(i * 2 * tok, 2 * tok), 2 * tok)
        lhs = big[pl.ds(2 * i, 2)].reshape(2 * tok, width)
        got = nn_dot(lhs, wo[...].reshape(width, half))
        cback[at, :] = got.astype(bf16)
        prod = got.astype(bf16).astype(f32) * ctx[at, :].astype(f32)
        for h in range(heads):
            s = jnp.sum(prod[:, h * HD : (h + 1) * HD], axis=1, keepdims=True)
            lse[at, h : h + 1] = s
        return carry

    lax.fori_loop(0, PLANE // 2, context_back, 0)
    while made < len(order):
        output_grad(order[made])
        made += 1
    del_t[...] = lse[...].T
    row_sends.finish()
    fill = pltpu.make_async_copy(seq_hbm, big, loads.at[len(pairs)])
    fill.start()
    small.third()
    dk[...] = jnp.zeros_like(dk)
    dv[...] = jnp.zeros_like(dv)
    dgain[...] = jnp.zeros_like(dgain)
    for copy in fetch[5:]:
        copy.wait()

    def norm_of(d, at, h, gain_row):
        d = d * tab[0, at, :] - turned(d) * tab[1, at, :]
        v = pre[at, pl.ds(h * HD if isinstance(h, int) else pl.multiple_of(h * HD, HD), HD)]
        r = rms_scale(v)
        hat = v * r
        s = d * hg_ref[pl.ds(gain_row, 1), :]
        got = r * (s - hat * jnp.mean(s * hat, axis=1, keepdims=True))
        dgain[pl.ds(gain_row, 1), :] += jnp.sum(d * hat, axis=0, keepdims=True)
        return got.astype(bf16)

    starts = [starts_ref[pc.z, j] for j in range(starts_ref.shape[1])]

    def attend(i):
        limit = key_limit(i, length)
        at = slice(i * QBLOCK, (i + 1) * QBLOCK)
        bias[:limit, :] = bias_block(starts, i * QBLOCK, limit, True)

        def body(h, carry):
            cols = pl.ds(pl.multiple_of(h * HD, HD), HD)
            query = rot[h, at, :]
            dctx = cback[at, cols]
            scores = nt_dot(rot[heads, :limit, :], query) * scale
            scores = scores + bias[:limit, :]
            probs = jnp.exp(scores - lse_t[pl.ds(h, 1), at])
            dprobs = nt_dot(val[:limit, :], dctx)
            dscores = (probs * (dprobs - del_t[pl.ds(h, 1), at])).astype(bf16)
            dv[:limit, :] += nn_dot(probs.astype(bf16), dctx)
            dk[:limit, :] += nn_dot(dscores, query)
            dq = nn_dot(key_t[:, :limit], dscores).T * scale
            aback[at, cols] = norm_of(dq, at, h, 0)
            return carry

        lax.fori_loop(0, heads, body, 0, unroll=2)

    for i in range(length // QBLOCK):
        attend(i)

    def keys(i, carry):
        at = pl.ds(pl.multiple_of(i * 256, 256), 256)
        aback[at, half : half + HD] = norm_of(dk[at, :] * scale, at, heads, 1)
        aback[at, half + HD : half + 2 * HD] = dv[at, :].astype(bf16)
        return carry

    if chunks > 1:
        result.mix(1, chunks)
    lax.fori_loop(0, length // 256, keys, 0)
    fill.wait()

    def query_grad(d):
        for h in range(2):
            cols = pl.ds((2 * d + h) * own_rows, own_rows) if own_rows % 128 == 0 else None
            if cols is None:
                lhs = big[:, :, pl.ds(2 * d * own_rows, 2 * own_rows)]
                lhs = lhs.reshape(length, 2 * own_rows)
                if h == 0:
                    gq[d] = tn_dot(lhs, aback[...]).astype(bf16)
            else:
                lhs = big[:, :, cols].reshape(length, own_rows)
                gq[d, h * own_rows : (h + 1) * own_rows, :] = tn_dot(lhs, aback[...]).astype(bf16)

    made = 0
    for k in range(zn - 1):
        while made < len(order) and not {zn - 1 - k, k} <= set(order[:made]):
            query_grad(order[made])
            made += 1
        if k == 0:
            q.step(0)
            if zn > 2:
                o.step(1)
    while made < len(order):
        query_grad(order[made])
        made += 1

    mixed = min(2, chunks)
    red = PlaneReduce(
        place, sends, big, grad_ref, (c1, s1, ra, rb, last), hs, hr, pl.ds(0, width)
    )

    def norm1_part(k):
        y, x, j = red.chip(*red.chips[k])
        lhs = aback[pl.ds(pl.multiple_of(j * 2 * tok, 2 * tok), 2 * tok), :]

        def body(i, carry):
            cols = pl.ds(pl.multiple_of(i * chunk, chunk), chunk)
            e = i * (chunk // own_rows)
            rhs = wq[pl.ds(e, chunk // own_rows)].reshape(chunk, half + 2 * HD)
            big[pl.ds(j * 2, 2), :, cols] = nt_dot(lhs, rhs).astype(bf16).reshape(2, tok, chunk)
            return carry

        lax.fori_loop(0, width // chunk, body, 0)

    for k in range(4):
        norm1_part(k)
        red.first(k)
    for j in range(4):
        red.second(j)
    for k in range(1, zn - 1):
        q.step(k)
        if k + 1 < zn - 1:
            o.step(k + 1)
        if k == 1:
            red.third()
        if mixed < chunks:
            result.mix(mixed, chunks)
            mixed += 1
    def split_o(at, v):
        first, second = v[:, :own_rows], v[:, own_rows:]
        low = pc.y == 0
        vo[at, :] = jnp.where(low, second, first).astype(bf16)
        oo_ref[pc.y, at, :] = jnp.where(low, first, second)

    o.own(split_o)
    sends.start(vo, to, ps.at[1], pr.at[1], pc.peer(dy=1))
    if zn <= 2:
        red.third()
    red.finish()

    def tokens_back(i, carry):
        at = pl.ds(pl.multiple_of(i * 16, 16), 16)
        v = tok_ref[at, :].astype(f32)
        r = rms_scale(v)
        hat = v * r
        d = grad_ref[at, :]
        s = d * gain_ref[...]
        got = r * (s - hat * jnp.mean(s * hat, axis=1, keepdims=True))
        grad_ref[at, :] = mid_ref[at, :] + got
        return carry + jnp.sum(d * hat, axis=0, keepdims=True)

    total = lax.fori_loop(0, tok // 16, tokens_back, jnp.zeros((1, width), f32))
    tiny.vec[:, :width] = total
    tiny.vec[:, width : width + HD] = dgain[0:1, :]
    tiny.vec[:, width + HD : width + 2 * HD] = dgain[1:2, :]
    tiny.first()
    while mixed < chunks:
        result.mix(mixed, chunks)
        mixed += 1

    tiny.second()
    q_own(q, pc, zn, gq, bq, vq, oq_ref, own_rows)
    sends.start(vq, tq, ps.at[0], pr.at[0], pc.peer(dy=1))
    tiny.last()
    small.last()
    result.last(chunks)
    arrived(to, pr.at[1])
    oo_ref[1 - pc.y] = to[...].astype(f32)
    arrived(tq, pr.at[0])
    oq_ref[1 - pc.y] = tq[...].astype(f32)
    sends.finish()


def q_own(q, pc, zn, part, buf, give, out, rows, step=32):
    lower, upper = pc.z > 0, pc.z < zn - 1
    arrived(buf.at[pc.z + 1], q.rs_r.at[pc.z], lower)
    arrived(buf.at[pc.z], q.rs_l.at[pc.z], upper)

    def total(at):
        v = part[pc.z, at, :].astype(f32)
        v = v + jnp.where(lower, buf[pc.z + 1, at, :].astype(f32), 0.0)
        return v + jnp.where(upper, buf[pc.z, at, :].astype(f32), 0.0)

    def body(i, carry):
        at = pl.ds(pl.multiple_of(i * step, step), step)
        theirs = pl.ds(pl.multiple_of((1 - pc.y) * rows + i * step, step), step)
        mine = pl.ds(pl.multiple_of(pc.y * rows + i * step, step), step)
        give[at, :] = total(theirs).astype(bf16)
        out[pc.y, at, :] = total(mine)
        return carry

    lax.fori_loop(0, rows // step, body, 0)


def rear(
    zn, heads, starts, middle, tokens, gain, gains, flat, comb, res, early, seq, full_q, full_o, pre, rot, val, lse,
    ctx, tables, chunk=512,
):
    tok, width = tokens.shape
    length = PLANE * tok
    e, own_rows, wide = full_q.shape
    half = heads * HD
    chunks = width // chunk
    slots = res.shape[1]
    lanes = width + 2 * HD
    shape = jax.ShapeDtypeStruct
    vmem = pltpu.VMEM
    return pl.pallas_call(
        functools.partial(rear_kernel, zn, chunk, heads),
        out_shape=(
            shape((tok, width), f32),
            shape((2, own_rows, wide), f32),
            shape((2, half, own_rows), f32),
            shape(flat.shape, f32),
            shape((1, lanes), f32),
            shape((zn, tok, width), bf16),
            shape((PLANE, slots, width), bf16),
        ),
        in_specs=[SSPEC] + [VSPEC] * 6 + [ASPEC] * 11,
        out_specs=(VSPEC,) * 5 + (ASPEC,) * 2,
        scratch_shapes=[
            vmem((PLANE, tok, width), bf16),
            vmem((e, own_rows, wide), bf16),
            vmem((e, own_rows, half), bf16),
            vmem((length, wide), f32),
            vmem((heads + 1, length, HD), bf16),
            vmem((length, HD), bf16),
            vmem((length, 128), f32),
            vmem((length, half), bf16),
            vmem((2, length, HD), f32),
            vmem((length, QBLOCK), f32),
            vmem((128, length), f32),
            vmem((128, length), f32),
            vmem((HD, length), bf16),
            vmem((length, half), bf16),
            vmem((length, wide), bf16),
            vmem((length, HD), f32),
            vmem((length, HD), f32),
            vmem((8, HD), f32),
            vmem((zn, 2 * own_rows, wide), bf16),
            vmem((zn + 1, 2 * own_rows, wide), bf16),
            vmem((own_rows, wide), bf16),
            vmem((own_rows, wide), bf16),
            vmem((zn, half, 2 * own_rows), bf16),
            vmem((zn + 1, half, 2 * own_rows), bf16),
            vmem((half, own_rows), bf16),
            vmem((half, own_rows), bf16),
        ]
        + PlaneReduce.scratch(tok, width)
        + [
            vmem((PLANE, slots, chunk), bf16),
            vmem((2, zn, tok, chunk), bf16),
            dma_sems(8),
            dma_sems(8),
            dma_sems(1, 10),
            dma_sems(1, 10),
            dma_sems(2, zn),
            dma_sems(2, zn),
            dma_sems(2, zn),
            dma_sems(2, zn),
            dma_sems(2),
            dma_sems(2),
            dma_sems(chunks, PLANE),
            dma_sems(chunks, PLANE),
            dma_sems(chunks, zn),
            dma_sems(chunks, zn),
            dma_sems(PLANE),
            dma_sems(chunks),
            dma_sems(10),
        ]
        + SmallSum.scratch(zn, flat.shape[1], flat.shape[2])
        + TinySum.scratch(zn, lanes),
        compiler_params=params(5),
        name="rear",
    )(
        starts, middle, tokens, gain, gains, flat, comb, res, early, seq, full_q, full_o, pre, rot, val, lse,
        ctx, tables,
    )


def local(
    tokens,
    out_grad,
    first_gain,
    second_gain,
    query_gain,
    key_gain,
    query_weight,
    key_weight,
    value_weight,
    output_weight,
    router_weight,
    gate_weight,
    up_weight,
    down_weight,
    expert_ids,
    router_order,
    image_starts,
):
    tok, width = tokens.shape
    zn = lax.axis_size("exp") // 2
    experts = PLANE * zn
    cap = (9 * tok * TOP + 8 * experts - 1) // (8 * experts)
    slots = zn * cap
    length = PLANE * tok
    own_rows = query_weight.shape[0]
    half = query_weight.shape[1] // 2
    heads = half // HD
    expert_axis = jnp.arange(experts, dtype=jnp.int32)
    member = jnp.any(expert_ids[:, :, None] == expert_axis[None, None, :], axis=1)
    order_here = router_order[0]
    earlier = (order_here[None, :] < order_here[:, None]).astype(bf16)
    counts = jnp.dot(earlier, member.astype(bf16), preferred_element_type=f32)
    keep = member & (counts < cap)
    slot_of = jnp.where(keep, counts, -1.0)

    resid_in = tokens.astype(f32)
    tables = jnp.asarray(rotary_tables(length))
    slot_t = slot_of.T.reshape(zn, PLANE, tok)
    gains = jnp.stack([query_gain, key_gain])
    (
        lse, attention, slots_all, seq_norm, full_q, full_o, pre, rot, value_rows, context_rows, rows_g,
    ) = front(
        zn, cap, heads, image_starts, tokens, first_gain[None], query_weight, key_weight, value_weight,
        output_weight, gains, out_grad, slot_t, tables,
    )
    resid_mid = resid_in + attention
    second_rms = rms_scale(resid_mid)
    second_hat = resid_mid * second_rms
    second_norm = (second_hat * second_gain).astype(bf16)
    logits = jnp.dot(second_norm, router_weight, preferred_element_type=f32)
    mix = jax.nn.softmax(jnp.where(member, logits, NEGATIVE), axis=-1)
    mix = jnp.where(member, mix, 0.0)
    keep_mix = jnp.where(keep, mix, 0.0)
    mix_t = keep_mix.T.reshape(zn, PLANE, tok)
    gate_w, up_w, down_w = gate_weight[0], up_weight[0], down_weight[0]
    dot_lanes, rows_n, mids, hot, comb = there(
        zn, cap, second_norm, slots_all, mix_t, rows_g, gate_w, up_w, down_w
    )
    dots_all, pairs, result, gate_grad, up_grad, down_grad, result_first = back_rows(
        zn, tok, dot_lanes, hot, mids, rows_n, rows_g, gate_w, up_w, down_w
    )
    pairs_sum = jnp.sum(pairs.astype(f32), axis=0)
    grad_out = out_grad.astype(f32)
    mix_dots = dots_all[:, :, :PLANE] + dots_all[:, :, PLANE : 2 * PLANE]
    mix_dots = mix_dots.transpose(1, 0, 2).reshape(tok, experts)
    chosen_grad = mix_dots - mix * jnp.sum(mix_dots, axis=1, keepdims=True)
    logit_grad = chosen_grad.astype(bf16)
    router_part = jnp.dot(second_norm.T, logit_grad, preferred_element_type=f32)
    norm2_back = pairs_sum + jnp.dot(logit_grad, router_weight.T, preferred_element_type=f32)
    mid_from_norm, second_gain_part = norm_back(norm2_back, second_hat, second_rms, second_gain)
    middle_grad = grad_out + mid_from_norm

    flat = jnp.concatenate([router_part.reshape(-1), second_gain_part])
    count = flat.shape[0]
    unit = PLANE * 8 * 128
    padded = -(-count // unit) * unit
    flat = jnp.pad(flat, (0, padded - count)).reshape(PLANE, padded // (PLANE * 128), 128)
    tokens_grad, sum_q, sum_o, flat, tiny, mixtures, _ = rear(
        zn, heads, image_starts, middle_grad, tokens, first_gain[None], gains, flat, comb,
        result, result_first, seq_norm, full_q, full_o, pre, rot, value_rows, lse,
        context_rows, tables,
    )
    block_out = (resid_mid + jnp.sum(mixtures.astype(f32), axis=0)).astype(bf16)
    query_grad = jnp.concatenate([sum_q[0, :, :half], sum_q[1, :, :half]], axis=1)
    kv_grad = sum_q[0, :, half:] + sum_q[1, :, half:]
    key_grad, value_grad = kv_grad[:, :HD], kv_grad[:, HD:]
    output_grad = sum_o.reshape(2 * half, own_rows)
    flat = flat.reshape(-1)
    n_router = width * experts
    router_grad = flat[:n_router].reshape(width, experts)
    second_gain_grad = flat[n_router : n_router + width]
    tiny = tiny[0]
    first_gain_grad = tiny[:width]
    query_gain_grad = tiny[width : width + HD]
    key_gain_grad = tiny[width + HD :]
    return (
        block_out,
        tokens_grad,
        first_gain_grad,
        second_gain_grad,
        query_gain_grad,
        key_gain_grad,
        query_grad,
        key_grad,
        value_grad,
        output_grad,
        router_grad,
        gate_grad[None].astype(f32),
        up_grad[None].astype(f32),
        down_grad[None].astype(f32),
    )


def solution(mesh):
    both = ("exp", "tp")
    in_specs = (
        P(both, None),
        P(both, None),
        P(),
        P(),
        P(),
        P(),
        P("exp", "tp"),
        P("exp", "tp"),
        P("exp", "tp"),
        P("tp", "exp"),
        P(),
        P(both, None, None),
        P(both, None, None),
        P(both, None, None),
        P(both, None),
        P(both, None),
        P(),
    )
    out_specs = (
        P(both, None),
        P(both, None),
        P(),
        P(),
        P(),
        P(),
        P("exp", "tp"),
        P("exp", "tp"),
        P("exp", "tp"),
        P("tp", "exp"),
        P(),
        P(both, None, None),
        P(both, None, None),
        P(both, None, None),
    )
    return jax.shard_map(local, mesh=mesh, in_specs=in_specs, out_specs=out_specs, check_vma=False)
```
